512 devices in a mesh: frames: 8 (over y, core), tiles: 64 (over z, x).
Axes of the slice: x: 4, y: 4, z: 16, core: 2. Of those that a mesh axis runs over, the one named last changes fastest.
Arguments:
- inputs: bfloat16 [8, 64, 128, 1024], P('frames', 'tiles'), may hold values from -0.375 to 0.375
- grad_out: bfloat16 [8, 64, 128, 1024], P('frames', 'tiles'), may hold values from -0.375 to 0.375
- b_proj: bfloat16 [8, 64, 128, 128], P('frames', 'tiles'), may hold values from -0.5 to 0.5
- c_proj: bfloat16 [8, 64, 128, 128], P('frames', 'tiles'), may hold values from -0.5 to 0.5
- log_decay: bfloat16 [16, 8, 64, 128], P(None, 'frames', 'tiles'), may hold values from -0.6 to 0
- saved_raster: float32 [8, 64, 16, 64, 128], P('frames', 'tiles'), may hold values from -6 to 6
- saved_column: float32 [8, 64, 16, 64, 128], P('frames', 'tiles'), may hold values from -6 to 6
Outputs:
- grad_x: bfloat16 [8, 64, 128, 1024], P('frames', 'tiles')
- grad_b: bfloat16 [8, 64, 128, 128], P('frames', 'tiles')
- grad_c: bfloat16 [8, 64, 128, 128], P('frames', 'tiles')
The draws below stay inside these ranges and needn't reach their ends.
All inputs are finite; a program needn't handle non-finite values.
Results may differ from the reference program's by a relative error of at most 0.015.
Values may be sent and summed in bfloat16 or wider, within the bound.
A program may use at most 64 MiB of HBM per device.

```python
import jax
import jax.numpy as jnp
from jax import lax

HEADS = 16
HEAD_DIM = 64
STATE = 128
WIDTH = 128
ROWS_DEV = 1
FRAMES = 8
HEIGHT = 64
LATENT_VERTICAL = 2
CHANNELS = 1024
N_TILES = 64


def draw_log_decay(key, part):
    key = jax.random.fold_in(key, 11)
    keys = jax.random.split(key, 7)
    slow_count = max(1, HEADS // 2)
    chain = FRAMES * ROWS_DEV * WIDTH
    slow_heads = jax.random.permutation(keys[0], HEADS) < slow_count
    slow_rate = jax.random.uniform(keys[1], (HEADS,), minval=0.1, maxval=0.25) * 2.302585 / chain
    fast_rate = 1.0 / jax.random.uniform(keys[2], (HEADS,), minval=30.0, maxval=50.0)
    base_rate = jnp.where(slow_heads, slow_rate, fast_rate)
    roughness = jax.random.uniform(keys[3], (HEADS, FRAMES, HEIGHT, WIDTH), minval=0.5, maxval=1.5)
    row_scale = jnp.exp(jax.random.uniform(keys[4], (1, FRAMES, HEIGHT, 1), minval=-0.69, maxval=0.69))
    fading_rate = base_rate[:, None, None, None] * roughness * row_scale
    hit_locations = jax.random.uniform(keys[5], (1, FRAMES, HEIGHT, WIDTH)) < 3.0 / chain
    objective_entries = jax.random.uniform(keys[6], (HEADS, 1, 1, 1), minval=0.2, maxval=0.33)
    spike_bundles = jnp.where(hit_locations, jnp.log(1.0 - objective_entries), 0.0)
    return (spike_bundles - fading_rate).astype(jnp.float32).astype(jnp.bfloat16)


def steps_of(stream_key, extent, cuts, least, top_value):
    level = 1.0
    for dim, blocks in cuts:
        heights = jax.random.uniform(jax.random.fold_in(jax.random.fold_in(stream_key, 6), dim), (blocks,), jnp.float32, least / len(cuts), top_value / len(cuts))
        level = level * jnp.repeat(jnp.exp(heights), extent[dim] // blocks).reshape((-1,) + (1,) * (len(extent) - 1 - dim))
    return level


def normal_values(stream_key, shape, scale, most, cuts=(), dtype=jnp.bfloat16):
    values = scale * jax.random.normal(stream_key, shape, jnp.float32)
    if cuts:
        values = values * steps_of(stream_key, shape, cuts, -0.22, 0.18)
    return jnp.clip(values, -most, most).astype(dtype)


def setup_inputs(seed: int = 0) -> dict:
    streams_of = jax.random.split(jax.random.key(seed), 8)
    inputs = normal_values(streams_of[0], (FRAMES, HEIGHT, WIDTH, CHANNELS), 0.0625, 0.375, ((0, 8), (1, 64)))
    grad_out = normal_values(streams_of[1], (FRAMES, HEIGHT, WIDTH, CHANNELS), 0.0625, 0.375, ((0, 8), (1, 64)))
    b_proj = normal_values(streams_of[2], (FRAMES, HEIGHT, WIDTH, STATE), STATE ** -0.5, 0.5, ((0, 8), (1, 64)))
    c_proj = normal_values(streams_of[3], (FRAMES, HEIGHT, WIDTH, STATE), STATE ** -0.5, 0.5, ((0, 8), (1, 64)))
    log_decay = draw_log_decay(jax.random.fold_in(streams_of[7], 71), 0)
    saved_raster = normal_values(streams_of[5], (FRAMES, N_TILES, HEADS, HEAD_DIM, STATE), 1.0, 6.0, ((0, 8), (1, 64)), jnp.float32)
    saved_column = normal_values(streams_of[6], (FRAMES, N_TILES, HEADS, HEAD_DIM, STATE), 1.0, 6.0, ((0, 8), (1, 64)), jnp.float32)
    return {"inputs": inputs, "grad_out": grad_out, "b_proj": b_proj, "c_proj": c_proj, "log_decay": log_decay, "saved_raster": saved_raster, "saved_column": saved_column}


def block_element(grad_rows, c_rows, decay_rows):
    length = grad_rows.shape[0]
    cumulative = jnp.cumsum(decay_rows.astype(jnp.float32), axis=0)
    weighted = (jnp.exp(cumulative)[:, :, None] * c_rows.astype(jnp.float32)[:, None, :]).astype(jnp.bfloat16)
    weighted = lax.optimization_barrier(weighted).astype(jnp.float32)
    grad_heads = grad_rows.reshape(length, HEADS, HEAD_DIM).astype(jnp.float32)
    state_term = jnp.einsum('tho,thn->hon', grad_heads, weighted)
    return jnp.exp(cumulative[-1]), state_term


def block_grads(x_rows, grad_rows, b_rows, c_rows, decay_rows, saved, carried):
    length = x_rows.shape[0]
    cumulative = jnp.cumsum(decay_rows.astype(jnp.float32), axis=0)
    block_total = cumulative[-1]
    input_heads = x_rows.reshape(length, HEADS, HEAD_DIM).astype(jnp.float32)
    grad_heads = grad_rows.reshape(length, HEADS, HEAD_DIM).astype(jnp.float32)
    b_full = b_rows.astype(jnp.float32)
    readout_matrix_whole = c_rows.astype(jnp.float32)
    row_index = lax.broadcasted_iota(jnp.int32, (length, length), 0)
    col_index = lax.broadcasted_iota(jnp.int32, (length, length), 1)
    causal = row_index >= col_index
    cum_heads = cumulative.T
    log_gap = cum_heads[:, :, None] - cum_heads[:, None, :]
    weight = jnp.where(causal[None], jnp.exp(jnp.minimum(log_gap, 0.0)), 0.0)
    scores = jnp.einsum('tho,sho->hts', grad_heads, input_heads)
    mixed_r = lax.optimization_barrier((weight * scores).astype(jnp.bfloat16)).astype(jnp.float32)
    pairing = jnp.dot(c_rows, b_rows.T, preferred_element_type=jnp.float32)
    mixed_z = lax.optimization_barrier((weight * pairing[None]).astype(jnp.bfloat16)).astype(jnp.float32)
    carry_low = lax.optimization_barrier(carried.astype(jnp.bfloat16)).astype(jnp.float32)
    saved_low = lax.optimization_barrier(saved.astype(jnp.bfloat16)).astype(jnp.float32)
    tail_scale = jnp.exp(block_total[None, :] - cumulative)
    head_scale = jnp.exp(cumulative)
    grad_input = jnp.einsum('hst,sho->tho', mixed_z, grad_heads)
    grad_input = grad_input + tail_scale[:, :, None] * jnp.einsum('tn,hon->tho', b_full, carry_low)
    grad_bmap = jnp.einsum('hst,sn->tn', mixed_r, readout_matrix_whole)
    grad_bmap = grad_bmap + jnp.sum(tail_scale[:, :, None] * jnp.einsum('tho,hon->thn', input_heads, carry_low), axis=1)
    grad_cmap = jnp.einsum('hts,sn->tn', mixed_r, b_full)
    grad_cmap = grad_cmap + jnp.sum(head_scale[:, :, None] * jnp.einsum('tho,hon->thn', grad_heads, saved_low), axis=1)
    return grad_input.reshape(length, HEADS * HEAD_DIM), grad_bmap, grad_cmap


def order_pass(x_blocks, grad_blocks, b_blocks, c_blocks, decay_blocks, saved_blocks):
    decay_all, state_term = lax.map(lambda pieces: block_element(pieces[0], pieces[1], pieces[2]), (grad_blocks, c_blocks, decay_blocks))
    decay_all = decay_all.reshape(FRAMES, N_TILES, HEADS)
    state_term = state_term.reshape(FRAMES, N_TILES, HEADS, HEAD_DIM, STATE)

    def forward_advance(carried, element):
        return element[0][:, :, None, None] * carried + element[1], carried

    start_state = jnp.zeros((N_TILES, HEADS, HEAD_DIM, STATE), jnp.float32)
    _, carries = lax.scan(forward_advance, start_state, (decay_all, state_term), reverse=True)
    carries = carries.reshape(FRAMES * N_TILES, HEADS, HEAD_DIM, STATE)
    return lax.map(lambda pieces: block_grads(pieces[0], pieces[1], pieces[2], pieces[3], pieces[4], pieces[5], pieces[6]), (x_blocks, grad_blocks, b_blocks, c_blocks, decay_blocks, saved_blocks, carries))


def reference(inputs, grad_out, b_proj, c_proj, log_decay, saved_raster, saved_column):
    blocks = FRAMES * N_TILES
    decay_last = jnp.transpose(log_decay, (1, 2, 3, 0))

    def rows_of(array):
        return array.reshape(blocks, ROWS_DEV * WIDTH, array.shape[-1])

    def columns_of(array):
        shaped = array.reshape(FRAMES, HEIGHT, N_TILES, LATENT_VERTICAL, array.shape[-1])
        return shaped.transpose(0, 2, 3, 1, 4).reshape(blocks, LATENT_VERTICAL * HEIGHT, array.shape[-1])

    def back_rows(array):
        shaped = array.reshape(FRAMES, N_TILES, LATENT_VERTICAL, HEIGHT, array.shape[-1])
        return shaped.transpose(0, 3, 1, 2, 4).reshape(FRAMES, HEIGHT, WIDTH, array.shape[-1])

    row_x, row_b, row_c = order_pass(rows_of(inputs), rows_of(grad_out), rows_of(b_proj), rows_of(c_proj), rows_of(decay_last), saved_raster.reshape(blocks, HEADS, HEAD_DIM, STATE))
    col_x, col_b, col_c = order_pass(columns_of(inputs), columns_of(grad_out), columns_of(b_proj), columns_of(c_proj), columns_of(decay_last), saved_column.reshape(blocks, HEADS, HEAD_DIM, STATE))

    def finish(row_part, col_part):
        col_round = lax.optimization_barrier(back_rows(col_part.astype(jnp.bfloat16)))
        return (row_part.reshape(FRAMES, HEIGHT, WIDTH, row_part.shape[-1]) + col_round.astype(jnp.float32)).astype(jnp.bfloat16)

    return finish(row_x, col_x), finish(row_b, col_b), finish(row_c, col_c)
```

```python
import jax
import jax.numpy as jnp
from jax import lax
from jax.experimental import pallas as pl
from jax.experimental.pallas import tpu as pltpu
from jax.sharding import PartitionSpec as P

HEADS = 16
HEAD_DIM = 64
STATE = 128
TOKENS = 128
CHANNELS = 1024
LANES = 128
PAIRS = CHANNELS // LANES
TILES = 64
DEPTH_Z = 16
DEPTH_X = 4
FRAMES = 8
HALF = PAIRS // 2
EARLY = 12
PER_HOP = 9
BF = jnp.bfloat16
F32 = jnp.float32
MESH = pl.DeviceIdType.MESH


def nn(a, b):
    return lax.dot_general(a, b, (((1,), (0,)), ((), ())), preferred_element_type=F32)


def nt(a, b):
    return lax.dot_general(a, b, (((1,), (1,)), ((), ())), preferred_element_type=F32)


def iota(shape, dim):
    return lax.broadcasted_iota(jnp.int32, shape, dim)


def ones_where(cond):
    return jnp.where(cond, 1.0, 0.0).astype(BF)


def square(shape=(TOKENS, TOKENS)):
    return iota(shape, 0), iota(shape, 1)


def place(index, column_order):
    if not column_order:
        return index
    return lax.shift_left(index & 1, 6) + lax.shift_right_logical(index, 1)


def causal(column_order):
    t, s = square()
    return place(s, column_order) <= place(t, column_order)


def causal_transposed(column_order):
    s, t = square()
    return place(s, column_order) <= place(t, column_order)


def high(index, bits):
    return lax.shift_right_logical(index, bits)


def interleave(back=False):
    r, c = square()
    if back:
        r, c = c, r
    return ones_where((high(r, 3) == (c & 15)) & ((r & 7) == high(c, 4)))


def identity():
    r, c = square()
    return ones_where(r == c)


def maps_matrix(bits, parts, back=False):
    shape = (16 << bits, 32 * parts)
    if back:
        c, r = square(shape[::-1])
    else:
        r, c = square(shape)
    part, token = high(c, 5), c & 31
    return ones_where(r == lax.shift_left(high(token, 1), bits) + part * 2 + (token & 1))


def pair(k):
    return slice(LANES * k, LANES * k + LANES)


def pack_channels(read, write):
    mix = interleave()
    for q in range(8):
        stack = jnp.concatenate([read(q, k) for k in range(PAIRS)], axis=0)
        write(q, nn(mix, stack).reshape(8, 2, 8, LANES).astype(BF))


def unpack_channels(read, write):
    mix = interleave(True)
    for q in range(8):
        tiles = read(q).astype(F32).reshape(TOKENS, LANES).astype(BF)
        out = nn(mix, tiles)
        for k in range(PAIRS):
            write(q, k, out[16 * k : 16 * k + 16, :])


def block_states(grad, c_rows, decays, column_order, refs, term, low):
    grow, ends, centred, headed = refs
    run = ones_where(causal(column_order))
    c_turned = nt(identity(), c_rows).astype(BF)
    head, channel = square((TOKENS, LANES))
    for k in range(PAIRS):
        spread = ones_where(high(channel, 6) + 2 * k == head)
        cum = nn(run, nn(decays, spread).astype(BF))
        total = cum[TOKENS - 1 : TOKENS, :]
        middle = total * 0.5
        to_middle = jnp.exp(middle)
        shrunk = grad[:, pair(k)].astype(F32) * jnp.exp(cum - middle)
        grow[:, pair(k)] = jnp.exp(middle - cum)
        ends[k, 0:1, :] = to_middle
        ends[k, 1:2, :] = jnp.exp(total)
        centred[:, pair(k)] = shrunk.astype(BF)
        by_head = (shrunk * to_middle).astype(BF)
        headed[:, pair(k)] = by_head
        state = nn(c_turned, by_head)
        term[k] = state
        low[k] = state.astype(BF)


def grad_of_x(b_rows, c_rows, carry, column_order, refs, tails, write):
    grow, ends, centred, headed = refs
    pairing = jnp.where(causal_transposed(column_order), nt(b_rows, c_rows), 0.0).astype(BF)
    both = jnp.concatenate([pairing, b_rows], axis=1)
    for k in range(PAIRS):
        tail = (carry[k].astype(F32) * ends[k, 0:1, :]).astype(BF)
        tails[:, pair(k)] = tail
        stack = jnp.concatenate([centred[:, pair(k)], tail], axis=0)
        write(k, nn(both, stack) * grow[:, pair(k)])


def grads_of_maps(x, b_rows, c_rows, saved, column_order, refs, tails, scaled):
    grow, ends, centred, headed = refs
    for k in range(PAIRS):
        scaled[:, pair(k)] = (x[:, pair(k)].astype(F32) * grow[:, pair(k)]).astype(BF)
    mixed = jnp.where(causal(column_order), nt(centred[...], scaled[...]), 0.0)
    part_b = nn(mixed.T.astype(BF), c_rows) + nt(scaled[...], tails[...])
    part_c = nn(mixed.astype(BF), b_rows) + nn(headed[...], saved[...].astype(BF))
    return part_b, part_c


def kernel(
    x_hbm, g_hbm, b_hbm, c_hbm, d_hbm, saved_row_hbm, saved_col_hbm,
    out_x, out_b, out_c,
    x_ref, g_ref, b_ref, c_ref, d_ref, saved_row, saved_col,
    send_g, send_x, got_g, got_x, back_x, back_m, home_x, home_m,
    row_grow, row_centred, row_headed, col_grow, col_centred, col_headed,
    term, low, ends, peer_low, peer_ends, incoming, outgoing, give, carry,
    tails, scaled, wide, col_maps, part_x,
    load_sem, send_sem, recv_sem, swap_send, swap_recv, hop_send, hop_recv, give_send, give_recv,
):
    f = lax.axis_index("frames")
    me = lax.axis_index("tiles")
    z, x = lax.div(me, DEPTH_X), lax.rem(me, DEPTH_X)

    loads = [
        pltpu.make_async_copy(source, target, load_sem.at[i])
        for i, (source, target) in enumerate([
            (g_hbm, g_ref), (b_hbm, b_ref), (c_hbm, c_ref), (d_hbm, d_ref), (x_hbm, x_ref),
            (saved_row_hbm, saved_row), (saved_col_hbm, saved_col),
        ])
    ]
    for load in loads:
        load.start()

    def partner(k):
        step = TILES - 1 - k
        u, dx = lax.div(step, DEPTH_X), lax.rem(step, DEPTH_X)
        dz = lax.div(u + 1, 2) * (2 * lax.rem(u, 2) - 1)
        return lax.rem(z + dz + DEPTH_Z, DEPTH_Z) * DEPTH_X + lax.rem(x + dx, DEPTH_X)

    barrier = pltpu.get_barrier_semaphore()

    @pl.loop(0, TILES - 1)
    def _(k):
        pl.semaphore_signal(barrier, inc=1, device_id=(f, partner(k)), device_id_type=MESH)

    core, chip_y = lax.rem(f, 2), lax.div(f, 2)
    other = f + 1 - 2 * core
    above, below = lax.rem(f + 2, FRAMES), lax.rem(f + FRAMES - 2, FRAMES)
    mine, theirs = core * HALF, HALF - core * HALF
    for neighbour in (other, above, below):
        pl.semaphore_signal(barrier, inc=1, device_id=(neighbour, me), device_id_type=MESH)

    def keep_own(source, target):
        target[pl.ds(me, 1)] = source[pl.ds(me, 1)]

    def exchange(source, target, which, first=0, last=TILES - 1):
        @pl.loop(first, last)
        def _(k):
            peer = partner(k)
            pltpu.make_async_remote_copy(
                src_ref=source.at[peer],
                dst_ref=target.at[me],
                send_sem=send_sem.at[which],
                recv_sem=recv_sem.at[which],
                device_id=(f, peer),
                device_id_type=MESH,
            ).start()

    def wait_all(ref, sem):
        some = ref.at[pl.ds(0, TILES - 1)]
        pltpu.make_async_copy(some, some, sem).wait()

    def put_g(q, value):
        send_g[8 * q : 8 * q + 8, 0:2] = value

    def put_x(q, value):
        send_x[8 * q : 8 * q + 8] = value

    def reader(ref):
        return lambda q, k: ref[16 * q : 16 * q + 16, pair(k)]

    loads[0].wait()
    pack_channels(reader(g_ref), put_g)
    for i in (1, 2, 3):
        loads[i].wait()
    decays = nt(identity(), jnp.concatenate(
        [d_ref[...], jnp.zeros((TOKENS - HEADS, TOKENS), BF)], axis=0)).astype(BF)
    b_rows, c_rows = b_ref[...], c_ref[...]
    spread_maps = maps_matrix(3, 3)
    for q in range(4):
        rows = slice(32 * q, 32 * q + 32)
        stack = jnp.concatenate([b_rows[rows], c_rows[rows], decays[rows]], axis=0)
        packed = nn(spread_maps, stack).reshape(16, 8, LANES).astype(BF)
        send_g[16 * q : 16 * q + 16, 2] = packed

    pl.semaphore_wait(barrier, TILES + 2)
    exchange(send_g, got_g, 0)
    keep_own(send_g, got_g)
    loads[4].wait()
    pack_channels(reader(x_ref), put_x)
    keep_own(send_x, got_x)

    @pl.when(chip_y == FRAMES // 2 - 1)
    def _():
        incoming[...] = jnp.zeros_like(incoming)

    def swap_copies(order):
        return [
            pltpu.make_async_remote_copy(
                src_ref=source,
                dst_ref=target,
                send_sem=swap_send.at[order, i],
                recv_sem=swap_recv.at[order, i],
                device_id=(other, me),
                device_id_type=MESH,
            )
            for i, (source, target) in enumerate([
                (ends.at[order], peer_ends.at[order]),
                (low.at[order, pl.ds(theirs, HALF)], peer_low.at[order]),
            ])
        ]

    def hop_copy(order, i):
        return pltpu.make_async_remote_copy(
            src_ref=outgoing.at[order, i],
            dst_ref=incoming.at[order, i],
            send_sem=hop_send.at[order, i],
            recv_sem=hop_recv.at[order, i],
            device_id=(below, me),
            device_id_type=MESH,
        )

    def give_copy(order, i):
        return pltpu.make_async_remote_copy(
            src_ref=give.at[order, i],
            dst_ref=carry.at[order, mine + i],
            send_sem=give_send.at[order, i],
            recv_sem=give_recv.at[order, i],
            device_id=(other, me),
            device_id_type=MESH,
        )

    def swapped(order):
        for copy in swap_copies(order):
            copy.wait_recv()

    def chain(order):
        for i in range(HALF):
            k = mine + i
            own_state, peer_state = term[order, k], peer_low[order, i].astype(F32)
            own_decay, peer_decay = ends[order, k, 1:2, :], peer_ends[order, k, 1:2, :]
            lower = core == 0
            lower_state = jnp.where(lower, own_state, peer_state)
            upper_state = jnp.where(lower, peer_state, own_state)
            lower_decay = jnp.where(lower, own_decay, peer_decay)
            upper_decay = jnp.where(lower, peer_decay, own_decay)

            @pl.when(chip_y < FRAMES // 2 - 1)
            def _():
                hop_copy(order, i).wait_recv()

            entering = incoming[order, i].astype(F32)
            between = upper_decay * entering + upper_state

            @pl.when(chip_y > 0)
            def _():
                outgoing[order, i] = (lower_decay * between + lower_state).astype(BF)
                hop_copy(order, i).start()

            carry[order, k] = jnp.where(lower, between, entering).astype(BF)
            give[order, i] = jnp.where(lower, entering, between).astype(BF)
            give_copy(order, i).start()

    def chain_end(order):
        for i in range(HALF):
            pltpu.make_async_copy(
                carry.at[order, theirs + i], carry.at[order, theirs + i], give_recv.at[order, i]
            ).wait()

    def chain_sent(order):
        for copy in swap_copies(order):
            copy.wait_send()
        for i in range(HALF):
            give_copy(order, i).wait_send()

            @pl.when(chip_y > 0)
            def _():
                hop_copy(order, i).wait_send()

    row_refs = (row_grow, ends.at[0], row_centred, row_headed)
    block_states(g_ref, c_rows, decays, False, row_refs, term.at[0], low.at[0])
    for copy in swap_copies(0):
        copy.start()

    wait_all(got_g, recv_sem.at[0])
    exchange(send_x, got_x, 1, 0, EARLY)

    def put_wide(q, k, value):
        wide[16 * q : 16 * q + 16, pair(k)] = value.astype(BF)

    unpack_channels(lambda q: got_g[8 * q : 8 * q + 8, 0:2], put_wide)
    gather_maps = maps_matrix(3, 3, True)
    for q in range(4):
        tiles = got_g[16 * q : 16 * q + 16, 2].astype(F32).reshape(TOKENS, LANES).astype(BF)
        piece = nn(gather_maps, tiles).astype(BF)
        for p in range(3):
            col_maps[p, 32 * q : 32 * q + 32] = piece[32 * p : 32 * p + 32]
    col_refs = (col_grow, ends.at[1], col_centred, col_headed)
    block_states(wide, col_maps[1], col_maps[2], True, col_refs, term.at[1], low.at[1])
    for copy in swap_copies(1):
        copy.start()
    filled = EARLY + PER_HOP * (FRAMES // 2 - 1 - chip_y)
    swapped(1)
    exchange(send_x, got_x, 1, EARLY, filled)
    chain(1)
    exchange(send_x, got_x, 1, filled)
    chain_end(1)

    def put_col(k, value):
        wide[:, pair(k)] = value.astype(BF)

    grad_of_x(col_maps[0], col_maps[1], carry.at[1], True, col_refs, tails, put_col)

    def put_back(q, value):
        back_x[8 * q : 8 * q + 8] = value

    pack_channels(reader(wide), put_back)
    swapped(0)
    chain(0)
    exchange(back_x, home_x, 2)
    keep_own(back_x, home_x)

    wait_all(got_x, recv_sem.at[1])
    loads[6].wait()
    unpack_channels(lambda q: got_x[8 * q : 8 * q + 8], put_wide)
    col_b, col_c = grads_of_maps(
        wide, col_maps[0], col_maps[1], saved_col, True, col_refs, tails, scaled)
    col_b, col_c = col_b.astype(BF), col_c.astype(BF)
    spread_back = maps_matrix(2, 2)
    for q in range(4):
        rows = slice(32 * q, 32 * q + 32)
        stack = jnp.concatenate([col_b[rows], col_c[rows]], axis=0)
        packed = nn(spread_back, stack).reshape(16, 4, LANES).astype(BF)
        back_m[16 * q : 16 * q + 16] = packed
    exchange(back_m, home_m, 3)
    keep_own(back_m, home_m)

    def put_row(k, value):
        part_x[:, pair(k)] = value

    chain_end(0)
    grad_of_x(b_rows, c_rows, carry.at[0], False, row_refs, tails, put_row)
    loads[5].wait()
    row_b, row_c = grads_of_maps(
        x_ref, b_rows, c_rows, saved_row, False, row_refs, tails, scaled)

    wait_all(home_x, recv_sem.at[2])

    def put_sum(q, k, value):
        rows = slice(16 * q, 16 * q + 16)
        out_x[rows, pair(k)] = (part_x[rows, pair(k)] + value).astype(BF)

    unpack_channels(lambda q: home_x[8 * q : 8 * q + 8], put_sum)

    wait_all(home_m, recv_sem.at[3])
    gather_back = maps_matrix(2, 2, True)
    for q in range(4):
        rows = slice(32 * q, 32 * q + 32)
        tiles = home_m[16 * q : 16 * q + 16].astype(F32).reshape(64, LANES).astype(BF)
        both = nn(gather_back, tiles)
        out_b[rows, :] = (row_b[rows] + both[0:32]).astype(BF)
        out_c[rows, :] = (row_c[rows] + both[32:64]).astype(BF)

    chain_sent(0)
    chain_sent(1)
    wait_all(send_g, send_sem.at[0])
    wait_all(send_x, send_sem.at[1])
    wait_all(back_x, send_sem.at[2])
    wait_all(back_m, send_sem.at[3])


def shards(inputs, grad_out, b_proj, c_proj, log_decay, saved_raster, saved_column):
    vmem = pl.BlockSpec(memory_space=pltpu.VMEM)
    out_x, out_b, out_c = pl.pallas_call(
        kernel,
        out_shape=(
            jax.ShapeDtypeStruct((TOKENS, CHANNELS), BF),
            jax.ShapeDtypeStruct((TOKENS, STATE), BF),
            jax.ShapeDtypeStruct((TOKENS, STATE), BF),
        ),
        in_specs=[pl.BlockSpec(memory_space=pltpu.HBM)] * 7,
        out_specs=(vmem, vmem, vmem),
        scratch_shapes=[
            pltpu.VMEM((TOKENS, CHANNELS), BF),
            pltpu.VMEM((TOKENS, CHANNELS), BF),
            pltpu.VMEM((TOKENS, STATE), BF),
            pltpu.VMEM((TOKENS, STATE), BF),
            pltpu.VMEM((HEADS, TOKENS), BF),
            pltpu.VMEM((CHANNELS, STATE), F32),
            pltpu.VMEM((CHANNELS, STATE), F32),
            pltpu.VMEM((TILES, 3, 8, LANES), BF),
            pltpu.VMEM((TILES, 2, 8, LANES), BF),
            pltpu.VMEM((TILES, 3, 8, LANES), BF),
            pltpu.VMEM((TILES, 2, 8, LANES), BF),
            pltpu.VMEM((TILES, 2, 8, LANES), BF),
            pltpu.VMEM((TILES, 4, LANES), BF),
            pltpu.VMEM((TILES, 2, 8, LANES), BF),
            pltpu.VMEM((TILES, 4, LANES), BF),
            pltpu.VMEM((TOKENS, CHANNELS), F32),
            pltpu.VMEM((TOKENS, CHANNELS), BF),
            pltpu.VMEM((TOKENS, CHANNELS), BF),
            pltpu.VMEM((TOKENS, CHANNELS), F32),
            pltpu.VMEM((TOKENS, CHANNELS), BF),
            pltpu.VMEM((TOKENS, CHANNELS), BF),
            pltpu.VMEM((2, PAIRS, STATE, LANES), F32),
            pltpu.VMEM((2, PAIRS, STATE, LANES), BF),
            pltpu.VMEM((2, PAIRS, 2, LANES), F32),
            pltpu.VMEM((2, HALF, STATE, LANES), BF),
            pltpu.VMEM((2, PAIRS, 2, LANES), F32),
            pltpu.VMEM((2, HALF, STATE, LANES), BF),
            pltpu.VMEM((2, HALF, STATE, LANES), BF),
            pltpu.VMEM((2, HALF, STATE, LANES), BF),
            pltpu.VMEM((2, PAIRS, STATE, LANES), BF),
            pltpu.VMEM((STATE, CHANNELS), BF),
            pltpu.VMEM((TOKENS, CHANNELS), BF),
            pltpu.VMEM((TOKENS, CHANNELS), BF),
            pltpu.VMEM((3, TOKENS, LANES), BF),
            pltpu.VMEM((TOKENS, CHANNELS), F32),
            pltpu.SemaphoreType.DMA((7,)),
            pltpu.SemaphoreType.DMA((4,)),
            pltpu.SemaphoreType.DMA((4,)),
            pltpu.SemaphoreType.DMA((2, 2)),
            pltpu.SemaphoreType.DMA((2, 2)),
            pltpu.SemaphoreType.DMA((2, HALF)),
            pltpu.SemaphoreType.DMA((2, HALF)),
            pltpu.SemaphoreType.DMA((2, HALF)),
            pltpu.SemaphoreType.DMA((2, HALF)),
        ],
        compiler_params=pltpu.CompilerParams(
            collective_id=0, has_side_effects=True, vmem_limit_bytes=63 * 1024 * 1024
        ),
        cost_estimate=pl.CostEstimate(
            flops=800_000_000, bytes_accessed=2_600_000, transcendentals=1_000_000
        ),
        name="scan_backward",
    )(
        inputs.reshape(TOKENS, CHANNELS),
        grad_out.reshape(TOKENS, CHANNELS),
        b_proj.reshape(TOKENS, STATE),
        c_proj.reshape(TOKENS, STATE),
        log_decay.reshape(HEADS, TOKENS),
        saved_raster.reshape(CHANNELS, STATE),
        saved_column.reshape(CHANNELS, STATE),
    )
    return (
        out_x.reshape(1, 1, TOKENS, CHANNELS),
        out_b.reshape(1, 1, TOKENS, STATE),
        out_c.reshape(1, 1, TOKENS, STATE),
    )


def solution(mesh):
    in_specs = (
        P("frames", "tiles", None, None),
        P("frames", "tiles", None, None),
        P("frames", "tiles", None, None),
        P("frames", "tiles", None, None),
        P(None, "frames", "tiles", None),
        P("frames", "tiles", None, None, None),
        P("frames", "tiles", None, None, None),
    )
    out_specs = (
        P("frames", "tiles", None, None),
        P("frames", "tiles", None, None),
        P("frames", "tiles", None, None),
    )
    return jax.shard_map(shards, mesh=mesh, in_specs=in_specs, out_specs=out_specs, check_vma=False)
```

```python
import jax
import jax.numpy as jnp
from jax import lax
from jax.experimental import pallas as pl
from jax.experimental.pallas import tpu as pltpu
from jax.sharding import PartitionSpec as P

HEADS = 16
HEAD_DIM = 64
STATE = 128
TOKENS = 128
CHANNELS = 1024
LANES = 128
PAIRS = CHANNELS // LANES
TILES = 64
DEPTH_Z = 16
DEPTH_X = 4
FRAMES = 8
HALF = PAIRS // 2
BEHIND = 8
EARLY = 20
PER_HOP = 7
BF = jnp.bfloat16
F32 = jnp.float32
MESH = pl.DeviceIdType.MESH


def nn(a, b):
    return lax.dot_general(a, b, (((1,), (0,)), ((), ())), preferred_element_type=F32)


def nt(a, b):
    return lax.dot_general(a, b, (((1,), (1,)), ((), ())), preferred_element_type=F32)


def iota(shape, dim):
    return lax.broadcasted_iota(jnp.int32, shape, dim)


def ones_where(cond):
    return jnp.where(cond, 1.0, 0.0).astype(BF)


def square(shape=(TOKENS, TOKENS)):
    return iota(shape, 0), iota(shape, 1)


def place(index, column_order):
    if not column_order:
        return index
    return lax.shift_left(index & 1, 6) + lax.shift_right_logical(index, 1)


def causal(column_order):
    t, s = square()
    return place(s, column_order) <= place(t, column_order)


def causal_transposed(column_order):
    s, t = square()
    return place(s, column_order) <= place(t, column_order)


def high(index, bits):
    return lax.shift_right_logical(index, bits)


def interleave(back=False):
    r, c = square()
    if back:
        r, c = c, r
    return ones_where((high(r, 3) == (c & 15)) & ((r & 7) == high(c, 4)))


def identity():
    r, c = square()
    return ones_where(r == c)


def maps_matrix(bits, parts, back=False):
    shape = (16 << bits, 32 * parts)
    if back:
        c, r = square(shape[::-1])
    else:
        r, c = square(shape)
    part, token = high(c, 5), c & 31
    return ones_where(r == lax.shift_left(high(token, 1), bits) + part * 2 + (token & 1))


def pair(k):
    return slice(LANES * k, LANES * k + LANES)


def pack_channels(read, write):
    mix = interleave()
    for q in range(8):
        stack = jnp.concatenate([read(q, k) for k in range(PAIRS)], axis=0)
        write(q, nn(mix, stack).reshape(8, 2, 8, LANES).astype(BF))


def unpack_channels(read, write):
    mix = interleave(True)
    for q in range(8):
        tiles = read(q).astype(F32).reshape(TOKENS, LANES).astype(BF)
        out = nn(mix, tiles)
        for k in range(PAIRS):
            write(q, k, out[16 * k : 16 * k + 16, :])


def block_scales(decays, column_order, shrink, grow, ends):
    run = ones_where(causal(column_order))
    head, channel = square((TOKENS, LANES))
    for k in range(PAIRS):
        spread = ones_where(high(channel, 6) + 2 * k == head)
        cum = nn(run, nn(decays, spread).astype(BF))
        total = cum[TOKENS - 1 : TOKENS, :]
        middle = total * 0.5
        shrink[:, pair(k)] = jnp.exp(cum - middle)
        grow[:, pair(k)] = jnp.exp(middle - cum)
        ends[k, 0:1, :] = jnp.exp(middle)
        ends[k, 1:2, :] = jnp.exp(total)


def block_states(grad, c_rows, shrink, refs, term, low):
    grow, ends, centred, headed = refs
    c_turned = nt(identity(), c_rows).astype(BF)
    for k in range(PAIRS):
        shrunk = grad[:, pair(k)].astype(F32) * shrink[:, pair(k)]
        centred[:, pair(k)] = shrunk.astype(BF)
        by_head = (shrunk * ends[k, 0:1, :]).astype(BF)
        headed[:, pair(k)] = by_head
        state = nn(c_turned, by_head)
        term[k] = state
        low[k] = state.astype(BF)


def grad_of_x(b_rows, c_rows, carry, column_order, refs, tails, write):
    grow, ends, centred, headed = refs
    pairing = jnp.where(causal_transposed(column_order), nt(b_rows, c_rows), 0.0).astype(BF)
    both = jnp.concatenate([pairing, b_rows], axis=1)
    for k in range(PAIRS):
        tail = (carry(k).astype(F32) * ends[k, 0:1, :]).astype(BF)
        tails[:, pair(k)] = tail
        stack = jnp.concatenate([centred[:, pair(k)], tail], axis=0)
        write(k, nn(both, stack) * grow[:, pair(k)])


def grads_of_maps(x, b_rows, c_rows, saved, column_order, refs, tails, scaled):
    grow, ends, centred, headed = refs
    for k in range(PAIRS):
        scaled[:, pair(k)] = (x[:, pair(k)].astype(F32) * grow[:, pair(k)]).astype(BF)
    mixed = jnp.where(causal(column_order), nt(centred[...], scaled[...]), 0.0)
    part_b = nn(mixed.T.astype(BF), c_rows) + nt(scaled[...], tails[...])
    part_c = nn(mixed.astype(BF), b_rows) + nn(headed[...], saved[...].astype(BF))
    return part_b, part_c


def kernel(
    x_hbm, g_hbm, b_hbm, c_hbm, d_hbm, saved_row_hbm, saved_col_hbm,
    out_x, out_b, out_c,
    x_ref, g_ref, b_ref, c_ref, d_ref, saved_row, saved_col,
    send_m, send_g, send_x, got_m, got_g, got_x, back_x, back_m, home_x, home_m,
    shrink, row_grow, row_centred, row_headed, col_grow, col_centred, col_headed,
    term, low, ends, peer_low, peer_ends, incoming, outgoing, give, carry,
    tails, scaled, wide, col_maps, part_x,
    load_sem, send_sem, recv_sem, swap_send, swap_recv, hop_send, hop_recv, give_send, give_recv,
):
    f = lax.axis_index("frames")
    me = lax.axis_index("tiles")
    z, x = lax.div(me, DEPTH_X), lax.rem(me, DEPTH_X)

    loads = [
        pltpu.make_async_copy(source, target, load_sem.at[i])
        for i, (source, target) in enumerate([
            (g_hbm, g_ref), (b_hbm, b_ref), (c_hbm, c_ref), (d_hbm, d_ref), (x_hbm, x_ref),
            (saved_row_hbm, saved_row), (saved_col_hbm, saved_col),
        ])
    ]
    for load in loads:
        load.start()

    def partner(k):
        step = TILES - 1 - k
        u, dx = lax.div(step, DEPTH_X), lax.rem(step, DEPTH_X)
        dz = lax.div(u + 1, 2) * (2 * lax.rem(u, 2) - 1)
        return lax.rem(z + dz + DEPTH_Z, DEPTH_Z) * DEPTH_X + lax.rem(x + dx, DEPTH_X)

    barrier = pltpu.get_barrier_semaphore()

    @pl.loop(0, TILES - 1)
    def _(k):
        pl.semaphore_signal(barrier, inc=1, device_id=(f, partner(k)), device_id_type=MESH)

    core, chip_y = lax.rem(f, 2), lax.div(f, 2)
    other = f + 1 - 2 * core
    above, below = lax.rem(f + 2, FRAMES), lax.rem(f + FRAMES - 2, FRAMES)
    mine, theirs = core * HALF, HALF - core * HALF
    for neighbour in (other, above, below):
        pl.semaphore_signal(barrier, inc=1, device_id=(neighbour, me), device_id_type=MESH)

    def keep_own(source, target):
        target[pl.ds(me, 1)] = source[pl.ds(me, 1)]

    def exchange(source, target, which, first=0, last=TILES - 1):
        @pl.loop(first, last)
        def _(k):
            peer = partner(k)
            pltpu.make_async_remote_copy(
                src_ref=source.at[peer],
                dst_ref=target.at[me],
                send_sem=send_sem.at[which],
                recv_sem=recv_sem.at[which],
                device_id=(f, peer),
                device_id_type=MESH,
            ).start()

    def wait_all(ref, sem):
        some = ref.at[pl.ds(0, TILES - 1)]
        pltpu.make_async_copy(some, some, sem).wait()

    def put_g(q, value):
        send_g[8 * q : 8 * q + 8] = value

    def put_x(q, value):
        send_x[8 * q : 8 * q + 8] = value

    def reader(ref):
        return lambda q, k: ref[16 * q : 16 * q + 16, pair(k)]

    for i in (1, 2, 3):
        loads[i].wait()
    decays = nt(identity(), jnp.concatenate(
        [d_ref[...], jnp.zeros((TOKENS - HEADS, TOKENS), BF)], axis=0)).astype(BF)
    b_rows, c_rows = b_ref[...], c_ref[...]
    spread_maps = maps_matrix(3, 3)
    for q in range(4):
        rows = slice(32 * q, 32 * q + 32)
        stack = jnp.concatenate([b_rows[rows], c_rows[rows], decays[rows]], axis=0)
        packed = nn(spread_maps, stack).reshape(16, 8, LANES).astype(BF)
        send_m[16 * q : 16 * q + 16] = packed
    loads[0].wait()
    pack_channels(reader(g_ref), put_g)

    pl.semaphore_wait(barrier, TILES + 2)
    exchange(send_m, got_m, 4)
    exchange(send_g, got_g, 0)
    keep_own(send_m, got_m)
    keep_own(send_g, got_g)

    @pl.when(chip_y == FRAMES // 2 - 1)
    def _():
        incoming[...] = jnp.zeros_like(incoming)

    def swap_copies(order):
        return [
            pltpu.make_async_remote_copy(
                src_ref=source,
                dst_ref=target,
                send_sem=swap_send.at[order, i],
                recv_sem=swap_recv.at[order, i],
                device_id=(other, me),
                device_id_type=MESH,
            )
            for i, (source, target) in enumerate([
                (ends.at[order], peer_ends.at[order]),
                (low.at[order, pl.ds(theirs, HALF)], peer_low.at[order]),
            ])
        ]

    def hop_copy(order, i):
        return pltpu.make_async_remote_copy(
            src_ref=outgoing.at[order, i],
            dst_ref=incoming.at[order, i],
            send_sem=hop_send.at[order, i],
            recv_sem=hop_recv.at[order, i],
            device_id=(below, me),
            device_id_type=MESH,
        )

    def give_copy(order, i):
        return pltpu.make_async_remote_copy(
            src_ref=give.at[order, i],
            dst_ref=carry.at[order, mine + i],
            send_sem=give_send.at[order, i],
            recv_sem=give_recv.at[order, i],
            device_id=(other, me),
            device_id_type=MESH,
        )

    def swapped(order):
        for copy in swap_copies(order):
            copy.wait_recv()

    def chain(order):
        for i in range(HALF):
            k = mine + i
            own_state, peer_state = term[order, k], peer_low[order, i].astype(F32)
            own_decay, peer_decay = ends[order, k, 1:2, :], peer_ends[order, k, 1:2, :]
            lower = core == 0
            lower_state = jnp.where(lower, own_state, peer_state)
            upper_state = jnp.where(lower, peer_state, own_state)
            lower_decay = jnp.where(lower, own_decay, peer_decay)
            upper_decay = jnp.where(lower, peer_decay, own_decay)

            @pl.when(chip_y < FRAMES // 2 - 1)
            def _():
                hop_copy(order, i).wait_recv()

            entering = incoming[order, i].astype(F32)
            between = upper_decay * entering + upper_state

            @pl.when(chip_y > 0)
            def _():
                outgoing[order, i] = (lower_decay * between + lower_state).astype(BF)
                hop_copy(order, i).start()

            carry[order, k] = jnp.where(lower, between, entering).astype(BF)
            give[order, i] = jnp.where(lower, entering, between).astype(BF)
            give_copy(order, i).start()

    def chain_end(order):
        for i in range(HALF):
            pltpu.make_async_copy(
                carry.at[order, theirs + i], carry.at[order, theirs + i], give_recv.at[order, i]
            ).wait()

    def chain_sent(order):
        for copy in swap_copies(order):
            copy.wait_send()
        for i in range(HALF):
            give_copy(order, i).wait_send()

            @pl.when(chip_y > 0)
            def _():
                hop_copy(order, i).wait_send()

    row_refs = (row_grow, ends.at[0], row_centred, row_headed)
    block_scales(decays, False, shrink, row_grow, ends.at[0])
    block_states(g_ref, c_rows, shrink, row_refs, term.at[0], low.at[0])
    for copy in swap_copies(0):
        copy.start()
    loads[4].wait()
    pack_channels(reader(x_ref), put_x)
    exchange(send_x, got_x, 1, 0, BEHIND)
    keep_own(send_x, got_x)

    wait_all(got_m, recv_sem.at[4])
    gather_maps = maps_matrix(3, 3, True)
    for q in range(4):
        tiles = got_m[16 * q : 16 * q + 16].astype(F32).reshape(TOKENS, LANES).astype(BF)
        piece = nn(gather_maps, tiles).astype(BF)
        for p in range(3):
            col_maps[p, 32 * q : 32 * q + 32] = piece[32 * p : 32 * p + 32]
    col_refs = (col_grow, ends.at[1], col_centred, col_headed)
    block_scales(col_maps[2], True, shrink, col_grow, ends.at[1])
    swapped(0)

    wait_all(got_g, recv_sem.at[0])
    exchange(send_x, got_x, 1, BEHIND, EARLY)

    def put_wide(q, k, value):
        wide[16 * q : 16 * q + 16, pair(k)] = value.astype(BF)

    unpack_channels(lambda q: got_g[8 * q : 8 * q + 8], put_wide)
    block_states(wide, col_maps[1], shrink, col_refs, term.at[1], low.at[1])
    for copy in swap_copies(1):
        copy.start()
    filled = EARLY + PER_HOP * (FRAMES // 2 - chip_y)
    exchange(send_x, got_x, 1, EARLY, filled)
    swapped(1)
    chain(1)

    @pl.when(chip_y > 0)
    def _():
        chain(0)

    exchange(send_x, got_x, 1, filled)
    chain_end(1)

    def put_col(k, value):
        wide[:, pair(k)] = value.astype(BF)

    grad_of_x(col_maps[0], col_maps[1], lambda k: carry[1, k], True, col_refs, tails, put_col)

    def put_back(q, value):
        back_x[8 * q : 8 * q + 8] = value

    pack_channels(reader(wide), put_back)

    @pl.when(chip_y == 0)
    def _():
        chain(0)

    exchange(back_x, home_x, 2)
    keep_own(back_x, home_x)

    wait_all(got_x, recv_sem.at[1])
    loads[6].wait()
    unpack_channels(lambda q: got_x[8 * q : 8 * q + 8], put_wide)
    col_b, col_c = grads_of_maps(
        wide, col_maps[0], col_maps[1], saved_col, True, col_refs, tails, scaled)
    col_b, col_c = col_b.astype(BF), col_c.astype(BF)
    spread_back = maps_matrix(2, 2)
    for q in range(4):
        rows = slice(32 * q, 32 * q + 32)
        stack = jnp.concatenate([col_b[rows], col_c[rows]], axis=0)
        packed = nn(spread_back, stack).reshape(16, 4, LANES).astype(BF)
        back_m[16 * q : 16 * q + 16] = packed
    exchange(back_m, home_m, 3)
    keep_own(back_m, home_m)

    def put_row(k, value):
        part_x[:, pair(k)] = value

    chain_end(0)
    grad_of_x(b_rows, c_rows, lambda k: carry[0, k], False, row_refs, tails, put_row)
    loads[5].wait()
    row_b, row_c = grads_of_maps(
        x_ref, b_rows, c_rows, saved_row, False, row_refs, tails, scaled)

    wait_all(home_x, recv_sem.at[2])

    def put_sum(q, k, value):
        rows = slice(16 * q, 16 * q + 16)
        out_x[rows, pair(k)] = (part_x[rows, pair(k)] + value).astype(BF)

    unpack_channels(lambda q: home_x[8 * q : 8 * q + 8], put_sum)

    wait_all(home_m, recv_sem.at[3])
    gather_back = maps_matrix(2, 2, True)
    for q in range(4):
        rows = slice(32 * q, 32 * q + 32)
        tiles = home_m[16 * q : 16 * q + 16].astype(F32).reshape(64, LANES).astype(BF)
        both = nn(gather_back, tiles)
        out_b[rows, :] = (row_b[rows] + both[0:32]).astype(BF)
        out_c[rows, :] = (row_c[rows] + both[32:64]).astype(BF)

    chain_sent(0)
    chain_sent(1)
    wait_all(send_m, send_sem.at[4])
    wait_all(send_g, send_sem.at[0])
    wait_all(send_x, send_sem.at[1])
    wait_all(back_x, send_sem.at[2])
    wait_all(back_m, send_sem.at[3])


def hand_over(x_in, b_in, c_in, x_out, b_out, c_out):
    x_out[...] = x_in[...]
    b_out[...] = b_in[...]
    c_out[...] = c_in[...]


def shards(inputs, grad_out, b_proj, c_proj, log_decay, saved_raster, saved_column):
    vmem = pl.BlockSpec(memory_space=pltpu.VMEM)
    out_x, out_b, out_c = pl.pallas_call(
        kernel,
        out_shape=(
            jax.ShapeDtypeStruct((TOKENS, CHANNELS), BF),
            jax.ShapeDtypeStruct((TOKENS, STATE), BF),
            jax.ShapeDtypeStruct((TOKENS, STATE), BF),
        ),
        in_specs=[pl.BlockSpec(memory_space=pltpu.HBM)] * 7,
        out_specs=(vmem, vmem, vmem),
        scratch_shapes=[
            pltpu.VMEM((TOKENS, CHANNELS), BF),
            pltpu.VMEM((TOKENS, CHANNELS), BF),
            pltpu.VMEM((TOKENS, STATE), BF),
            pltpu.VMEM((TOKENS, STATE), BF),
            pltpu.VMEM((HEADS, TOKENS), BF),
            pltpu.VMEM((CHANNELS, STATE), F32),
            pltpu.VMEM((CHANNELS, STATE), F32),
            pltpu.VMEM((TILES, 8, LANES), BF),
            pltpu.VMEM((TILES, 2, 8, LANES), BF),
            pltpu.VMEM((TILES, 2, 8, LANES), BF),
            pltpu.VMEM((TILES, 8, LANES), BF),
            pltpu.VMEM((TILES, 2, 8, LANES), BF),
            pltpu.VMEM((TILES, 2, 8, LANES), BF),
            pltpu.VMEM((TILES, 2, 8, LANES), BF),
            pltpu.VMEM((TILES, 4, LANES), BF),
            pltpu.VMEM((TILES, 2, 8, LANES), BF),
            pltpu.VMEM((TILES, 4, LANES), BF),
            pltpu.VMEM((TOKENS, CHANNELS), F32),
            pltpu.VMEM((TOKENS, CHANNELS), F32),
            pltpu.VMEM((TOKENS, CHANNELS), BF),
            pltpu.VMEM((TOKENS, CHANNELS), BF),
            pltpu.VMEM((TOKENS, CHANNELS), F32),
            pltpu.VMEM((TOKENS, CHANNELS), BF),
            pltpu.VMEM((TOKENS, CHANNELS), BF),
            pltpu.VMEM((2, PAIRS, STATE, LANES), F32),
            pltpu.VMEM((2, PAIRS, STATE, LANES), BF),
            pltpu.VMEM((2, PAIRS, 2, LANES), F32),
            pltpu.VMEM((2, HALF, STATE, LANES), BF),
            pltpu.VMEM((2, PAIRS, 2, LANES), F32),
            pltpu.VMEM((2, HALF, STATE, LANES), BF),
            pltpu.VMEM((2, HALF, STATE, LANES), BF),
            pltpu.VMEM((2, HALF, STATE, LANES), BF),
            pltpu.VMEM((2, PAIRS, STATE, LANES), BF),
            pltpu.VMEM((STATE, CHANNELS), BF),
            pltpu.VMEM((TOKENS, CHANNELS), BF),
            pltpu.VMEM((TOKENS, CHANNELS), BF),
            pltpu.VMEM((3, TOKENS, LANES), BF),
            pltpu.VMEM((TOKENS, CHANNELS), F32),
            pltpu.SemaphoreType.DMA((7,)),
            pltpu.SemaphoreType.DMA((5,)),
            pltpu.SemaphoreType.DMA((5,)),
            pltpu.SemaphoreType.DMA((2, 2)),
            pltpu.SemaphoreType.DMA((2, 2)),
            pltpu.SemaphoreType.DMA((2, HALF)),
            pltpu.SemaphoreType.DMA((2, HALF)),
            pltpu.SemaphoreType.DMA((2, HALF)),
            pltpu.SemaphoreType.DMA((2, HALF)),
        ],
        compiler_params=pltpu.CompilerParams(
            collective_id=0, has_side_effects=True, vmem_limit_bytes=63 * 1024 * 1024
        ),
        cost_estimate=pl.CostEstimate(
            flops=800_000_000, bytes_accessed=2_600_000, transcendentals=1_000_000
        ),
        name="scan_backward",
    )(
        inputs.reshape(TOKENS, CHANNELS),
        grad_out.reshape(TOKENS, CHANNELS),
        b_proj.reshape(TOKENS, STATE),
        c_proj.reshape(TOKENS, STATE),
        log_decay.reshape(HEADS, TOKENS),
        saved_raster.reshape(CHANNELS, STATE),
        saved_column.reshape(CHANNELS, STATE),
    )
    out_x, out_b, out_c = pl.pallas_call(
        hand_over,
        out_shape=(
            jax.ShapeDtypeStruct((TOKENS, CHANNELS), BF),
            jax.ShapeDtypeStruct((TOKENS, STATE), BF),
            jax.ShapeDtypeStruct((TOKENS, STATE), BF),
        ),
        in_specs=[vmem] * 3,
        out_specs=(vmem, vmem, vmem),
        compiler_params=pltpu.CompilerParams(vmem_limit_bytes=63 * 1024 * 1024),
        cost_estimate=pl.CostEstimate(flops=0, bytes_accessed=640_000, transcendentals=0),
        name="hand_over",
    )(out_x, out_b, out_c)
    return (
        out_x.reshape(1, 1, TOKENS, CHANNELS),
        out_b.reshape(1, 1, TOKENS, STATE),
        out_c.reshape(1, 1, TOKENS, STATE),
    )


def solution(mesh):
    in_specs = (
        P("frames", "tiles", None, None),
        P("frames", "tiles", None, None),
        P("frames", "tiles", None, None),
        P("frames", "tiles", None, None),
        P(None, "frames", "tiles", None),
        P("frames", "tiles", None, None, None),
        P("frames", "tiles", None, None, None),
    )
    out_specs = (
        P("frames", "tiles", None, None),
        P("frames", "tiles", None, None),
        P("frames", "tiles", None, None),
    )
    return jax.shard_map(shards, mesh=mesh, in_specs=in_specs, out_specs=out_specs, check_vma=False)
```

```python
import jax
import jax.numpy as jnp
from jax import lax
from jax.experimental import pallas as pl
from jax.experimental.pallas import tpu as pltpu
from jax.sharding import PartitionSpec as P

HEADS = 16
HEAD_DIM = 64
STATE = 128
TOKENS = 128
CHANNELS = 1024
LANES = 128
PAIRS = CHANNELS // LANES
TILES = 64
DEPTH_Z = 16
DEPTH_X = 4
FRAMES = 8
HALF = PAIRS // 2
BEHIND = 8
EARLY = 14
PER_HOP = 4
PIECES = (1, 2)
PIECES_MAX = 2
BF = jnp.bfloat16
F32 = jnp.float32
MESH = pl.DeviceIdType.MESH


def nn(a, b):
    return lax.dot_general(a, b, (((1,), (0,)), ((), ())), preferred_element_type=F32)


def nt(a, b):
    return lax.dot_general(a, b, (((1,), (1,)), ((), ())), preferred_element_type=F32)


def iota(shape, dim):
    return lax.broadcasted_iota(jnp.int32, shape, dim)


def ones_where(cond):
    return jnp.where(cond, 1.0, 0.0).astype(BF)


def square(shape=(TOKENS, TOKENS)):
    return iota(shape, 0), iota(shape, 1)


def place(index, column_order):
    if not column_order:
        return index
    return lax.shift_left(index & 1, 6) + lax.shift_right_logical(index, 1)


def causal(column_order):
    t, s = square()
    return place(s, column_order) <= place(t, column_order)


def causal_transposed(column_order):
    s, t = square()
    return place(s, column_order) <= place(t, column_order)


def high(index, bits):
    return lax.shift_right_logical(index, bits)


def interleave(back=False):
    r, c = square()
    if back:
        r, c = c, r
    return ones_where((high(r, 3) == (c & 15)) & ((r & 7) == high(c, 4)))


def identity():
    r, c = square()
    return ones_where(r == c)


def maps_matrix(bits, parts, back=False):
    shape = (16 << bits, 32 * parts)
    if back:
        c, r = square(shape[::-1])
    else:
        r, c = square(shape)
    part, token = high(c, 5), c & 31
    return ones_where(r == lax.shift_left(high(token, 1), bits) + part * 2 + (token & 1))


def pair(k):
    return slice(LANES * k, LANES * k + LANES)


def pack_channels(read, write):
    mix = interleave()
    for q in range(8):
        stack = jnp.concatenate([read(q, k) for k in range(PAIRS)], axis=0)
        write(q, nn(mix, stack).reshape(8, 2, 8, LANES).astype(BF))


def unpack_channels(read, write):
    mix = interleave(True)
    for q in range(8):
        tiles = read(q).astype(F32).reshape(TOKENS, LANES).astype(BF)
        out = nn(mix, tiles)
        for k in range(PAIRS):
            write(q, k, out[16 * k : 16 * k + 16, :])


def block_scales(decays, column_order, shrink, grow, ends):
    run = ones_where(causal(column_order))
    head, channel = square((TOKENS, LANES))
    for k in range(PAIRS):
        spread = ones_where(high(channel, 6) + 2 * k == head)
        cum = nn(run, nn(decays, spread).astype(BF))
        total = cum[TOKENS - 1 : TOKENS, :]
        middle = total * 0.5
        shrink[:, pair(k)] = jnp.exp(cum - middle)
        grow[:, pair(k)] = jnp.exp(middle - cum)
        ends[k, 0:1, :] = jnp.exp(middle)
        ends[k, 1:2, :] = jnp.exp(total)


def scale_grad(value, rows, k, shrink, refs):
    grow, ends, centred, headed = refs
    shrunk = value.astype(F32) * shrink[rows, pair(k)]
    centred[rows, pair(k)] = shrunk.astype(BF)
    headed[rows, pair(k)] = (shrunk * ends[k, 0:1, :]).astype(BF)


def block_states(c_rows, refs, term, low):
    grow, ends, centred, headed = refs
    c_turned = nt(identity(), c_rows).astype(BF)
    for k in range(PAIRS):
        state = nn(c_turned, headed[:, pair(k)])
        term[k] = state
        low[k] = state.astype(BF)


def grad_of_x(b_rows, c_rows, carry, column_order, refs, tails, write):
    grow, ends, centred, headed = refs
    pairing = jnp.where(causal_transposed(column_order), nt(b_rows, c_rows), 0.0).astype(BF)
    both = jnp.concatenate([pairing, b_rows], axis=1)
    for k in range(PAIRS):
        tail = (carry(k).astype(F32) * ends[k, 0:1, :]).astype(BF)
        tails[:, pair(k)] = tail
        stack = jnp.concatenate([centred[:, pair(k)], tail], axis=0)
        write(k, nn(both, stack) * grow[:, pair(k)])


def grads_of_maps(x, b_rows, c_rows, saved, column_order, refs, tails, scaled):
    grow, ends, centred, headed = refs
    for k in range(PAIRS):
        scaled[:, pair(k)] = (x[:, pair(k)].astype(F32) * grow[:, pair(k)]).astype(BF)
    mixed = jnp.where(causal(column_order), nt(centred[...], scaled[...]), 0.0)
    part_b = nn(mixed.T.astype(BF), c_rows) + nt(scaled[...], tails[...])
    part_c = nn(mixed.astype(BF), b_rows) + nn(headed[...], saved[...].astype(BF))
    return part_b, part_c


def kernel(
    x_hbm, g_hbm, b_hbm, c_hbm, d_hbm, saved_row_hbm, saved_col_hbm,
    out_x_hbm, out_b_hbm, out_c_hbm,
    out_x, out_b, out_c,
    x_ref, g_ref, b_ref, c_ref, d_ref, saved_row, saved_col,
    send_m, send_g, send_x, got_m, got_g, got_x, back_x, back_m, home_x, home_m,
    shrink, row_grow, row_centred, row_headed, col_grow, col_centred, col_headed,
    term, low, ends, peer_low, peer_ends, incoming, outgoing, give, carry,
    tails, scaled, wide, col_maps, part_x,
    load_sem, store_sem, send_sem, recv_sem, swap_send, swap_recv, hop_send, hop_recv, give_send, give_recv,
):
    f = lax.axis_index("frames")
    me = lax.axis_index("tiles")
    z, x = lax.div(me, DEPTH_X), lax.rem(me, DEPTH_X)

    loads = [
        pltpu.make_async_copy(source, target, load_sem.at[i])
        for i, (source, target) in enumerate([
            (g_hbm, g_ref), (b_hbm, b_ref), (c_hbm, c_ref), (d_hbm, d_ref), (x_hbm, x_ref),
            (saved_row_hbm, saved_row), (saved_col_hbm, saved_col),
        ])
    ]
    for load in loads:
        load.start()

    def partner(k):
        step = TILES - 1 - k
        u, dx = lax.div(step, DEPTH_X), lax.rem(step, DEPTH_X)
        dz = lax.div(u + 1, 2) * (2 * lax.rem(u, 2) - 1)
        return lax.rem(z + dz + DEPTH_Z, DEPTH_Z) * DEPTH_X + lax.rem(x + dx, DEPTH_X)

    barrier = pltpu.get_barrier_semaphore()

    @pl.loop(0, TILES - 1)
    def _(k):
        pl.semaphore_signal(barrier, inc=1, device_id=(f, partner(k)), device_id_type=MESH)

    core, chip_y = lax.rem(f, 2), lax.div(f, 2)
    other = f + 1 - 2 * core
    above, below = lax.rem(f + 2, FRAMES), lax.rem(f + FRAMES - 2, FRAMES)
    mine, theirs = core * HALF, HALF - core * HALF
    for neighbour in (other, above, below):
        pl.semaphore_signal(barrier, inc=1, device_id=(neighbour, me), device_id_type=MESH)

    def keep_own(source, target):
        target[pl.ds(me, 1)] = source[pl.ds(me, 1)]

    def exchange(source, target, which, first=0, last=TILES - 1):
        @pl.loop(first, last)
        def _(k):
            peer = partner(k)
            pltpu.make_async_remote_copy(
                src_ref=source.at[peer],
                dst_ref=target.at[me],
                send_sem=send_sem.at[which],
                recv_sem=recv_sem.at[which],
                device_id=(f, peer),
                device_id_type=MESH,
            ).start()

    def wait_all(ref, sem):
        some = ref.at[pl.ds(0, TILES - 1)]
        pltpu.make_async_copy(some, some, sem).wait()

    def put_g(q, value):
        send_g[8 * q : 8 * q + 8] = value

    def put_x(q, value):
        send_x[8 * q : 8 * q + 8] = value

    def reader(ref):
        return lambda q, k: ref[16 * q : 16 * q + 16, pair(k)]

    for i in (1, 2, 3):
        loads[i].wait()
    decays = nt(identity(), jnp.concatenate(
        [d_ref[...], jnp.zeros((TOKENS - HEADS, TOKENS), BF)], axis=0)).astype(BF)
    b_rows, c_rows = b_ref[...], c_ref[...]
    spread_maps = maps_matrix(3, 3)
    for q in range(4):
        rows = slice(32 * q, 32 * q + 32)
        stack = jnp.concatenate([b_rows[rows], c_rows[rows], decays[rows]], axis=0)
        packed = nn(spread_maps, stack).reshape(16, 8, LANES).astype(BF)
        send_m[16 * q : 16 * q + 16] = packed
    pl.semaphore_wait(barrier, TILES + 2)
    exchange(send_m, got_m, 4)
    loads[0].wait()
    pack_channels(reader(g_ref), put_g)
    exchange(send_g, got_g, 0)
    keep_own(send_m, got_m)
    keep_own(send_g, got_g)

    @pl.when(chip_y == FRAMES // 2 - 1)
    def _():
        incoming[...] = jnp.zeros_like(incoming)

    def swap_copies(order):
        return [
            pltpu.make_async_remote_copy(
                src_ref=source,
                dst_ref=target,
                send_sem=swap_send.at[order, i],
                recv_sem=swap_recv.at[order, i],
                device_id=(other, me),
                device_id_type=MESH,
            )
            for i, (source, target) in enumerate([
                (ends.at[order], peer_ends.at[order]),
                (low.at[order, pl.ds(theirs, HALF)], peer_low.at[order]),
            ])
        ]

    def rows_of(order, p):
        rows = STATE // PIECES[order]
        return pl.ds(rows * p, rows)

    def hop_copy(order, i, p):
        return pltpu.make_async_remote_copy(
            src_ref=outgoing.at[order, i, rows_of(order, p)],
            dst_ref=incoming.at[order, i, rows_of(order, p)],
            send_sem=hop_send.at[order, i, p],
            recv_sem=hop_recv.at[order, i, p],
            device_id=(below, me),
            device_id_type=MESH,
        )

    def give_copy(order, i, p):
        return pltpu.make_async_remote_copy(
            src_ref=give.at[order, i, rows_of(order, p)],
            dst_ref=carry.at[order, mine + i, rows_of(order, p)],
            send_sem=give_send.at[order, i, p],
            recv_sem=give_recv.at[order, i, p],
            device_id=(other, me),
            device_id_type=MESH,
        )

    def swapped(order):
        for copy in swap_copies(order):
            copy.wait_recv()

    def steps(order):
        return [(i, p) for i in range(HALF) for p in range(PIECES[order])]

    def chain(order):
        lower = core == 0
        for i, p in steps(order):
            k, rows = mine + i, rows_of(order, p)

            @pl.when(chip_y < FRAMES // 2 - 1)
            def _():
                hop_copy(order, i, p).wait_recv()

            own_state, peer_state = term[order, k, rows], peer_low[order, i, rows].astype(F32)
            own_decay, peer_decay = ends[order, k, 1:2, :], peer_ends[order, k, 1:2, :]
            lower_state = jnp.where(lower, own_state, peer_state)
            upper_state = jnp.where(lower, peer_state, own_state)
            lower_decay = jnp.where(lower, own_decay, peer_decay)
            upper_decay = jnp.where(lower, peer_decay, own_decay)
            entering = incoming[order, i, rows].astype(F32)
            between = upper_decay * entering + upper_state

            @pl.when(chip_y > 0)
            def _():
                outgoing[order, i, rows] = (lower_decay * between + lower_state).astype(BF)
                hop_copy(order, i, p).start()

            carry[order, k, rows] = jnp.where(lower, between, entering).astype(BF)
            give[order, i, rows] = jnp.where(lower, entering, between).astype(BF)
            give_copy(order, i, p).start()

    def chain_end(order):
        for i, p in steps(order):
            some = carry.at[order, theirs + i, rows_of(order, p)]
            pltpu.make_async_copy(some, some, give_recv.at[order, i, p]).wait()

    def chain_sent(order):
        for copy in swap_copies(order):
            copy.wait_send()
        for i, p in steps(order):
            give_copy(order, i, p).wait_send()

            @pl.when(chip_y > 0)
            def _():
                hop_copy(order, i, p).wait_send()

    row_refs = (row_grow, ends.at[0], row_centred, row_headed)
    block_scales(decays, False, shrink, row_grow, ends.at[0])
    for k in range(PAIRS):
        scale_grad(g_ref[:, pair(k)], slice(0, TOKENS), k, shrink, row_refs)
    block_states(c_rows, row_refs, term.at[0], low.at[0])
    for copy in swap_copies(0):
        copy.start()
    loads[4].wait()
    pack_channels(reader(x_ref), put_x)
    exchange(send_x, got_x, 1, 0, BEHIND)
    keep_own(send_x, got_x)

    wait_all(got_m, recv_sem.at[4])
    gather_maps = maps_matrix(3, 3, True)
    for q in range(4):
        tiles = got_m[16 * q : 16 * q + 16].astype(F32).reshape(TOKENS, LANES).astype(BF)
        piece = nn(gather_maps, tiles).astype(BF)
        for p in range(3):
            col_maps[p, 32 * q : 32 * q + 32] = piece[32 * p : 32 * p + 32]
    col_refs = (col_grow, ends.at[1], col_centred, col_headed)
    block_scales(col_maps[2], True, shrink, col_grow, ends.at[1])
    swapped(0)

    wait_all(got_g, recv_sem.at[0])
    exchange(send_x, got_x, 1, BEHIND, EARLY)

    def put_wide(q, k, value):
        wide[16 * q : 16 * q + 16, pair(k)] = value.astype(BF)

    def put_scaled(q, k, value):
        scale_grad(value, slice(16 * q, 16 * q + 16), k, shrink, col_refs)

    unpack_channels(lambda q: got_g[8 * q : 8 * q + 8], put_scaled)
    block_states(col_maps[1], col_refs, term.at[1], low.at[1])
    for copy in swap_copies(1):
        copy.start()
    filled = EARLY + PER_HOP * (FRAMES // 2 - chip_y)
    exchange(send_x, got_x, 1, EARLY, filled)
    swapped(1)
    chain(1)

    @pl.when(chip_y > 0)
    def _():
        chain(0)

    exchange(send_x, got_x, 1, filled)
    chain_end(1)

    def put_col(k, value):
        wide[:, pair(k)] = value.astype(BF)

    grad_of_x(col_maps[0], col_maps[1], lambda k: carry[1, k], True, col_refs, tails, put_col)

    def put_back(q, value):
        back_x[8 * q : 8 * q + 8] = value

    pack_channels(reader(wide), put_back)

    @pl.when(chip_y == 0)
    def _():
        chain(0)

    exchange(back_x, home_x, 2)
    keep_own(back_x, home_x)

    wait_all(got_x, recv_sem.at[1])
    loads[6].wait()
    unpack_channels(lambda q: got_x[8 * q : 8 * q + 8], put_wide)
    col_b, col_c = grads_of_maps(
        wide, col_maps[0], col_maps[1], saved_col, True, col_refs, tails, scaled)
    col_b, col_c = col_b.astype(BF), col_c.astype(BF)
    spread_back = maps_matrix(2, 2)
    for q in range(4):
        rows = slice(32 * q, 32 * q + 32)
        stack = jnp.concatenate([col_b[rows], col_c[rows]], axis=0)
        packed = nn(spread_back, stack).reshape(16, 4, LANES).astype(BF)
        back_m[16 * q : 16 * q + 16] = packed
    exchange(back_m, home_m, 3)
    keep_own(back_m, home_m)

    def put_row(k, value):
        part_x[:, pair(k)] = value

    chain_end(0)
    grad_of_x(b_rows, c_rows, lambda k: carry[0, k], False, row_refs, tails, put_row)
    loads[5].wait()
    row_b, row_c = grads_of_maps(
        x_ref, b_rows, c_rows, saved_row, False, row_refs, tails, scaled)

    wait_all(home_x, recv_sem.at[2])

    def put_sum(q, k, value):
        rows = slice(16 * q, 16 * q + 16)
        out_x[rows, pair(k)] = (part_x[rows, pair(k)] + value).astype(BF)

    unpack_channels(lambda q: home_x[8 * q : 8 * q + 8], put_sum)

    stores = [
        pltpu.make_async_copy(source, target, store_sem.at[i])
        for i, (source, target) in enumerate(
            [(out_x, out_x_hbm), (out_b, out_b_hbm), (out_c, out_c_hbm)])
    ]
    stores[0].start()

    wait_all(home_m, recv_sem.at[3])
    gather_back = maps_matrix(2, 2, True)
    for q in range(4):
        rows = slice(32 * q, 32 * q + 32)
        tiles = home_m[16 * q : 16 * q + 16].astype(F32).reshape(64, LANES).astype(BF)
        both = nn(gather_back, tiles)
        out_b[rows, :] = (row_b[rows] + both[0:32]).astype(BF)
        out_c[rows, :] = (row_c[rows] + both[32:64]).astype(BF)

    stores[1].start()
    stores[2].start()
    chain_sent(0)
    chain_sent(1)
    wait_all(send_m, send_sem.at[4])
    wait_all(send_g, send_sem.at[0])
    wait_all(send_x, send_sem.at[1])
    wait_all(back_x, send_sem.at[2])
    wait_all(back_m, send_sem.at[3])
    for store in stores:
        store.wait()


def hand_over(x_in, b_in, c_in, x_out, b_out, c_out, x_held, b_held, c_held, load_sem, store_sem):
    parts = [(x_in, x_held, x_out), (b_in, b_held, b_out), (c_in, c_held, c_out)]
    loads = [pltpu.make_async_copy(p[0], p[1], load_sem.at[i]) for i, p in enumerate(parts)]
    stores = [pltpu.make_async_copy(p[1], p[2], store_sem.at[i]) for i, p in enumerate(parts)]
    for load in loads:
        load.start()
    for load, store in zip(loads, stores):
        load.wait()
        store.start()
    for store in stores:
        store.wait()


def shards(inputs, grad_out, b_proj, c_proj, log_decay, saved_raster, saved_column):
    anywhere = pl.BlockSpec(memory_space=pl.ANY)
    out_x, out_b, out_c = pl.pallas_call(
        kernel,
        out_shape=(
            jax.ShapeDtypeStruct((TOKENS, CHANNELS), BF),
            jax.ShapeDtypeStruct((TOKENS, STATE), BF),
            jax.ShapeDtypeStruct((TOKENS, STATE), BF),
        ),
        in_specs=[pl.BlockSpec(memory_space=pltpu.HBM)] * 7,
        out_specs=(anywhere, anywhere, anywhere),
        scratch_shapes=[
            pltpu.VMEM((TOKENS, CHANNELS), BF),
            pltpu.VMEM((TOKENS, STATE), BF),
            pltpu.VMEM((TOKENS, STATE), BF),
            pltpu.VMEM((TOKENS, CHANNELS), BF),
            pltpu.VMEM((TOKENS, CHANNELS), BF),
            pltpu.VMEM((TOKENS, STATE), BF),
            pltpu.VMEM((TOKENS, STATE), BF),
            pltpu.VMEM((HEADS, TOKENS), BF),
            pltpu.VMEM((CHANNELS, STATE), F32),
            pltpu.VMEM((CHANNELS, STATE), F32),
            pltpu.VMEM((TILES, 8, LANES), BF),
            pltpu.VMEM((TILES, 2, 8, LANES), BF),
            pltpu.VMEM((TILES, 2, 8, LANES), BF),
            pltpu.VMEM((TILES, 8, LANES), BF),
            pltpu.VMEM((TILES, 2, 8, LANES), BF),
            pltpu.VMEM((TILES, 2, 8, LANES), BF),
            pltpu.VMEM((TILES, 2, 8, LANES), BF),
            pltpu.VMEM((TILES, 4, LANES), BF),
            pltpu.VMEM((TILES, 2, 8, LANES), BF),
            pltpu.VMEM((TILES, 4, LANES), BF),
            pltpu.VMEM((TOKENS, CHANNELS), F32),
            pltpu.VMEM((TOKENS, CHANNELS), F32),
            pltpu.VMEM((TOKENS, CHANNELS), BF),
            pltpu.VMEM((TOKENS, CHANNELS), BF),
            pltpu.VMEM((TOKENS, CHANNELS), F32),
            pltpu.VMEM((TOKENS, CHANNELS), BF),
            pltpu.VMEM((TOKENS, CHANNELS), BF),
            pltpu.VMEM((2, PAIRS, STATE, LANES), F32),
            pltpu.VMEM((2, PAIRS, STATE, LANES), BF),
            pltpu.VMEM((2, PAIRS, 2, LANES), F32),
            pltpu.VMEM((2, HALF, STATE, LANES), BF),
            pltpu.VMEM((2, PAIRS, 2, LANES), F32),
            pltpu.VMEM((2, HALF, STATE, LANES), BF),
            pltpu.VMEM((2, HALF, STATE, LANES), BF),
            pltpu.VMEM((2, HALF, STATE, LANES), BF),
            pltpu.VMEM((2, PAIRS, STATE, LANES), BF),
            pltpu.VMEM((STATE, CHANNELS), BF),
            pltpu.VMEM((TOKENS, CHANNELS), BF),
            pltpu.VMEM((TOKENS, CHANNELS), BF),
            pltpu.VMEM((3, TOKENS, LANES), BF),
            pltpu.VMEM((TOKENS, CHANNELS), F32),
            pltpu.SemaphoreType.DMA((7,)),
            pltpu.SemaphoreType.DMA((3,)),
            pltpu.SemaphoreType.DMA((5,)),
            pltpu.SemaphoreType.DMA((5,)),
            pltpu.SemaphoreType.DMA((2, 2)),
            pltpu.SemaphoreType.DMA((2, 2)),
            pltpu.SemaphoreType.DMA((2, HALF, PIECES_MAX)),
            pltpu.SemaphoreType.DMA((2, HALF, PIECES_MAX)),
            pltpu.SemaphoreType.DMA((2, HALF, PIECES_MAX)),
            pltpu.SemaphoreType.DMA((2, HALF, PIECES_MAX)),
        ],
        compiler_params=pltpu.CompilerParams(
            collective_id=0, has_side_effects=True, vmem_limit_bytes=63 * 1024 * 1024
        ),
        cost_estimate=pl.CostEstimate(
            flops=800_000_000, bytes_accessed=2_600_000, transcendentals=1_000_000
        ),
        name="scan_backward",
    )(
        inputs.reshape(TOKENS, CHANNELS),
        grad_out.reshape(TOKENS, CHANNELS),
        b_proj.reshape(TOKENS, STATE),
        c_proj.reshape(TOKENS, STATE),
        log_decay.reshape(HEADS, TOKENS),
        saved_raster.reshape(CHANNELS, STATE),
        saved_column.reshape(CHANNELS, STATE),
    )
    out_x, out_b, out_c = pl.pallas_call(
        hand_over,
        out_shape=(
            jax.ShapeDtypeStruct((TOKENS, CHANNELS), BF),
            jax.ShapeDtypeStruct((TOKENS, STATE), BF),
            jax.ShapeDtypeStruct((TOKENS, STATE), BF),
        ),
        in_specs=[anywhere] * 3,
        out_specs=(anywhere, anywhere, anywhere),
        scratch_shapes=[
            pltpu.VMEM((TOKENS, CHANNELS), BF),
            pltpu.VMEM((TOKENS, STATE), BF),
            pltpu.VMEM((TOKENS, STATE), BF),
            pltpu.SemaphoreType.DMA((3,)),
            pltpu.SemaphoreType.DMA((3,)),
        ],
        compiler_params=pltpu.CompilerParams(vmem_limit_bytes=63 * 1024 * 1024),
        cost_estimate=pl.CostEstimate(flops=0, bytes_accessed=640_000, transcendentals=0),
        name="hand_over",
    )(out_x, out_b, out_c)
    return (
        out_x.reshape(1, 1, TOKENS, CHANNELS),
        out_b.reshape(1, 1, TOKENS, STATE),
        out_c.reshape(1, 1, TOKENS, STATE),
    )


def solution(mesh):
    in_specs = (
        P("frames", "tiles", None, None),
        P("frames", "tiles", None, None),
        P("frames", "tiles", None, None),
        P("frames", "tiles", None, None),
        P(None, "frames", "tiles", None),
        P("frames", "tiles", None, None, None),
        P("frames", "tiles", None, None, None),
    )
    out_specs = (
        P("frames", "tiles", None, None),
        P("frames", "tiles", None, None),
        P("frames", "tiles", None, None),
    )
    return jax.shard_map(shards, mesh=mesh, in_specs=in_specs, out_specs=out_specs, check_vma=False)
```

```python
import jax
import jax.numpy as jnp
from jax import lax
from jax.experimental import pallas as pl
from jax.experimental.pallas import tpu as pltpu
from jax.sharding import PartitionSpec as P

HEADS = 16
HEAD_DIM = 64
STATE = 128
TOKENS = 128
CHANNELS = 1024
LANES = 128
PAIRS = CHANNELS // LANES
TILES = 64
DEPTH_Z = 16
DEPTH_X = 4
FRAMES = 8
HALF = PAIRS // 2
BEHIND = 8
EARLY = 14
PER_HOP = 4
MEANWHILE = 12
PIECES = (1, 2)
PIECES_MAX = 2
BF = jnp.bfloat16
F32 = jnp.float32
MESH = pl.DeviceIdType.MESH


def nn(a, b):
    return lax.dot_general(a, b, (((1,), (0,)), ((), ())), preferred_element_type=F32)


def nt(a, b):
    return lax.dot_general(a, b, (((1,), (1,)), ((), ())), preferred_element_type=F32)


def iota(shape, dim):
    return lax.broadcasted_iota(jnp.int32, shape, dim)


def ones_where(cond):
    return jnp.where(cond, 1.0, 0.0).astype(BF)


def square(shape=(TOKENS, TOKENS)):
    return iota(shape, 0), iota(shape, 1)


def place(index, column_order):
    if not column_order:
        return index
    return lax.shift_left(index & 1, 6) + lax.shift_right_logical(index, 1)


def causal(column_order):
    t, s = square()
    return place(s, column_order) <= place(t, column_order)


def causal_transposed(column_order):
    s, t = square()
    return place(s, column_order) <= place(t, column_order)


def high(index, bits):
    return lax.shift_right_logical(index, bits)


def interleave(back=False):
    r, c = square()
    if back:
        r, c = c, r
    return ones_where((high(r, 3) == (c & 15)) & ((r & 7) == high(c, 4)))


def identity():
    r, c = square()
    return ones_where(r == c)


def maps_matrix(bits, parts, back=False):
    shape = (16 << bits, 32 * parts)
    if back:
        c, r = square(shape[::-1])
    else:
        r, c = square(shape)
    part, token = high(c, 5), c & 31
    return ones_where(r == lax.shift_left(high(token, 1), bits) + part * 2 + (token & 1))


def pair(k):
    return slice(LANES * k, LANES * k + LANES)


def pack_channels(read, write):
    mix = interleave()
    for q in range(8):
        stack = jnp.concatenate([read(q, k) for k in range(PAIRS)], axis=0)
        write(q, nn(mix, stack).reshape(8, 2, 8, LANES).astype(BF))


def unpack_channels(read, write):
    mix = interleave(True)
    for q in range(8):
        tiles = read(q).astype(F32).reshape(TOKENS, LANES).astype(BF)
        out = nn(mix, tiles)
        for k in range(PAIRS):
            write(q, k, out[16 * k : 16 * k + 16, :])


def block_scales(decays, column_order, shrink, grow, ends):
    run = ones_where(causal(column_order))
    head, channel = square((TOKENS, LANES))
    for k in range(PAIRS):
        spread = ones_where(high(channel, 6) + 2 * k == head)
        cum = nn(run, nn(decays, spread).astype(BF))
        total = cum[TOKENS - 1 : TOKENS, :]
        middle = total * 0.5
        shrink[:, pair(k)] = jnp.exp(cum - middle)
        grow[:, pair(k)] = jnp.exp(middle - cum)
        ends[k, 0:1, :] = jnp.exp(middle)
        ends[k, 1:2, :] = jnp.exp(total)


def scale_grad(value, rows, k, shrink, refs):
    grow, ends, centred, headed = refs
    shrunk = value.astype(F32) * shrink[rows, pair(k)]
    centred[rows, pair(k)] = shrunk.astype(BF)
    headed[rows, pair(k)] = (shrunk * ends[k, 0:1, :]).astype(BF)


def block_states(c_rows, refs, term, low):
    grow, ends, centred, headed = refs
    c_turned = nt(identity(), c_rows).astype(BF)
    for k in range(PAIRS):
        state = nn(c_turned, headed[:, pair(k)])
        term[k] = state
        low[k] = state.astype(BF)


def grad_of_x(b_rows, c_rows, carry, column_order, refs, tails, write):
    grow, ends, centred, headed = refs
    pairing = jnp.where(causal_transposed(column_order), nt(b_rows, c_rows), 0.0).astype(BF)
    both = jnp.concatenate([pairing, b_rows], axis=1)
    for k in range(PAIRS):
        tail = (carry(k).astype(F32) * ends[k, 0:1, :]).astype(BF)
        tails[:, pair(k)] = tail
        stack = jnp.concatenate([centred[:, pair(k)], tail], axis=0)
        write(k, nn(both, stack) * grow[:, pair(k)])


def grads_of_maps(x, b_rows, c_rows, saved, column_order, refs, tails, scaled):
    grow, ends, centred, headed = refs
    for k in range(PAIRS):
        scaled[:, pair(k)] = (x[:, pair(k)].astype(F32) * grow[:, pair(k)]).astype(BF)
    mixed = jnp.where(causal(column_order), nt(centred[...], scaled[...]), 0.0)
    part_b = nn(mixed.T.astype(BF), c_rows) + nt(scaled[...], tails[...])
    part_c = nn(mixed.astype(BF), b_rows) + nn(headed[...], saved[...].astype(BF))
    return part_b, part_c


def kernel(
    x_hbm, g_hbm, b_hbm, c_hbm, d_hbm, saved_row_hbm, saved_col_hbm,
    out_x_hbm, out_b_hbm, out_c_hbm,
    out_x, out_b, out_c,
    x_ref, g_ref, b_ref, c_ref, d_ref, saved_row, saved_col,
    send_m, send_g, send_x, got_m, got_g, got_x, back_x, back_m, home_x, home_m,
    shrink, row_grow, row_centred, row_headed, col_grow, col_centred, col_headed,
    term, low, ends, peer_low, peer_ends, incoming, outgoing, give, carry,
    tails, scaled, wide, col_maps, part_x,
    load_sem, store_sem, send_sem, recv_sem, swap_send, swap_recv, hop_send, hop_recv, give_send, give_recv,
):
    f = lax.axis_index("frames")
    me = lax.axis_index("tiles")
    z, x = lax.div(me, DEPTH_X), lax.rem(me, DEPTH_X)

    loads = [
        pltpu.make_async_copy(source, target, load_sem.at[i])
        for i, (source, target) in enumerate([
            (g_hbm, g_ref), (b_hbm, b_ref), (c_hbm, c_ref), (d_hbm, d_ref), (x_hbm, x_ref),
            (saved_row_hbm, saved_row), (saved_col_hbm, saved_col),
        ])
    ]
    for load in loads:
        load.start()

    def partner(k):
        step = TILES - 1 - k
        u, dx = lax.div(step, DEPTH_X), lax.rem(step, DEPTH_X)
        dz = lax.div(u + 1, 2) * (2 * lax.rem(u, 2) - 1)
        return lax.rem(z + dz + DEPTH_Z, DEPTH_Z) * DEPTH_X + lax.rem(x + dx, DEPTH_X)

    barrier = pltpu.get_barrier_semaphore()

    @pl.loop(0, TILES - 1)
    def _(k):
        pl.semaphore_signal(barrier, inc=1, device_id=(f, partner(k)), device_id_type=MESH)

    core, chip_y = lax.rem(f, 2), lax.div(f, 2)
    other = f + 1 - 2 * core
    above, below = lax.rem(f + 2, FRAMES), lax.rem(f + FRAMES - 2, FRAMES)
    mine, theirs = core * HALF, HALF - core * HALF
    for neighbour in (other, above, below):
        pl.semaphore_signal(barrier, inc=1, device_id=(neighbour, me), device_id_type=MESH)

    def keep_own(source, target):
        target[pl.ds(me, 1)] = source[pl.ds(me, 1)]

    def exchange(source, target, which, first=0, last=TILES - 1):
        @pl.loop(first, last)
        def _(k):
            peer = partner(k)
            pltpu.make_async_remote_copy(
                src_ref=source.at[peer],
                dst_ref=target.at[me],
                send_sem=send_sem.at[which],
                recv_sem=recv_sem.at[which],
                device_id=(f, peer),
                device_id_type=MESH,
            ).start()

    def wait_all(ref, sem):
        some = ref.at[pl.ds(0, TILES - 1)]
        pltpu.make_async_copy(some, some, sem).wait()

    def put_g(q, value):
        send_g[8 * q : 8 * q + 8] = value

    def put_x(q, value):
        send_x[8 * q : 8 * q + 8] = value

    def reader(ref):
        return lambda q, k: ref[16 * q : 16 * q + 16, pair(k)]

    for i in (1, 2, 3):
        loads[i].wait()
    decays = nt(identity(), jnp.concatenate(
        [d_ref[...], jnp.zeros((TOKENS - HEADS, TOKENS), BF)], axis=0)).astype(BF)
    b_rows, c_rows = b_ref[...], c_ref[...]
    spread_maps = maps_matrix(3, 3)
    for q in range(4):
        rows = slice(32 * q, 32 * q + 32)
        stack = jnp.concatenate([b_rows[rows], c_rows[rows], decays[rows]], axis=0)
        packed = nn(spread_maps, stack).reshape(16, 8, LANES).astype(BF)
        send_m[16 * q : 16 * q + 16] = packed
    pl.semaphore_wait(barrier, TILES + 2)
    exchange(send_m, got_m, 4)
    loads[0].wait()
    pack_channels(reader(g_ref), put_g)
    exchange(send_g, got_g, 0)
    keep_own(send_m, got_m)
    keep_own(send_g, got_g)

    @pl.when(chip_y == FRAMES // 2 - 1)
    def _():
        incoming[...] = jnp.zeros_like(incoming)

    def swap_copies(order):
        return [
            pltpu.make_async_remote_copy(
                src_ref=source,
                dst_ref=target,
                send_sem=swap_send.at[order, i],
                recv_sem=swap_recv.at[order, i],
                device_id=(other, me),
                device_id_type=MESH,
            )
            for i, (source, target) in enumerate([
                (ends.at[order], peer_ends.at[order]),
                (low.at[order, pl.ds(theirs, HALF)], peer_low.at[order]),
            ])
        ]

    def rows_of(order, p):
        rows = STATE // PIECES[order]
        return pl.ds(rows * p, rows)

    def hop_copy(order, i, p):
        return pltpu.make_async_remote_copy(
            src_ref=outgoing.at[order, i, rows_of(order, p)],
            dst_ref=incoming.at[order, i, rows_of(order, p)],
            send_sem=hop_send.at[order, i, p],
            recv_sem=hop_recv.at[order, i, p],
            device_id=(below, me),
            device_id_type=MESH,
        )

    def give_copy(order, i, p):
        return pltpu.make_async_remote_copy(
            src_ref=give.at[order, i, rows_of(order, p)],
            dst_ref=carry.at[order, mine + i, rows_of(order, p)],
            send_sem=give_send.at[order, i, p],
            recv_sem=give_recv.at[order, i, p],
            device_id=(other, me),
            device_id_type=MESH,
        )

    def swapped(order):
        for copy in swap_copies(order):
            copy.wait_recv()

    def steps(order):
        return [(i, p) for i in range(HALF) for p in range(PIECES[order])]

    def chain(order):
        lower = core == 0
        for i, p in steps(order):
            k, rows = mine + i, rows_of(order, p)

            @pl.when(chip_y < FRAMES // 2 - 1)
            def _():
                hop_copy(order, i, p).wait_recv()

            own_state, peer_state = term[order, k, rows], peer_low[order, i, rows].astype(F32)
            own_decay, peer_decay = ends[order, k, 1:2, :], peer_ends[order, k, 1:2, :]
            lower_state = jnp.where(lower, own_state, peer_state)
            upper_state = jnp.where(lower, peer_state, own_state)
            lower_decay = jnp.where(lower, own_decay, peer_decay)
            upper_decay = jnp.where(lower, peer_decay, own_decay)
            entering = incoming[order, i, rows].astype(F32)
            between = upper_decay * entering + upper_state

            @pl.when(chip_y > 0)
            def _():
                outgoing[order, i, rows] = (lower_decay * between + lower_state).astype(BF)
                hop_copy(order, i, p).start()

            carry[order, k, rows] = jnp.where(lower, between, entering).astype(BF)
            give[order, i, rows] = jnp.where(lower, entering, between).astype(BF)
            give_copy(order, i, p).start()

    def chain_end(order):
        for i, p in steps(order):
            some = carry.at[order, theirs + i, rows_of(order, p)]
            pltpu.make_async_copy(some, some, give_recv.at[order, i, p]).wait()

    def chain_sent(order):
        for copy in swap_copies(order):
            copy.wait_send()
        for i, p in steps(order):
            give_copy(order, i, p).wait_send()

            @pl.when(chip_y > 0)
            def _():
                hop_copy(order, i, p).wait_send()

    row_refs = (row_grow, ends.at[0], row_centred, row_headed)
    block_scales(decays, False, shrink, row_grow, ends.at[0])
    for k in range(PAIRS):
        scale_grad(g_ref[:, pair(k)], slice(0, TOKENS), k, shrink, row_refs)
    block_states(c_rows, row_refs, term.at[0], low.at[0])
    for copy in swap_copies(0):
        copy.start()
    loads[4].wait()
    pack_channels(reader(x_ref), put_x)
    exchange(send_x, got_x, 1, 0, BEHIND)
    keep_own(send_x, got_x)

    wait_all(got_m, recv_sem.at[4])
    gather_maps = maps_matrix(3, 3, True)
    for q in range(4):
        tiles = got_m[16 * q : 16 * q + 16].astype(F32).reshape(TOKENS, LANES).astype(BF)
        piece = nn(gather_maps, tiles).astype(BF)
        for p in range(3):
            col_maps[p, 32 * q : 32 * q + 32] = piece[32 * p : 32 * p + 32]
    col_refs = (col_grow, ends.at[1], col_centred, col_headed)
    block_scales(col_maps[2], True, shrink, col_grow, ends.at[1])
    swapped(0)

    wait_all(got_g, recv_sem.at[0])
    exchange(send_x, got_x, 1, BEHIND, EARLY)

    def put_wide(q, k, value):
        wide[16 * q : 16 * q + 16, pair(k)] = value.astype(BF)

    def put_scaled(q, k, value):
        scale_grad(value, slice(16 * q, 16 * q + 16), k, shrink, col_refs)

    unpack_channels(lambda q: got_g[8 * q : 8 * q + 8], put_scaled)
    block_states(col_maps[1], col_refs, term.at[1], low.at[1])
    for copy in swap_copies(1):
        copy.start()
    filled = EARLY + PER_HOP * (FRAMES // 2 - chip_y)
    exchange(send_x, got_x, 1, EARLY, filled)
    swapped(1)
    chain(1)
    exchange(send_x, got_x, 1, filled, filled + MEANWHILE)
    chain_end(1)

    def put_col(k, value):
        wide[:, pair(k)] = value.astype(BF)

    grad_of_x(col_maps[0], col_maps[1], lambda k: carry[1, k], True, col_refs, tails, put_col)

    def put_back(q, value):
        back_x[8 * q : 8 * q + 8] = value

    pack_channels(reader(wide), put_back)
    chain(0)
    exchange(send_x, got_x, 1, filled + MEANWHILE)
    exchange(back_x, home_x, 2)
    keep_own(back_x, home_x)

    wait_all(got_x, recv_sem.at[1])
    loads[6].wait()
    unpack_channels(lambda q: got_x[8 * q : 8 * q + 8], put_wide)
    col_b, col_c = grads_of_maps(
        wide, col_maps[0], col_maps[1], saved_col, True, col_refs, tails, scaled)
    col_b, col_c = col_b.astype(BF), col_c.astype(BF)
    spread_back = maps_matrix(2, 2)
    for q in range(4):
        rows = slice(32 * q, 32 * q + 32)
        stack = jnp.concatenate([col_b[rows], col_c[rows]], axis=0)
        packed = nn(spread_back, stack).reshape(16, 4, LANES).astype(BF)
        back_m[16 * q : 16 * q + 16] = packed
    exchange(back_m, home_m, 3)
    keep_own(back_m, home_m)

    def put_row(k, value):
        part_x[:, pair(k)] = value

    chain_end(0)
    grad_of_x(b_rows, c_rows, lambda k: carry[0, k], False, row_refs, tails, put_row)
    loads[5].wait()
    row_b, row_c = grads_of_maps(
        x_ref, b_rows, c_rows, saved_row, False, row_refs, tails, scaled)

    wait_all(home_x, recv_sem.at[2])

    def put_sum(q, k, value):
        rows = slice(16 * q, 16 * q + 16)
        out_x[rows, pair(k)] = (part_x[rows, pair(k)] + value).astype(BF)

    unpack_channels(lambda q: home_x[8 * q : 8 * q + 8], put_sum)

    stores = [
        pltpu.make_async_copy(source, target, store_sem.at[i])
        for i, (source, target) in enumerate(
            [(out_x, out_x_hbm), (out_b, out_b_hbm), (out_c, out_c_hbm)])
    ]
    stores[0].start()

    wait_all(home_m, recv_sem.at[3])
    gather_back = maps_matrix(2, 2, True)
    for q in range(4):
        rows = slice(32 * q, 32 * q + 32)
        tiles = home_m[16 * q : 16 * q + 16].astype(F32).reshape(64, LANES).astype(BF)
        both = nn(gather_back, tiles)
        out_b[rows, :] = (row_b[rows] + both[0:32]).astype(BF)
        out_c[rows, :] = (row_c[rows] + both[32:64]).astype(BF)

    stores[1].start()
    stores[2].start()
    chain_sent(0)
    chain_sent(1)
    wait_all(send_m, send_sem.at[4])
    wait_all(send_g, send_sem.at[0])
    wait_all(send_x, send_sem.at[1])
    wait_all(back_x, send_sem.at[2])
    wait_all(back_m, send_sem.at[3])
    for store in stores:
        store.wait()


def hand_over(x_in, b_in, c_in, x_out, b_out, c_out, x_held, b_held, c_held, load_sem, store_sem):
    parts = [(x_in, x_held, x_out), (b_in, b_held, b_out), (c_in, c_held, c_out)]
    loads = [pltpu.make_async_copy(p[0], p[1], load_sem.at[i]) for i, p in enumerate(parts)]
    stores = [pltpu.make_async_copy(p[1], p[2], store_sem.at[i]) for i, p in enumerate(parts)]
    for load in loads:
        load.start()
    for load, store in zip(loads, stores):
        load.wait()
        store.start()
    for store in stores:
        store.wait()


def shards(inputs, grad_out, b_proj, c_proj, log_decay, saved_raster, saved_column):
    anywhere = pl.BlockSpec(memory_space=pl.ANY)
    out_x, out_b, out_c = pl.pallas_call(
        kernel,
        out_shape=(
            jax.ShapeDtypeStruct((TOKENS, CHANNELS), BF),
            jax.ShapeDtypeStruct((TOKENS, STATE), BF),
            jax.ShapeDtypeStruct((TOKENS, STATE), BF),
        ),
        in_specs=[pl.BlockSpec(memory_space=pltpu.HBM)] * 7,
        out_specs=(anywhere, anywhere, anywhere),
        scratch_shapes=[
            pltpu.VMEM((TOKENS, CHANNELS), BF),
            pltpu.VMEM((TOKENS, STATE), BF),
            pltpu.VMEM((TOKENS, STATE), BF),
            pltpu.VMEM((TOKENS, CHANNELS), BF),
            pltpu.VMEM((TOKENS, CHANNELS), BF),
            pltpu.VMEM((TOKENS, STATE), BF),
            pltpu.VMEM((TOKENS, STATE), BF),
            pltpu.VMEM((HEADS, TOKENS), BF),
            pltpu.VMEM((CHANNELS, STATE), F32),
            pltpu.VMEM((CHANNELS, STATE), F32),
            pltpu.VMEM((TILES, 8, LANES), BF),
            pltpu.VMEM((TILES, 2, 8, LANES), BF),
            pltpu.VMEM((TILES, 2, 8, LANES), BF),
            pltpu.VMEM((TILES, 8, LANES), BF),
            pltpu.VMEM((TILES, 2, 8, LANES), BF),
            pltpu.VMEM((TILES, 2, 8, LANES), BF),
            pltpu.VMEM((TILES, 2, 8, LANES), BF),
            pltpu.VMEM((TILES, 4, LANES), BF),
            pltpu.VMEM((TILES, 2, 8, LANES), BF),
            pltpu.VMEM((TILES, 4, LANES), BF),
            pltpu.VMEM((TOKENS, CHANNELS), F32),
            pltpu.VMEM((TOKENS, CHANNELS), F32),
            pltpu.VMEM((TOKENS, CHANNELS), BF),
            pltpu.VMEM((TOKENS, CHANNELS), BF),
            pltpu.VMEM((TOKENS, CHANNELS), F32),
            pltpu.VMEM((TOKENS, CHANNELS), BF),
            pltpu.VMEM((TOKENS, CHANNELS), BF),
            pltpu.VMEM((2, PAIRS, STATE, LANES), F32),
            pltpu.VMEM((2, PAIRS, STATE, LANES), BF),
            pltpu.VMEM((2, PAIRS, 2, LANES), F32),
            pltpu.VMEM((2, HALF, STATE, LANES), BF),
            pltpu.VMEM((2, PAIRS, 2, LANES), F32),
            pltpu.VMEM((2, HALF, STATE, LANES), BF),
            pltpu.VMEM((2, HALF, STATE, LANES), BF),
            pltpu.VMEM((2, HALF, STATE, LANES), BF),
            pltpu.VMEM((2, PAIRS, STATE, LANES), BF),
            pltpu.VMEM((STATE, CHANNELS), BF),
            pltpu.VMEM((TOKENS, CHANNELS), BF),
            pltpu.VMEM((TOKENS, CHANNELS), BF),
            pltpu.VMEM((3, TOKENS, LANES), BF),
            pltpu.VMEM((TOKENS, CHANNELS), F32),
            pltpu.SemaphoreType.DMA((7,)),
            pltpu.SemaphoreType.DMA((3,)),
            pltpu.SemaphoreType.DMA((5,)),
            pltpu.SemaphoreType.DMA((5,)),
            pltpu.SemaphoreType.DMA((2, 2)),
            pltpu.SemaphoreType.DMA((2, 2)),
            pltpu.SemaphoreType.DMA((2, HALF, PIECES_MAX)),
            pltpu.SemaphoreType.DMA((2, HALF, PIECES_MAX)),
            pltpu.SemaphoreType.DMA((2, HALF, PIECES_MAX)),
            pltpu.SemaphoreType.DMA((2, HALF, PIECES_MAX)),
        ],
        compiler_params=pltpu.CompilerParams(
            collective_id=0, has_side_effects=True, vmem_limit_bytes=63 * 1024 * 1024
        ),
        cost_estimate=pl.CostEstimate(
            flops=800_000_000, bytes_accessed=2_600_000, transcendentals=1_000_000
        ),
        name="scan_backward",
    )(
        inputs.reshape(TOKENS, CHANNELS),
        grad_out.reshape(TOKENS, CHANNELS),
        b_proj.reshape(TOKENS, STATE),
        c_proj.reshape(TOKENS, STATE),
        log_decay.reshape(HEADS, TOKENS),
        saved_raster.reshape(CHANNELS, STATE),
        saved_column.reshape(CHANNELS, STATE),
    )
    out_x, out_b, out_c = pl.pallas_call(
        hand_over,
        out_shape=(
            jax.ShapeDtypeStruct((TOKENS, CHANNELS), BF),
            jax.ShapeDtypeStruct((TOKENS, STATE), BF),
            jax.ShapeDtypeStruct((TOKENS, STATE), BF),
        ),
        in_specs=[anywhere] * 3,
        out_specs=(anywhere, anywhere, anywhere),
        scratch_shapes=[
            pltpu.VMEM((TOKENS, CHANNELS), BF),
            pltpu.VMEM((TOKENS, STATE), BF),
            pltpu.VMEM((TOKENS, STATE), BF),
            pltpu.SemaphoreType.DMA((3,)),
            pltpu.SemaphoreType.DMA((3,)),
        ],
        compiler_params=pltpu.CompilerParams(vmem_limit_bytes=63 * 1024 * 1024),
        cost_estimate=pl.CostEstimate(flops=0, bytes_accessed=640_000, transcendentals=0),
        name="hand_over",
    )(out_x, out_b, out_c)
    return (
        out_x.reshape(1, 1, TOKENS, CHANNELS),
        out_b.reshape(1, 1, TOKENS, STATE),
        out_c.reshape(1, 1, TOKENS, STATE),
    )


def solution(mesh):
    in_specs = (
        P("frames", "tiles", None, None),
        P("frames", "tiles", None, None),
        P("frames", "tiles", None, None),
        P("frames", "tiles", None, None),
        P(None, "frames", "tiles", None),
        P("frames", "tiles", None, None, None),
        P("frames", "tiles", None, None, None),
    )
    out_specs = (
        P("frames", "tiles", None, None),
        P("frames", "tiles", None, None),
        P("frames", "tiles", None, None),
    )
    return jax.shard_map(shards, mesh=mesh, in_specs=in_specs, out_specs=out_specs, check_vma=False)
```

```python
import jax
import jax.numpy as jnp
from jax import lax
from jax.experimental import pallas as pl
from jax.experimental.pallas import tpu as pltpu
from jax.sharding import PartitionSpec as P

HEADS = 16
HEAD_DIM = 64
STATE = 128
TOKENS = 128
CHANNELS = 1024
LANES = 128
PAIRS = CHANNELS // LANES
TILES = 64
DEPTH_Z = 16
DEPTH_X = 4
FRAMES = 8
HALF = PAIRS // 2
BEHIND = 8
EARLY = 20
PER_HOP = 7
LEFT = 6
PIECES = (1, 2)
PIECES_MAX = 2
BF = jnp.bfloat16
F32 = jnp.float32
MESH = pl.DeviceIdType.MESH


def nn(a, b):
    return lax.dot_general(a, b, (((1,), (0,)), ((), ())), preferred_element_type=F32)


def nt(a, b):
    return lax.dot_general(a, b, (((1,), (1,)), ((), ())), preferred_element_type=F32)


def iota(shape, dim):
    return lax.broadcasted_iota(jnp.int32, shape, dim)


def ones_where(cond):
    return jnp.where(cond, 1.0, 0.0).astype(BF)


def square(shape=(TOKENS, TOKENS)):
    return iota(shape, 0), iota(shape, 1)


def place(index, column_order):
    if not column_order:
        return index
    return lax.shift_left(index & 1, 6) + lax.shift_right_logical(index, 1)


def causal(column_order):
    t, s = square()
    return place(s, column_order) <= place(t, column_order)


def causal_transposed(column_order):
    s, t = square()
    return place(s, column_order) <= place(t, column_order)


def high(index, bits):
    return lax.shift_right_logical(index, bits)


def interleave(back=False):
    r, c = square()
    if back:
        r, c = c, r
    return ones_where((high(r, 3) == (c & 15)) & ((r & 7) == high(c, 4)))


def identity():
    r, c = square()
    return ones_where(r == c)


def maps_matrix(bits, parts, back=False):
    shape = (16 << bits, 32 * parts)
    if back:
        c, r = square(shape[::-1])
    else:
        r, c = square(shape)
    part, token = high(c, 5), c & 31
    return ones_where(r == lax.shift_left(high(token, 1), bits) + part * 2 + (token & 1))


def pair(k):
    return slice(LANES * k, LANES * k + LANES)


def pack_channels(read, write):
    mix = interleave()
    for q in range(8):
        stack = jnp.concatenate([read(q, k) for k in range(PAIRS)], axis=0)
        write(q, nn(mix, stack).reshape(8, 2, 8, LANES).astype(BF))


def unpack_channels(read, write):
    mix = interleave(True)
    for q in range(8):
        tiles = read(q).astype(F32).reshape(TOKENS, LANES).astype(BF)
        out = nn(mix, tiles)
        for k in range(PAIRS):
            write(q, k, out[16 * k : 16 * k + 16, :])


def block_scales(decays, column_order, shrink, grow, ends):
    run = ones_where(causal(column_order))
    head, channel = square((TOKENS, LANES))
    for k in range(PAIRS):
        spread = ones_where(high(channel, 6) + 2 * k == head)
        cum = nn(run, nn(decays, spread).astype(BF))
        total = cum[TOKENS - 1 : TOKENS, :]
        middle = total * 0.5
        shrink[:, pair(k)] = jnp.exp(cum - middle)
        grow[:, pair(k)] = jnp.exp(middle - cum)
        ends[k, 0:1, :] = jnp.exp(middle)
        ends[k, 1:2, :] = jnp.exp(total)


def scale_grad(value, rows, k, shrink, refs):
    grow, ends, centred, headed = refs
    shrunk = value.astype(F32) * shrink[rows, pair(k)]
    centred[rows, pair(k)] = shrunk.astype(BF)
    headed[rows, pair(k)] = (shrunk * ends[k, 0:1, :]).astype(BF)


def block_states(c_rows, refs, term, low):
    grow, ends, centred, headed = refs
    c_turned = nt(identity(), c_rows).astype(BF)
    for k in range(PAIRS):
        state = nn(c_turned, headed[:, pair(k)])
        term[k] = state
        low[k] = state.astype(BF)


def grad_of_x(b_rows, c_rows, carry, column_order, refs, tails, write):
    grow, ends, centred, headed = refs
    pairing = jnp.where(causal_transposed(column_order), nt(b_rows, c_rows), 0.0).astype(BF)
    both = jnp.concatenate([pairing, b_rows], axis=1)
    for k in range(PAIRS):
        tail = (carry(k).astype(F32) * ends[k, 0:1, :]).astype(BF)
        tails[:, pair(k)] = tail
        stack = jnp.concatenate([centred[:, pair(k)], tail], axis=0)
        write(k, nn(both, stack) * grow[:, pair(k)])


def grads_of_maps(x, b_rows, c_rows, saved, column_order, refs, tails, scaled):
    grow, ends, centred, headed = refs
    for k in range(PAIRS):
        scaled[:, pair(k)] = (x[:, pair(k)].astype(F32) * grow[:, pair(k)]).astype(BF)
    mixed = jnp.where(causal(column_order), nt(centred[...], scaled[...]), 0.0)
    part_b = nn(mixed.T.astype(BF), c_rows) + nt(scaled[...], tails[...])
    part_c = nn(mixed.astype(BF), b_rows) + nn(headed[...], saved[...].astype(BF))
    return part_b, part_c


def kernel(
    x_hbm, g_hbm, b_hbm, c_hbm, d_hbm, saved_row_hbm, saved_col_hbm,
    out_x_hbm, out_b_hbm, out_c_hbm,
    out_x, out_b, out_c,
    x_ref, g_ref, b_ref, c_ref, d_ref, saved_row, saved_col,
    send_m, send_g, send_x, got_m, got_g, got_x, back_x, back_m, home_x, home_m,
    shrink, row_grow, row_centred, row_headed, col_grow, col_centred, col_headed,
    term, low, ends, peer_low, peer_ends, incoming, outgoing, give, carry,
    tails, scaled, wide, col_maps, part_x,
    load_sem, store_sem, send_sem, recv_sem, swap_send, swap_recv, hop_send, hop_recv, give_send, give_recv,
):
    f = lax.axis_index("frames")
    me = lax.axis_index("tiles")
    z, x = lax.div(me, DEPTH_X), lax.rem(me, DEPTH_X)

    loads = [
        pltpu.make_async_copy(source, target, load_sem.at[i])
        for i, (source, target) in enumerate([
            (g_hbm, g_ref), (b_hbm, b_ref), (c_hbm, c_ref), (d_hbm, d_ref), (x_hbm, x_ref),
            (saved_row_hbm, saved_row), (saved_col_hbm, saved_col),
        ])
    ]
    for load in loads:
        load.start()

    def partner(k):
        step = TILES + 3 - k
        far, r = lax.div(step, 8), lax.rem(step, 8)
        most, none = lax.div(far, 8), lax.div(8 - far, 8)
        dx = (1 - most - none) * lax.div(r, 2) + most * r + none * (r - DEPTH_X)
        dz = far * (1 - 2 * lax.rem(r, 2))
        return lax.rem(z + dz + DEPTH_Z, DEPTH_Z) * DEPTH_X + lax.rem(x + dx, DEPTH_X)

    barrier = pltpu.get_barrier_semaphore()

    @pl.loop(0, TILES - 1)
    def _(k):
        pl.semaphore_signal(barrier, inc=1, device_id=(f, partner(k)), device_id_type=MESH)

    core, chip_y = lax.rem(f, 2), lax.div(f, 2)
    other = f + 1 - 2 * core
    above, below = lax.rem(f + 2, FRAMES), lax.rem(f + FRAMES - 2, FRAMES)
    mine, theirs = core * HALF, HALF - core * HALF
    for neighbour in (other, above, below):
        pl.semaphore_signal(barrier, inc=1, device_id=(neighbour, me), device_id_type=MESH)

    def keep_own(source, target):
        target[pl.ds(me, 1)] = source[pl.ds(me, 1)]

    def exchange(source, target, which, first=0, last=TILES - 1):
        @pl.loop(first, last)
        def _(k):
            peer = partner(k)
            pltpu.make_async_remote_copy(
                src_ref=source.at[peer],
                dst_ref=target.at[me],
                send_sem=send_sem.at[which],
                recv_sem=recv_sem.at[which],
                device_id=(f, peer),
                device_id_type=MESH,
            ).start()

    def wait_all(ref, sem):
        some = ref.at[pl.ds(0, TILES - 1)]
        pltpu.make_async_copy(some, some, sem).wait()

    def put_g(q, value):
        send_g[8 * q : 8 * q + 8] = value

    def put_x(q, value):
        send_x[8 * q : 8 * q + 8] = value

    def reader(ref):
        return lambda q, k: ref[16 * q : 16 * q + 16, pair(k)]

    for i in (1, 2, 3):
        loads[i].wait()
    decays = nt(identity(), jnp.concatenate(
        [d_ref[...], jnp.zeros((TOKENS - HEADS, TOKENS), BF)], axis=0)).astype(BF)
    b_rows, c_rows = b_ref[...], c_ref[...]
    spread_maps = maps_matrix(3, 3)
    for q in range(4):
        rows = slice(32 * q, 32 * q + 32)
        stack = jnp.concatenate([b_rows[rows], c_rows[rows], decays[rows]], axis=0)
        packed = nn(spread_maps, stack).reshape(16, 8, LANES).astype(BF)
        send_m[16 * q : 16 * q + 16] = packed
    pl.semaphore_wait(barrier, TILES + 2)
    exchange(send_m, got_m, 4)
    loads[0].wait()
    pack_channels(reader(g_ref), put_g)
    exchange(send_g, got_g, 0)
    keep_own(send_m, got_m)
    keep_own(send_g, got_g)

    @pl.when(chip_y == FRAMES // 2 - 1)
    def _():
        incoming[...] = jnp.zeros_like(incoming)

    def swap_copies(order):
        return [
            pltpu.make_async_remote_copy(
                src_ref=source,
                dst_ref=target,
                send_sem=swap_send.at[order, i],
                recv_sem=swap_recv.at[order, i],
                device_id=(other, me),
                device_id_type=MESH,
            )
            for i, (source, target) in enumerate([
                (ends.at[order], peer_ends.at[order]),
                (low.at[order, pl.ds(theirs, HALF)], peer_low.at[order]),
            ])
        ]

    def rows_of(order, p):
        rows = STATE // PIECES[order]
        return pl.ds(rows * p, rows)

    def hop_copy(order, i, p):
        return pltpu.make_async_remote_copy(
            src_ref=outgoing.at[order, i, rows_of(order, p)],
            dst_ref=incoming.at[order, i, rows_of(order, p)],
            send_sem=hop_send.at[order, i, p],
            recv_sem=hop_recv.at[order, i, p],
            device_id=(below, me),
            device_id_type=MESH,
        )

    def give_copy(order, i, p):
        return pltpu.make_async_remote_copy(
            src_ref=give.at[order, i, rows_of(order, p)],
            dst_ref=carry.at[order, mine + i, rows_of(order, p)],
            send_sem=give_send.at[order, i, p],
            recv_sem=give_recv.at[order, i, p],
            device_id=(other, me),
            device_id_type=MESH,
        )

    def swapped(order):
        for copy in swap_copies(order):
            copy.wait_recv()

    def steps(order):
        return [(i, p) for i in range(HALF) for p in range(PIECES[order])]

    def chain(order):
        lower = core == 0
        for i, p in steps(order):
            k, rows = mine + i, rows_of(order, p)

            @pl.when(chip_y < FRAMES // 2 - 1)
            def _():
                hop_copy(order, i, p).wait_recv()

            own_state, peer_state = term[order, k, rows], peer_low[order, i, rows].astype(F32)
            own_decay, peer_decay = ends[order, k, 1:2, :], peer_ends[order, k, 1:2, :]
            lower_state = jnp.where(lower, own_state, peer_state)
            upper_state = jnp.where(lower, peer_state, own_state)
            lower_decay = jnp.where(lower, own_decay, peer_decay)
            upper_decay = jnp.where(lower, peer_decay, own_decay)
            entering = incoming[order, i, rows].astype(F32)
            between = upper_decay * entering + upper_state

            @pl.when(chip_y > 0)
            def _():
                outgoing[order, i, rows] = (lower_decay * between + lower_state).astype(BF)
                hop_copy(order, i, p).start()

            carry[order, k, rows] = jnp.where(lower, between, entering).astype(BF)
            give[order, i, rows] = jnp.where(lower, entering, between).astype(BF)
            give_copy(order, i, p).start()

    def chain_end(order):
        for i, p in steps(order):
            some = carry.at[order, theirs + i, rows_of(order, p)]
            pltpu.make_async_copy(some, some, give_recv.at[order, i, p]).wait()

    def chain_sent(order):
        for copy in swap_copies(order):
            copy.wait_send()
        for i, p in steps(order):
            give_copy(order, i, p).wait_send()

            @pl.when(chip_y > 0)
            def _():
                hop_copy(order, i, p).wait_send()

    row_refs = (row_grow, ends.at[0], row_centred, row_headed)
    block_scales(decays, False, shrink, row_grow, ends.at[0])
    for k in range(PAIRS):
        scale_grad(g_ref[:, pair(k)], slice(0, TOKENS), k, shrink, row_refs)
    block_states(c_rows, row_refs, term.at[0], low.at[0])
    for copy in swap_copies(0):
        copy.start()
    loads[4].wait()
    pack_channels(reader(x_ref), put_x)
    exchange(send_x, got_x, 1, 0, BEHIND)
    keep_own(send_x, got_x)

    wait_all(got_m, recv_sem.at[4])
    gather_maps = maps_matrix(3, 3, True)
    for q in range(4):
        tiles = got_m[16 * q : 16 * q + 16].astype(F32).reshape(TOKENS, LANES).astype(BF)
        piece = nn(gather_maps, tiles).astype(BF)
        for p in range(3):
            col_maps[p, 32 * q : 32 * q + 32] = piece[32 * p : 32 * p + 32]
    col_refs = (col_grow, ends.at[1], col_centred, col_headed)
    block_scales(col_maps[2], True, shrink, col_grow, ends.at[1])
    swapped(0)

    wait_all(got_g, recv_sem.at[0])
    exchange(send_x, got_x, 1, BEHIND, EARLY)

    def put_wide(q, k, value):
        wide[16 * q : 16 * q + 16, pair(k)] = value.astype(BF)

    def put_scaled(q, k, value):
        scale_grad(value, slice(16 * q, 16 * q + 16), k, shrink, col_refs)

    unpack_channels(lambda q: got_g[8 * q : 8 * q + 8], put_scaled)
    block_states(col_maps[1], col_refs, term.at[1], low.at[1])
    for copy in swap_copies(1):
        copy.start()
    filled = EARLY + 3 + PER_HOP * (FRAMES // 2 - 1 - chip_y)
    packed_by = TILES - 1 - LEFT * chip_y
    exchange(send_x, got_x, 1, EARLY, filled)
    swapped(1)
    chain(1)
    exchange(send_x, got_x, 1, filled, packed_by)
    chain_end(1)

    def put_col(k, value):
        wide[:, pair(k)] = value.astype(BF)

    grad_of_x(col_maps[0], col_maps[1], lambda k: carry[1, k], True, col_refs, tails, put_col)

    def put_back(q, value):
        back_x[8 * q : 8 * q + 8] = value

    pack_channels(reader(wide), put_back)
    chain(0)
    exchange(send_x, got_x, 1, packed_by)
    exchange(back_x, home_x, 2)
    keep_own(back_x, home_x)

    wait_all(got_x, recv_sem.at[1])
    loads[6].wait()
    unpack_channels(lambda q: got_x[8 * q : 8 * q + 8], put_wide)
    col_b, col_c = grads_of_maps(
        wide, col_maps[0], col_maps[1], saved_col, True, col_refs, tails, scaled)
    col_b, col_c = col_b.astype(BF), col_c.astype(BF)
    spread_back = maps_matrix(2, 2)
    for q in range(4):
        rows = slice(32 * q, 32 * q + 32)
        stack = jnp.concatenate([col_b[rows], col_c[rows]], axis=0)
        packed = nn(spread_back, stack).reshape(16, 4, LANES).astype(BF)
        back_m[16 * q : 16 * q + 16] = packed
    exchange(back_m, home_m, 3)
    keep_own(back_m, home_m)

    def put_row(k, value):
        part_x[:, pair(k)] = value

    chain_end(0)
    grad_of_x(b_rows, c_rows, lambda k: carry[0, k], False, row_refs, tails, put_row)
    loads[5].wait()
    row_b, row_c = grads_of_maps(
        x_ref, b_rows, c_rows, saved_row, False, row_refs, tails, scaled)

    wait_all(home_x, recv_sem.at[2])

    def put_sum(q, k, value):
        rows = slice(16 * q, 16 * q + 16)
        out_x[rows, pair(k)] = (part_x[rows, pair(k)] + value).astype(BF)

    unpack_channels(lambda q: home_x[8 * q : 8 * q + 8], put_sum)

    stores = [
        pltpu.make_async_copy(source, target, store_sem.at[i])
        for i, (source, target) in enumerate(
            [(out_x, out_x_hbm), (out_b, out_b_hbm), (out_c, out_c_hbm)])
    ]
    stores[0].start()

    wait_all(home_m, recv_sem.at[3])
    gather_back = maps_matrix(2, 2, True)
    for q in range(4):
        rows = slice(32 * q, 32 * q + 32)
        tiles = home_m[16 * q : 16 * q + 16].astype(F32).reshape(64, LANES).astype(BF)
        both = nn(gather_back, tiles)
        out_b[rows, :] = (row_b[rows] + both[0:32]).astype(BF)
        out_c[rows, :] = (row_c[rows] + both[32:64]).astype(BF)

    stores[1].start()
    stores[2].start()
    chain_sent(0)
    chain_sent(1)
    wait_all(send_m, send_sem.at[4])
    wait_all(send_g, send_sem.at[0])
    wait_all(send_x, send_sem.at[1])
    wait_all(back_x, send_sem.at[2])
    wait_all(back_m, send_sem.at[3])
    for store in stores:
        store.wait()


def hand_over(x_in, b_in, c_in, x_out, b_out, c_out, x_held, b_held, c_held, load_sem, store_sem):
    parts = [(x_in, x_held, x_out), (b_in, b_held, b_out), (c_in, c_held, c_out)]
    loads = [pltpu.make_async_copy(p[0], p[1], load_sem.at[i]) for i, p in enumerate(parts)]
    stores = [pltpu.make_async_copy(p[1], p[2], store_sem.at[i]) for i, p in enumerate(parts)]
    for load in loads:
        load.start()
    for load, store in zip(loads, stores):
        load.wait()
        store.start()
    for store in stores:
        store.wait()


def shards(inputs, grad_out, b_proj, c_proj, log_decay, saved_raster, saved_column):
    anywhere = pl.BlockSpec(memory_space=pl.ANY)
    out_x, out_b, out_c = pl.pallas_call(
        kernel,
        out_shape=(
            jax.ShapeDtypeStruct((TOKENS, CHANNELS), BF),
            jax.ShapeDtypeStruct((TOKENS, STATE), BF),
            jax.ShapeDtypeStruct((TOKENS, STATE), BF),
        ),
        in_specs=[pl.BlockSpec(memory_space=pltpu.HBM)] * 7,
        out_specs=(anywhere, anywhere, anywhere),
        scratch_shapes=[
            pltpu.VMEM((TOKENS, CHANNELS), BF),
            pltpu.VMEM((TOKENS, STATE), BF),
            pltpu.VMEM((TOKENS, STATE), BF),
            pltpu.VMEM((TOKENS, CHANNELS), BF),
            pltpu.VMEM((TOKENS, CHANNELS), BF),
            pltpu.VMEM((TOKENS, STATE), BF),
            pltpu.VMEM((TOKENS, STATE), BF),
            pltpu.VMEM((HEADS, TOKENS), BF),
            pltpu.VMEM((CHANNELS, STATE), F32),
            pltpu.VMEM((CHANNELS, STATE), F32),
            pltpu.VMEM((TILES, 8, LANES), BF),
            pltpu.VMEM((TILES, 2, 8, LANES), BF),
            pltpu.VMEM((TILES, 2, 8, LANES), BF),
            pltpu.VMEM((TILES, 8, LANES), BF),
            pltpu.VMEM((TILES, 2, 8, LANES), BF),
            pltpu.VMEM((TILES, 2, 8, LANES), BF),
            pltpu.VMEM((TILES, 2, 8, LANES), BF),
            pltpu.VMEM((TILES, 4, LANES), BF),
            pltpu.VMEM((TILES, 2, 8, LANES), BF),
            pltpu.VMEM((TILES, 4, LANES), BF),
            pltpu.VMEM((TOKENS, CHANNELS), F32),
            pltpu.VMEM((TOKENS, CHANNELS), F32),
            pltpu.VMEM((TOKENS, CHANNELS), BF),
            pltpu.VMEM((TOKENS, CHANNELS), BF),
            pltpu.VMEM((TOKENS, CHANNELS), F32),
            pltpu.VMEM((TOKENS, CHANNELS), BF),
            pltpu.VMEM((TOKENS, CHANNELS), BF),
            pltpu.VMEM((2, PAIRS, STATE, LANES), F32),
            pltpu.VMEM((2, PAIRS, STATE, LANES), BF),
            pltpu.VMEM((2, PAIRS, 2, LANES), F32),
            pltpu.VMEM((2, HALF, STATE, LANES), BF),
            pltpu.VMEM((2, PAIRS, 2, LANES), F32),
            pltpu.VMEM((2, HALF, STATE, LANES), BF),
            pltpu.VMEM((2, HALF, STATE, LANES), BF),
            pltpu.VMEM((2, HALF, STATE, LANES), BF),
            pltpu.VMEM((2, PAIRS, STATE, LANES), BF),
            pltpu.VMEM((STATE, CHANNELS), BF),
            pltpu.VMEM((TOKENS, CHANNELS), BF),
            pltpu.VMEM((TOKENS, CHANNELS), BF),
            pltpu.VMEM((3, TOKENS, LANES), BF),
            pltpu.VMEM((TOKENS, CHANNELS), F32),
            pltpu.SemaphoreType.DMA((7,)),
            pltpu.SemaphoreType.DMA((3,)),
            pltpu.SemaphoreType.DMA((5,)),
            pltpu.SemaphoreType.DMA((5,)),
            pltpu.SemaphoreType.DMA((2, 2)),
            pltpu.SemaphoreType.DMA((2, 2)),
            pltpu.SemaphoreType.DMA((2, HALF, PIECES_MAX)),
            pltpu.SemaphoreType.DMA((2, HALF, PIECES_MAX)),
            pltpu.SemaphoreType.DMA((2, HALF, PIECES_MAX)),
            pltpu.SemaphoreType.DMA((2, HALF, PIECES_MAX)),
        ],
        compiler_params=pltpu.CompilerParams(
            collective_id=0, has_side_effects=True, vmem_limit_bytes=63 * 1024 * 1024
        ),
        cost_estimate=pl.CostEstimate(
            flops=800_000_000, bytes_accessed=2_600_000, transcendentals=1_000_000
        ),
        name="scan_backward",
    )(
        inputs.reshape(TOKENS, CHANNELS),
        grad_out.reshape(TOKENS, CHANNELS),
        b_proj.reshape(TOKENS, STATE),
        c_proj.reshape(TOKENS, STATE),
        log_decay.reshape(HEADS, TOKENS),
        saved_raster.reshape(CHANNELS, STATE),
        saved_column.reshape(CHANNELS, STATE),
    )
    out_x, out_b, out_c = pl.pallas_call(
        hand_over,
        out_shape=(
            jax.ShapeDtypeStruct((TOKENS, CHANNELS), BF),
            jax.ShapeDtypeStruct((TOKENS, STATE), BF),
            jax.ShapeDtypeStruct((TOKENS, STATE), BF),
        ),
        in_specs=[anywhere] * 3,
        out_specs=(anywhere, anywhere, anywhere),
        scratch_shapes=[
            pltpu.VMEM((TOKENS, CHANNELS), BF),
            pltpu.VMEM((TOKENS, STATE), BF),
            pltpu.VMEM((TOKENS, STATE), BF),
            pltpu.SemaphoreType.DMA((3,)),
            pltpu.SemaphoreType.DMA((3,)),
        ],
        compiler_params=pltpu.CompilerParams(vmem_limit_bytes=63 * 1024 * 1024),
        cost_estimate=pl.CostEstimate(flops=0, bytes_accessed=640_000, transcendentals=0),
        name="hand_over",
    )(out_x, out_b, out_c)
    return (
        out_x.reshape(1, 1, TOKENS, CHANNELS),
        out_b.reshape(1, 1, TOKENS, STATE),
        out_c.reshape(1, 1, TOKENS, STATE),
    )


def solution(mesh):
    in_specs = (
        P("frames", "tiles", None, None),
        P("frames", "tiles", None, None),
        P("frames", "tiles", None, None),
        P("frames", "tiles", None, None),
        P(None, "frames", "tiles", None),
        P("frames", "tiles", None, None, None),
        P("frames", "tiles", None, None, None),
    )
    out_specs = (
        P("frames", "tiles", None, None),
        P("frames", "tiles", None, None),
        P("frames", "tiles", None, None),
    )
    return jax.shard_map(shards, mesh=mesh, in_specs=in_specs, out_specs=out_specs, check_vma=False)
```

```python
import jax
import jax.numpy as jnp
from jax import lax
from jax.experimental import pallas as pl
from jax.experimental.pallas import tpu as pltpu
from jax.sharding import PartitionSpec as P

HEADS = 16
HEAD_DIM = 64
STATE = 128
TOKENS = 128
CHANNELS = 1024
LANES = 128
PAIRS = CHANNELS // LANES
TILES = 64
DEPTH_Z = 16
DEPTH_X = 4
FRAMES = 8
HALF = PAIRS // 2
BEHIND = 20
EARLY = 20
PER_HOP = 7
LEFT = 6
PIECES = (1, 2)
PIECES_MAX = 2
BF = jnp.bfloat16
F32 = jnp.float32
MESH = pl.DeviceIdType.MESH


def nn(a, b):
    return lax.dot_general(a, b, (((1,), (0,)), ((), ())), preferred_element_type=F32)


def nt(a, b):
    return lax.dot_general(a, b, (((1,), (1,)), ((), ())), preferred_element_type=F32)


def iota(shape, dim):
    return lax.broadcasted_iota(jnp.int32, shape, dim)


def ones_where(cond):
    return jnp.where(cond, 1.0, 0.0).astype(BF)


def square(shape=(TOKENS, TOKENS)):
    return iota(shape, 0), iota(shape, 1)


def place(index, column_order):
    if not column_order:
        return index
    return lax.shift_left(index & 1, 6) + lax.shift_right_logical(index, 1)


def causal(column_order):
    t, s = square()
    return place(s, column_order) <= place(t, column_order)


def causal_transposed(column_order):
    s, t = square()
    return place(s, column_order) <= place(t, column_order)


def high(index, bits):
    return lax.shift_right_logical(index, bits)


def interleave(back=False):
    r, c = square()
    if back:
        r, c = c, r
    return ones_where((high(r, 3) == (c & 15)) & ((r & 7) == high(c, 4)))


def identity():
    r, c = square()
    return ones_where(r == c)


def maps_matrix(parts, back=False):
    shape = (32 * parts, 32 * parts)
    if back:
        c, r = square(shape[::-1])
    else:
        r, c = square(shape)
    part, token = high(c, 5), c & 31
    return ones_where(r == high(token, 1) * (2 * parts) + part * 2 + (token & 1))


def pair(k):
    return slice(LANES * k, LANES * k + LANES)


def pack_channels(read, write):
    mix = interleave()
    for q in range(8):
        stack = jnp.concatenate([read(q, k) for k in range(PAIRS)], axis=0)
        write(q, nn(mix, stack).reshape(8, 2, 8, LANES).astype(BF))


def unpack_channels(read, write):
    mix = interleave(True)
    for q in range(8):
        tiles = read(q).astype(F32).reshape(TOKENS, LANES).astype(BF)
        out = nn(mix, tiles)
        for k in range(PAIRS):
            write(q, k, out[16 * k : 16 * k + 16, :])


def block_scales(decays, column_order, shrink, grow, ends):
    run = ones_where(causal(column_order))
    head, channel = square((TOKENS, LANES))
    for k in range(PAIRS):
        spread = ones_where(high(channel, 6) + 2 * k == head)
        cum = nn(run, nn(decays, spread).astype(BF))
        total = cum[TOKENS - 1 : TOKENS, :]
        middle = total * 0.5
        shrink[:, pair(k)] = jnp.exp(cum - middle)
        grow[:, pair(k)] = jnp.exp(middle - cum)
        ends[k, 0:1, :] = jnp.exp(middle)
        ends[k, 1:2, :] = jnp.exp(total)


def scale_grad(value, rows, k, shrink, refs):
    grow, ends, centred, headed = refs
    shrunk = value.astype(F32) * shrink[rows, pair(k)]
    centred[rows, pair(k)] = shrunk.astype(BF)
    headed[rows, pair(k)] = (shrunk * ends[k, 0:1, :]).astype(BF)


def block_states(c_rows, refs, term, low):
    grow, ends, centred, headed = refs
    c_turned = nt(identity(), c_rows).astype(BF)
    for k in range(PAIRS):
        state = nn(c_turned, headed[:, pair(k)])
        term[k] = state
        low[k] = state.astype(BF)


def grad_of_x(b_rows, c_rows, carry, column_order, refs, tails, write):
    grow, ends, centred, headed = refs
    pairing = jnp.where(causal_transposed(column_order), nt(b_rows, c_rows), 0.0).astype(BF)
    both = jnp.concatenate([pairing, b_rows], axis=1)
    for k in range(PAIRS):
        tail = (carry(k).astype(F32) * ends[k, 0:1, :]).astype(BF)
        tails[:, pair(k)] = tail
        stack = jnp.concatenate([centred[:, pair(k)], tail], axis=0)
        write(k, nn(both, stack) * grow[:, pair(k)])


def grads_of_maps(x, b_rows, c_rows, saved, column_order, refs, tails, scaled):
    grow, ends, centred, headed = refs
    for k in range(PAIRS):
        scaled[:, pair(k)] = (x[:, pair(k)].astype(F32) * grow[:, pair(k)]).astype(BF)
    mixed = jnp.where(causal(column_order), nt(centred[...], scaled[...]), 0.0)
    part_b = nn(mixed.T.astype(BF), c_rows) + nt(scaled[...], tails[...])
    part_c = nn(mixed.astype(BF), b_rows) + nn(headed[...], saved[...].astype(BF))
    return part_b, part_c


def kernel(
    x_hbm, g_hbm, b_hbm, c_hbm, d_hbm, saved_row_hbm, saved_col_hbm,
    out_x_hbm, out_b_hbm, out_c_hbm,
    out_x, out_b, out_c,
    x_ref, g_ref, b_ref, c_ref, d_ref, saved_row, saved_col,
    send_m, send_g, send_x, got_m, got_g, got_x, back_x, back_m, home_x, home_m,
    shrink, row_grow, row_centred, row_headed, col_grow, col_centred, col_headed,
    term, low, ends, peer_low, peer_ends, incoming, outgoing, give, carry,
    tails, scaled, wide, col_maps, part_x,
    load_sem, store_sem, send_sem, recv_sem, swap_send, swap_recv, hop_send, hop_recv, give_send, give_recv,
):
    f = lax.axis_index("frames")
    me = lax.axis_index("tiles")
    z, x = lax.div(me, DEPTH_X), lax.rem(me, DEPTH_X)

    loads = [
        pltpu.make_async_copy(source, target, load_sem.at[i])
        for i, (source, target) in enumerate([
            (g_hbm, g_ref), (b_hbm, b_ref), (c_hbm, c_ref), (d_hbm, d_ref), (x_hbm, x_ref),
            (saved_row_hbm, saved_row), (saved_col_hbm, saved_col),
        ])
    ]
    for load in loads[:4]:
        load.start()

    xs = [lax.rem(x + dx, DEPTH_X) for dx in range(DEPTH_X)]

    def each_partner(act):
        opposite = lax.rem(z + DEPTH_Z // 2, DEPTH_Z) * DEPTH_X
        for dx in range(DEPTH_X):
            act(opposite + xs[dx])

        @pl.loop(1, DEPTH_Z // 2)
        def _(k):
            far = DEPTH_Z // 2 - k
            ahead = lax.rem(z + far, DEPTH_Z) * DEPTH_X
            behind = lax.rem(z - far + DEPTH_Z, DEPTH_Z) * DEPTH_X
            for dx in range(DEPTH_X):
                act(ahead + xs[dx])
                act(behind + xs[dx])

        for dx in range(1, DEPTH_X):
            act(z * DEPTH_X + xs[dx])

    def partner(k):
        step = TILES + 3 - k
        far, r = lax.div(step, 8), lax.rem(step, 8)
        most, none = lax.div(far, 8), lax.div(8 - far, 8)
        dx = (1 - most - none) * lax.div(r, 2) + most * r + none * (r - DEPTH_X)
        dz = far * (1 - 2 * lax.rem(r, 2))
        return lax.rem(z + dz + DEPTH_Z, DEPTH_Z) * DEPTH_X + lax.rem(x + dx, DEPTH_X)

    barrier = pltpu.get_barrier_semaphore()

    def greet(peer):
        pl.semaphore_signal(barrier, inc=1, device_id=(f, peer), device_id_type=MESH)

    each_partner(greet)

    core, chip_y = lax.rem(f, 2), lax.div(f, 2)
    other = f + 1 - 2 * core
    above, below = lax.rem(f + 2, FRAMES), lax.rem(f + FRAMES - 2, FRAMES)
    mine, theirs = core * HALF, HALF - core * HALF
    for neighbour in (other, above, below):
        pl.semaphore_signal(barrier, inc=1, device_id=(neighbour, me), device_id_type=MESH)

    for load in loads[4:]:
        load.start()

    def keep_own(source, target):
        target[pl.ds(me, 1)] = source[pl.ds(me, 1)]

    def send(source, target, which, peer):
        pltpu.make_async_remote_copy(
            src_ref=source.at[peer],
            dst_ref=target.at[me],
            send_sem=send_sem.at[which],
            recv_sem=recv_sem.at[which],
            device_id=(f, peer),
            device_id_type=MESH,
        ).start()

    def exchange(source, target, which):
        each_partner(lambda peer: send(source, target, which, peer))

    def exchange_some(source, target, which, first, last=TILES - 1):
        @pl.loop(first, last)
        def _(k):
            send(source, target, which, partner(k))

    def wait_all(ref, sem):
        some = ref.at[pl.ds(0, TILES - 1)]
        pltpu.make_async_copy(some, some, sem).wait()

    def put_g(q, value):
        send_g[8 * q : 8 * q + 8] = value

    def put_x(q, value):
        send_x[8 * q : 8 * q + 8] = value

    def reader(ref):
        return lambda q, k: ref[16 * q : 16 * q + 16, pair(k)]

    for i in (1, 2, 3):
        loads[i].wait()
    decays = nt(identity(), jnp.concatenate(
        [d_ref[...], jnp.zeros((TOKENS - HEADS, TOKENS), BF)], axis=0)).astype(BF)
    b_rows, c_rows = b_ref[...], c_ref[...]
    spread_maps = maps_matrix(3)
    for q in range(4):
        rows = slice(32 * q, 32 * q + 32)
        stack = jnp.concatenate([b_rows[rows], c_rows[rows], decays[rows]], axis=0)
        packed = nn(spread_maps, stack).reshape(16, 3, 2, LANES).astype(BF)
        send_m[16 * q : 16 * q + 16] = packed
    pl.semaphore_wait(barrier, TILES + 2)
    exchange(send_m, got_m, 4)
    loads[0].wait()
    pack_channels(reader(g_ref), put_g)
    exchange(send_g, got_g, 0)
    keep_own(send_m, got_m)
    keep_own(send_g, got_g)

    @pl.when(chip_y == FRAMES // 2 - 1)
    def _():
        incoming[...] = jnp.zeros_like(incoming)

    def swap_copies(order):
        return [
            pltpu.make_async_remote_copy(
                src_ref=source,
                dst_ref=target,
                send_sem=swap_send.at[order, i],
                recv_sem=swap_recv.at[order, i],
                device_id=(other, me),
                device_id_type=MESH,
            )
            for i, (source, target) in enumerate([
                (ends.at[order], peer_ends.at[order]),
                (low.at[order, pl.ds(theirs, HALF)], peer_low.at[order]),
            ])
        ]

    def rows_of(order, p):
        rows = STATE // PIECES[order]
        return pl.ds(rows * p, rows)

    def hop_copy(order, i, p):
        return pltpu.make_async_remote_copy(
            src_ref=outgoing.at[order, i, rows_of(order, p)],
            dst_ref=incoming.at[order, i, rows_of(order, p)],
            send_sem=hop_send.at[order, i, p],
            recv_sem=hop_recv.at[order, i, p],
            device_id=(below, me),
            device_id_type=MESH,
        )

    def give_copy(order, i, p):
        return pltpu.make_async_remote_copy(
            src_ref=give.at[order, i, rows_of(order, p)],
            dst_ref=carry.at[order, mine + i, rows_of(order, p)],
            send_sem=give_send.at[order, i, p],
            recv_sem=give_recv.at[order, i, p],
            device_id=(other, me),
            device_id_type=MESH,
        )

    def swapped(order):
        for copy in swap_copies(order):
            copy.wait_recv()

    def steps(order):
        return [(i, p) for i in range(HALF) for p in range(PIECES[order])]

    def chain(order):
        lower = core == 0
        for i, p in steps(order):
            k, rows = mine + i, rows_of(order, p)

            @pl.when(chip_y < FRAMES // 2 - 1)
            def _():
                hop_copy(order, i, p).wait_recv()

            own_state, peer_state = term[order, k, rows], peer_low[order, i, rows].astype(F32)
            own_decay, peer_decay = ends[order, k, 1:2, :], peer_ends[order, k, 1:2, :]
            lower_state = jnp.where(lower, own_state, peer_state)
            upper_state = jnp.where(lower, peer_state, own_state)
            lower_decay = jnp.where(lower, own_decay, peer_decay)
            upper_decay = jnp.where(lower, peer_decay, own_decay)
            entering = incoming[order, i, rows].astype(F32)
            between = upper_decay * entering + upper_state

            @pl.when(chip_y > 0)
            def _():
                outgoing[order, i, rows] = (lower_decay * between + lower_state).astype(BF)
                hop_copy(order, i, p).start()

            carry[order, k, rows] = jnp.where(lower, between, entering).astype(BF)
            give[order, i, rows] = jnp.where(lower, entering, between).astype(BF)
            give_copy(order, i, p).start()

    def chain_end(order):
        for i, p in steps(order):
            some = carry.at[order, theirs + i, rows_of(order, p)]
            pltpu.make_async_copy(some, some, give_recv.at[order, i, p]).wait()

    def chain_sent(order):
        for copy in swap_copies(order):
            copy.wait_send()
        for i, p in steps(order):
            give_copy(order, i, p).wait_send()

            @pl.when(chip_y > 0)
            def _():
                hop_copy(order, i, p).wait_send()

    row_refs = (row_grow, ends.at[0], row_centred, row_headed)
    block_scales(decays, False, shrink, row_grow, ends.at[0])
    for k in range(PAIRS):
        scale_grad(g_ref[:, pair(k)], slice(0, TOKENS), k, shrink, row_refs)
    block_states(c_rows, row_refs, term.at[0], low.at[0])
    for copy in swap_copies(0):
        copy.start()
    loads[4].wait()
    pack_channels(reader(x_ref), put_x)
    exchange_some(send_x, got_x, 1, 0, BEHIND)
    keep_own(send_x, got_x)

    wait_all(got_m, recv_sem.at[4])
    gather_maps = maps_matrix(3, True)
    for q in range(4):
        tiles = got_m[16 * q : 16 * q + 16].astype(F32).reshape(96, LANES).astype(BF)
        piece = nn(gather_maps, tiles).astype(BF)
        for p in range(3):
            col_maps[p, 32 * q : 32 * q + 32] = piece[32 * p : 32 * p + 32]
    col_refs = (col_grow, ends.at[1], col_centred, col_headed)
    block_scales(col_maps[2], True, shrink, col_grow, ends.at[1])
    swapped(0)

    wait_all(got_g, recv_sem.at[0])

    def put_wide(q, k, value):
        wide[16 * q : 16 * q + 16, pair(k)] = value.astype(BF)

    def put_scaled(q, k, value):
        scale_grad(value, slice(16 * q, 16 * q + 16), k, shrink, col_refs)

    unpack_channels(lambda q: got_g[8 * q : 8 * q + 8], put_scaled)
    block_states(col_maps[1], col_refs, term.at[1], low.at[1])
    for copy in swap_copies(1):
        copy.start()
    filled = EARLY + 3 + PER_HOP * (FRAMES // 2 - 1 - chip_y)
    packed_by = TILES - 1 - LEFT * chip_y
    exchange_some(send_x, got_x, 1, EARLY, filled)
    swapped(1)
    chain(1)
    exchange_some(send_x, got_x, 1, filled, packed_by)
    chain_end(1)

    def put_col(k, value):
        wide[:, pair(k)] = value.astype(BF)

    grad_of_x(col_maps[0], col_maps[1], lambda k: carry[1, k], True, col_refs, tails, put_col)

    def put_back(q, value):
        back_x[8 * q : 8 * q + 8] = value

    pack_channels(reader(wide), put_back)
    chain(0)
    exchange_some(send_x, got_x, 1, packed_by)
    exchange(back_x, home_x, 2)
    keep_own(back_x, home_x)

    wait_all(got_x, recv_sem.at[1])
    loads[6].wait()
    unpack_channels(lambda q: got_x[8 * q : 8 * q + 8], put_wide)
    col_b, col_c = grads_of_maps(
        wide, col_maps[0], col_maps[1], saved_col, True, col_refs, tails, scaled)
    col_b, col_c = col_b.astype(BF), col_c.astype(BF)
    spread_back = maps_matrix(2)
    for q in range(4):
        rows = slice(32 * q, 32 * q + 32)
        stack = jnp.concatenate([col_b[rows], col_c[rows]], axis=0)
        packed = nn(spread_back, stack).reshape(16, 4, LANES).astype(BF)
        back_m[16 * q : 16 * q + 16] = packed
    exchange(back_m, home_m, 3)
    keep_own(back_m, home_m)

    def put_row(k, value):
        part_x[:, pair(k)] = value

    chain_end(0)
    grad_of_x(b_rows, c_rows, lambda k: carry[0, k], False, row_refs, tails, put_row)
    loads[5].wait()
    row_b, row_c = grads_of_maps(
        x_ref, b_rows, c_rows, saved_row, False, row_refs, tails, scaled)

    wait_all(home_x, recv_sem.at[2])

    def put_sum(q, k, value):
        rows = slice(16 * q, 16 * q + 16)
        out_x[rows, pair(k)] = (part_x[rows, pair(k)] + value).astype(BF)

    unpack_channels(lambda q: home_x[8 * q : 8 * q + 8], put_sum)

    stores = [
        pltpu.make_async_copy(source, target, store_sem.at[i])
        for i, (source, target) in enumerate(
            [(out_x, out_x_hbm), (out_b, out_b_hbm), (out_c, out_c_hbm)])
    ]
    stores[0].start()

    wait_all(home_m, recv_sem.at[3])
    gather_back = maps_matrix(2, True)
    for q in range(4):
        rows = slice(32 * q, 32 * q + 32)
        tiles = home_m[16 * q : 16 * q + 16].astype(F32).reshape(64, LANES).astype(BF)
        both = nn(gather_back, tiles)
        out_b[rows, :] = (row_b[rows] + both[0:32]).astype(BF)
        out_c[rows, :] = (row_c[rows] + both[32:64]).astype(BF)

    stores[1].start()
    stores[2].start()
    chain_sent(0)
    chain_sent(1)
    wait_all(send_m, send_sem.at[4])
    wait_all(send_g, send_sem.at[0])
    wait_all(send_x, send_sem.at[1])
    wait_all(back_x, send_sem.at[2])
    wait_all(back_m, send_sem.at[3])
    for store in stores:
        store.wait()


def hand_over(x_in, b_in, c_in, x_out, b_out, c_out, x_held, b_held, c_held, load_sem, store_sem):
    parts = [(x_in, x_held, x_out), (b_in, b_held, b_out), (c_in, c_held, c_out)]
    loads = [pltpu.make_async_copy(p[0], p[1], load_sem.at[i]) for i, p in enumerate(parts)]
    stores = [pltpu.make_async_copy(p[1], p[2], store_sem.at[i]) for i, p in enumerate(parts)]
    for load in loads:
        load.start()
    for load, store in zip(loads, stores):
        load.wait()
        store.start()
    for store in stores:
        store.wait()


def shards(inputs, grad_out, b_proj, c_proj, log_decay, saved_raster, saved_column):
    anywhere = pl.BlockSpec(memory_space=pl.ANY)
    out_x, out_b, out_c = pl.pallas_call(
        kernel,
        out_shape=(
            jax.ShapeDtypeStruct((TOKENS, CHANNELS), BF),
            jax.ShapeDtypeStruct((TOKENS, STATE), BF),
            jax.ShapeDtypeStruct((TOKENS, STATE), BF),
        ),
        in_specs=[pl.BlockSpec(memory_space=pltpu.HBM)] * 7,
        out_specs=(anywhere, anywhere, anywhere),
        scratch_shapes=[
            pltpu.VMEM((TOKENS, CHANNELS), BF),
            pltpu.VMEM((TOKENS, STATE), BF),
            pltpu.VMEM((TOKENS, STATE), BF),
            pltpu.VMEM((TOKENS, CHANNELS), BF),
            pltpu.VMEM((TOKENS, CHANNELS), BF),
            pltpu.VMEM((TOKENS, STATE), BF),
            pltpu.VMEM((TOKENS, STATE), BF),
            pltpu.VMEM((HEADS, TOKENS), BF),
            pltpu.VMEM((CHANNELS, STATE), F32),
            pltpu.VMEM((CHANNELS, STATE), F32),
            pltpu.VMEM((TILES, 3, 2, LANES), BF),
            pltpu.VMEM((TILES, 2, 8, LANES), BF),
            pltpu.VMEM((TILES, 2, 8, LANES), BF),
            pltpu.VMEM((TILES, 3, 2, LANES), BF),
            pltpu.VMEM((TILES, 2, 8, LANES), BF),
            pltpu.VMEM((TILES, 2, 8, LANES), BF),
            pltpu.VMEM((TILES, 2, 8, LANES), BF),
            pltpu.VMEM((TILES, 4, LANES), BF),
            pltpu.VMEM((TILES, 2, 8, LANES), BF),
            pltpu.VMEM((TILES, 4, LANES), BF),
            pltpu.VMEM((TOKENS, CHANNELS), F32),
            pltpu.VMEM((TOKENS, CHANNELS), F32),
            pltpu.VMEM((TOKENS, CHANNELS), BF),
            pltpu.VMEM((TOKENS, CHANNELS), BF),
            pltpu.VMEM((TOKENS, CHANNELS), F32),
            pltpu.VMEM((TOKENS, CHANNELS), BF),
            pltpu.VMEM((TOKENS, CHANNELS), BF),
            pltpu.VMEM((2, PAIRS, STATE, LANES), F32),
            pltpu.VMEM((2, PAIRS, STATE, LANES), BF),
            pltpu.VMEM((2, PAIRS, 2, LANES), F32),
            pltpu.VMEM((2, HALF, STATE, LANES), BF),
            pltpu.VMEM((2, PAIRS, 2, LANES), F32),
            pltpu.VMEM((2, HALF, STATE, LANES), BF),
            pltpu.VMEM((2, HALF, STATE, LANES), BF),
            pltpu.VMEM((2, HALF, STATE, LANES), BF),
            pltpu.VMEM((2, PAIRS, STATE, LANES), BF),
            pltpu.VMEM((STATE, CHANNELS), BF),
            pltpu.VMEM((TOKENS, CHANNELS), BF),
            pltpu.VMEM((TOKENS, CHANNELS), BF),
            pltpu.VMEM((3, TOKENS, LANES), BF),
            pltpu.VMEM((TOKENS, CHANNELS), F32),
            pltpu.SemaphoreType.DMA((7,)),
            pltpu.SemaphoreType.DMA((3,)),
            pltpu.SemaphoreType.DMA((5,)),
            pltpu.SemaphoreType.DMA((5,)),
            pltpu.SemaphoreType.DMA((2, 2)),
            pltpu.SemaphoreType.DMA((2, 2)),
            pltpu.SemaphoreType.DMA((2, HALF, PIECES_MAX)),
            pltpu.SemaphoreType.DMA((2, HALF, PIECES_MAX)),
            pltpu.SemaphoreType.DMA((2, HALF, PIECES_MAX)),
            pltpu.SemaphoreType.DMA((2, HALF, PIECES_MAX)),
        ],
        compiler_params=pltpu.CompilerParams(
            collective_id=0, has_side_effects=True, vmem_limit_bytes=63 * 1024 * 1024
        ),
        cost_estimate=pl.CostEstimate(
            flops=800_000_000, bytes_accessed=2_600_000, transcendentals=1_000_000
        ),
        name="scan_backward",
    )(
        inputs.reshape(TOKENS, CHANNELS),
        grad_out.reshape(TOKENS, CHANNELS),
        b_proj.reshape(TOKENS, STATE),
        c_proj.reshape(TOKENS, STATE),
        log_decay.reshape(HEADS, TOKENS),
        saved_raster.reshape(CHANNELS, STATE),
        saved_column.reshape(CHANNELS, STATE),
    )
    out_x, out_b, out_c = pl.pallas_call(
        hand_over,
        out_shape=(
            jax.ShapeDtypeStruct((TOKENS, CHANNELS), BF),
            jax.ShapeDtypeStruct((TOKENS, STATE), BF),
            jax.ShapeDtypeStruct((TOKENS, STATE), BF),
        ),
        in_specs=[anywhere] * 3,
        out_specs=(anywhere, anywhere, anywhere),
        scratch_shapes=[
            pltpu.VMEM((TOKENS, CHANNELS), BF),
            pltpu.VMEM((TOKENS, STATE), BF),
            pltpu.VMEM((TOKENS, STATE), BF),
            pltpu.SemaphoreType.DMA((3,)),
            pltpu.SemaphoreType.DMA((3,)),
        ],
        compiler_params=pltpu.CompilerParams(vmem_limit_bytes=63 * 1024 * 1024),
        cost_estimate=pl.CostEstimate(flops=0, bytes_accessed=640_000, transcendentals=0),
        name="hand_over",
    )(out_x, out_b, out_c)
    return (
        out_x.reshape(1, 1, TOKENS, CHANNELS),
        out_b.reshape(1, 1, TOKENS, STATE),
        out_c.reshape(1, 1, TOKENS, STATE),
    )


def solution(mesh):
    in_specs = (
        P("frames", "tiles", None, None),
        P("frames", "tiles", None, None),
        P("frames", "tiles", None, None),
        P("frames", "tiles", None, None),
        P(None, "frames", "tiles", None),
        P("frames", "tiles", None, None, None),
        P("frames", "tiles", None, None, None),
    )
    out_specs = (
        P("frames", "tiles", None, None),
        P("frames", "tiles", None, None),
        P("frames", "tiles", None, None),
    )
    return jax.shard_map(shards, mesh=mesh, in_specs=in_specs, out_specs=out_specs, check_vma=False)
```

```python
import jax
import jax.numpy as jnp
from jax import lax
from jax.experimental import pallas as pl
from jax.experimental.pallas import tpu as pltpu
from jax.sharding import PartitionSpec as P

HEADS = 16
HEAD_DIM = 64
STATE = 128
TOKENS = 128
CHANNELS = 1024
LANES = 128
PAIRS = CHANNELS // LANES
TILES = 64
DEPTH_Z = 16
DEPTH_X = 4
FRAMES = 8
HALF = PAIRS // 2
BEHIND = 8
PER_HOP = 7
LEFT = 6
PIECES = (1, 2)
PIECES_MAX = 2
BF = jnp.bfloat16
F32 = jnp.float32
MESH = pl.DeviceIdType.MESH


def nn(a, b):
    return lax.dot_general(a, b, (((1,), (0,)), ((), ())), preferred_element_type=F32)


def nt(a, b):
    return lax.dot_general(a, b, (((1,), (1,)), ((), ())), preferred_element_type=F32)


def iota(shape, dim):
    return lax.broadcasted_iota(jnp.int32, shape, dim)


def ones_where(cond):
    return jnp.where(cond, 1.0, 0.0).astype(BF)


def square(shape=(TOKENS, TOKENS)):
    return iota(shape, 0), iota(shape, 1)


def place(index, column_order):
    if not column_order:
        return index
    return lax.shift_left(index & 1, 6) + lax.shift_right_logical(index, 1)


def causal(column_order):
    t, s = square()
    return place(s, column_order) <= place(t, column_order)


def causal_transposed(column_order):
    s, t = square()
    return place(s, column_order) <= place(t, column_order)


def high(index, bits):
    return lax.shift_right_logical(index, bits)


def interleave(back=False):
    r, c = square()
    if back:
        r, c = c, r
    return ones_where((high(r, 3) == (c & 15)) & ((r & 7) == high(c, 4)))


def identity():
    r, c = square()
    return ones_where(r == c)


def maps_matrix(parts, back=False):
    shape = (32 * parts, 32 * parts)
    if back:
        c, r = square(shape[::-1])
    else:
        r, c = square(shape)
    part, token = high(c, 5), c & 31
    return ones_where(r == high(token, 1) * (2 * parts) + part * 2 + (token & 1))


def pair(k):
    return slice(LANES * k, LANES * k + LANES)


def pack_channels(read, write):
    mix = interleave()
    for q in range(8):
        stack = jnp.concatenate([read(q, k) for k in range(PAIRS)], axis=0)
        write(q, nn(mix, stack).reshape(8, 2, 8, LANES).astype(BF))


def unpack_channels(read, write):
    mix = interleave(True)
    for q in range(8):
        tiles = read(q).astype(F32).reshape(TOKENS, LANES).astype(BF)
        out = nn(mix, tiles)
        for k in range(PAIRS):
            write(q, k, out[16 * k : 16 * k + 16, :])


def block_scales(decays, column_order, shrink, grow, ends):
    run = ones_where(causal(column_order))
    head, channel = square((TOKENS, LANES))
    for k in range(PAIRS):
        spread = ones_where(high(channel, 6) + 2 * k == head)
        cum = nn(run, nn(decays, spread).astype(BF))
        total = cum[TOKENS - 1 : TOKENS, :]
        middle = total * 0.5
        shrink[:, pair(k)] = jnp.exp(cum - middle)
        grow[:, pair(k)] = jnp.exp(middle - cum)
        ends[k, 0:1, :] = jnp.exp(middle)
        ends[k, 1:2, :] = jnp.exp(total)


def scale_grad(value, rows, k, shrink, refs):
    grow, ends, centred, headed = refs
    shrunk = value.astype(F32) * shrink[rows, pair(k)]
    centred[rows, pair(k)] = shrunk.astype(BF)
    headed[rows, pair(k)] = (shrunk * ends[k, 0:1, :]).astype(BF)


def block_states(c_rows, refs, term, low):
    grow, ends, centred, headed = refs
    c_turned = nt(identity(), c_rows).astype(BF)
    for k in range(PAIRS):
        state = nn(c_turned, headed[:, pair(k)])
        term[k] = state
        low[k] = state.astype(BF)


def grad_of_x(b_rows, c_rows, carry, column_order, refs, tails, write):
    grow, ends, centred, headed = refs
    pairing = jnp.where(causal_transposed(column_order), nt(b_rows, c_rows), 0.0).astype(BF)
    both = jnp.concatenate([pairing, b_rows], axis=1)
    for k in range(PAIRS):
        tail = (carry(k).astype(F32) * ends[k, 0:1, :]).astype(BF)
        tails[:, pair(k)] = tail
        stack = jnp.concatenate([centred[:, pair(k)], tail], axis=0)
        write(k, nn(both, stack) * grow[:, pair(k)])


def grads_of_maps(x, b_rows, c_rows, saved, column_order, refs, tails, scaled):
    grow, ends, centred, headed = refs
    for k in range(PAIRS):
        scaled[:, pair(k)] = (x[:, pair(k)].astype(F32) * grow[:, pair(k)]).astype(BF)
    mixed = jnp.where(causal(column_order), nt(centred[...], scaled[...]), 0.0)
    part_b = nn(mixed.T.astype(BF), c_rows) + nt(scaled[...], tails[...])
    part_c = nn(mixed.astype(BF), b_rows) + nn(headed[...], saved[...].astype(BF))
    return part_b, part_c


def kernel(
    x_hbm, g_hbm, b_hbm, c_hbm, d_hbm, saved_row_hbm, saved_col_hbm,
    out_x_hbm, out_b_hbm, out_c_hbm,
    out_x, out_b, out_c,
    x_ref, g_ref, b_ref, c_ref, d_ref, saved_row, saved_col,
    send_m, send_g, send_x, got_m, got_g, got_x, back_x, back_m, home_x, home_m,
    shrink, row_grow, row_centred, row_headed, col_grow, col_centred, col_headed,
    term, low, ends, peer_low, peer_ends, incoming, outgoing, give, carry,
    tails, scaled, wide, col_maps, part_x,
    load_sem, store_sem, send_sem, recv_sem, swap_send, swap_recv, hop_send, hop_recv, give_send, give_recv,
):
    f = lax.axis_index("frames")
    me = lax.axis_index("tiles")
    z, x = lax.div(me, DEPTH_X), lax.rem(me, DEPTH_X)

    loads = [
        pltpu.make_async_copy(source, target, load_sem.at[i])
        for i, (source, target) in enumerate([
            (g_hbm, g_ref), (b_hbm, b_ref), (c_hbm, c_ref), (d_hbm, d_ref), (x_hbm, x_ref),
            (saved_row_hbm, saved_row), (saved_col_hbm, saved_col),
        ])
    ]
    for load in loads[:4]:
        load.start()

    xs = [lax.rem(x + dx, DEPTH_X) for dx in range(DEPTH_X)]

    def each_partner(act):
        opposite = lax.rem(z + DEPTH_Z // 2, DEPTH_Z) * DEPTH_X
        for dx in range(DEPTH_X):
            act(opposite + xs[dx])

        @pl.loop(1, DEPTH_Z // 2)
        def _(k):
            far = DEPTH_Z // 2 - k
            ahead = lax.rem(z + far, DEPTH_Z) * DEPTH_X
            behind = lax.rem(z - far + DEPTH_Z, DEPTH_Z) * DEPTH_X
            for dx in range(DEPTH_X):
                act(ahead + xs[dx])
                act(behind + xs[dx])

        for dx in range(1, DEPTH_X):
            act(z * DEPTH_X + xs[dx])

    def partner(k):
        step = TILES + 3 - k
        far, r = lax.div(step, 8), lax.rem(step, 8)
        most, none = lax.div(far, 8), lax.div(8 - far, 8)
        dx = (1 - most - none) * lax.div(r, 2) + most * r + none * (r - DEPTH_X)
        dz = far * (1 - 2 * lax.rem(r, 2))
        return lax.rem(z + dz + DEPTH_Z, DEPTH_Z) * DEPTH_X + lax.rem(x + dx, DEPTH_X)

    barrier = pltpu.get_barrier_semaphore()

    def greet(peer):
        pl.semaphore_signal(barrier, inc=1, device_id=(f, peer), device_id_type=MESH)

    each_partner(greet)

    core, chip_y = lax.rem(f, 2), lax.div(f, 2)
    other = f + 1 - 2 * core
    above, below = lax.rem(f + 2, FRAMES), lax.rem(f + FRAMES - 2, FRAMES)
    mine, theirs = core * HALF, HALF - core * HALF
    for neighbour in (other, above, below):
        pl.semaphore_signal(barrier, inc=1, device_id=(neighbour, me), device_id_type=MESH)

    for load in loads[4:]:
        load.start()

    def keep_own(source, target):
        target[pl.ds(me, 1)] = source[pl.ds(me, 1)]

    def send(source, target, which, peer):
        pltpu.make_async_remote_copy(
            src_ref=source.at[peer],
            dst_ref=target.at[me],
            send_sem=send_sem.at[which],
            recv_sem=recv_sem.at[which],
            device_id=(f, peer),
            device_id_type=MESH,
        ).start()

    def exchange(source, target, which):
        each_partner(lambda peer: send(source, target, which, peer))

    def exchange_some(source, target, which, first, last=TILES - 1):
        @pl.loop(first, last)
        def _(k):
            send(source, target, which, partner(k))

    def wait_all(ref, sem):
        some = ref.at[pl.ds(0, TILES - 1)]
        pltpu.make_async_copy(some, some, sem).wait()

    def put_g(q, value):
        send_g[8 * q : 8 * q + 8] = value

    def put_x(q, value):
        send_x[8 * q : 8 * q + 8] = value

    def reader(ref):
        return lambda q, k: ref[16 * q : 16 * q + 16, pair(k)]

    for i in (1, 2, 3):
        loads[i].wait()
    decays = nt(identity(), jnp.concatenate(
        [d_ref[...], jnp.zeros((TOKENS - HEADS, TOKENS), BF)], axis=0)).astype(BF)
    b_rows, c_rows = b_ref[...], c_ref[...]
    spread_maps = maps_matrix(3)
    for q in range(4):
        rows = slice(32 * q, 32 * q + 32)
        stack = jnp.concatenate([b_rows[rows], c_rows[rows], decays[rows]], axis=0)
        packed = nn(spread_maps, stack).reshape(16, 3, 2, LANES).astype(BF)
        send_m[16 * q : 16 * q + 16] = packed
    pl.semaphore_wait(barrier, TILES + 2)
    exchange(send_m, got_m, 4)
    loads[0].wait()
    pack_channels(reader(g_ref), put_g)
    exchange(send_g, got_g, 0)
    keep_own(send_m, got_m)
    keep_own(send_g, got_g)

    @pl.when(chip_y == FRAMES // 2 - 1)
    def _():
        incoming[...] = jnp.zeros_like(incoming)

    def swap_copies(order):
        return [
            pltpu.make_async_remote_copy(
                src_ref=source,
                dst_ref=target,
                send_sem=swap_send.at[order, i],
                recv_sem=swap_recv.at[order, i],
                device_id=(other, me),
                device_id_type=MESH,
            )
            for i, (source, target) in enumerate([
                (ends.at[order], peer_ends.at[order]),
                (low.at[order, pl.ds(theirs, HALF)], peer_low.at[order]),
            ])
        ]

    def rows_of(order, p):
        rows = STATE // PIECES[order]
        return pl.ds(rows * p, rows)

    def hop_copy(order, i, p):
        return pltpu.make_async_remote_copy(
            src_ref=outgoing.at[order, i, rows_of(order, p)],
            dst_ref=incoming.at[order, i, rows_of(order, p)],
            send_sem=hop_send.at[order, i, p],
            recv_sem=hop_recv.at[order, i, p],
            device_id=(below, me),
            device_id_type=MESH,
        )

    def give_copy(order, i, p):
        return pltpu.make_async_remote_copy(
            src_ref=give.at[order, i, rows_of(order, p)],
            dst_ref=carry.at[order, mine + i, rows_of(order, p)],
            send_sem=give_send.at[order, i, p],
            recv_sem=give_recv.at[order, i, p],
            device_id=(other, me),
            device_id_type=MESH,
        )

    def swapped(order):
        for copy in swap_copies(order):
            copy.wait_recv()

    def steps(order):
        return [(i, p) for i in range(HALF) for p in range(PIECES[order])]

    def chain(order):
        lower = core == 0
        for i, p in steps(order):
            k, rows = mine + i, rows_of(order, p)

            @pl.when(chip_y < FRAMES // 2 - 1)
            def _():
                hop_copy(order, i, p).wait_recv()

            own_state, peer_state = term[order, k, rows], peer_low[order, i, rows].astype(F32)
            own_decay, peer_decay = ends[order, k, 1:2, :], peer_ends[order, k, 1:2, :]
            lower_state = jnp.where(lower, own_state, peer_state)
            upper_state = jnp.where(lower, peer_state, own_state)
            lower_decay = jnp.where(lower, own_decay, peer_decay)
            upper_decay = jnp.where(lower, peer_decay, own_decay)
            entering = incoming[order, i, rows].astype(F32)
            between = upper_decay * entering + upper_state

            @pl.when(chip_y > 0)
            def _():
                outgoing[order, i, rows] = (lower_decay * between + lower_state).astype(BF)
                hop_copy(order, i, p).start()

            carry[order, k, rows] = jnp.where(lower, between, entering).astype(BF)
            give[order, i, rows] = jnp.where(lower, entering, between).astype(BF)
            give_copy(order, i, p).start()

    def chain_end(order):
        for i, p in steps(order):
            some = carry.at[order, theirs + i, rows_of(order, p)]
            pltpu.make_async_copy(some, some, give_recv.at[order, i, p]).wait()

    def chain_sent(order):
        for copy in swap_copies(order):
            copy.wait_send()
        for i, p in steps(order):
            give_copy(order, i, p).wait_send()

            @pl.when(chip_y > 0)
            def _():
                hop_copy(order, i, p).wait_send()

    row_refs = (row_grow, ends.at[0], row_centred, row_headed)
    block_scales(decays, False, shrink, row_grow, ends.at[0])
    for k in range(PAIRS):
        scale_grad(g_ref[:, pair(k)], slice(0, TOKENS), k, shrink, row_refs)
    block_states(c_rows, row_refs, term.at[0], low.at[0])
    for copy in swap_copies(0):
        copy.start()
    loads[4].wait()
    pack_channels(reader(x_ref), put_x)
    exchange_some(send_x, got_x, 1, 0, BEHIND)
    keep_own(send_x, got_x)

    wait_all(got_m, recv_sem.at[4])
    gather_maps = maps_matrix(3, True)
    for q in range(4):
        tiles = got_m[16 * q : 16 * q + 16].astype(F32).reshape(96, LANES).astype(BF)
        piece = nn(gather_maps, tiles).astype(BF)
        for p in range(3):
            col_maps[p, 32 * q : 32 * q + 32] = piece[32 * p : 32 * p + 32]
    col_refs = (col_grow, ends.at[1], col_centred, col_headed)
    block_scales(col_maps[2], True, shrink, col_grow, ends.at[1])
    swapped(0)

    wait_all(got_g, recv_sem.at[0])

    def put_wide(q, k, value):
        wide[16 * q : 16 * q + 16, pair(k)] = value.astype(BF)

    def put_scaled(q, k, value):
        scale_grad(value, slice(16 * q, 16 * q + 16), k, shrink, col_refs)

    unpack_channels(lambda q: got_g[8 * q : 8 * q + 8], put_scaled)
    block_states(col_maps[1], col_refs, term.at[1], low.at[1])
    for copy in swap_copies(1):
        copy.start()
    filled = BEHIND + PER_HOP * (FRAMES // 2 - chip_y)
    packed_by = TILES - 1 - LEFT * chip_y
    exchange_some(send_x, got_x, 1, BEHIND, filled)
    swapped(1)
    chain(1)
    exchange_some(send_x, got_x, 1, filled, packed_by)
    chain_end(1)

    def put_col(k, value):
        wide[:, pair(k)] = value.astype(BF)

    grad_of_x(col_maps[0], col_maps[1], lambda k: carry[1, k], True, col_refs, tails, put_col)

    def put_back(q, value):
        back_x[8 * q : 8 * q + 8] = value

    pack_channels(reader(wide), put_back)
    chain(0)
    exchange_some(send_x, got_x, 1, packed_by)
    exchange(back_x, home_x, 2)
    keep_own(back_x, home_x)

    wait_all(got_x, recv_sem.at[1])
    loads[6].wait()
    unpack_channels(lambda q: got_x[8 * q : 8 * q + 8], put_wide)
    col_b, col_c = grads_of_maps(
        wide, col_maps[0], col_maps[1], saved_col, True, col_refs, tails, scaled)
    col_b, col_c = col_b.astype(BF), col_c.astype(BF)
    spread_back = maps_matrix(2)
    for q in range(4):
        rows = slice(32 * q, 32 * q + 32)
        stack = jnp.concatenate([col_b[rows], col_c[rows]], axis=0)
        packed = nn(spread_back, stack).reshape(16, 4, LANES).astype(BF)
        back_m[16 * q : 16 * q + 16] = packed
    exchange(back_m, home_m, 3)
    keep_own(back_m, home_m)

    def put_row(k, value):
        part_x[:, pair(k)] = value

    chain_end(0)
    grad_of_x(b_rows, c_rows, lambda k: carry[0, k], False, row_refs, tails, put_row)
    loads[5].wait()
    row_b, row_c = grads_of_maps(
        x_ref, b_rows, c_rows, saved_row, False, row_refs, tails, scaled)

    wait_all(home_x, recv_sem.at[2])

    def put_sum(q, k, value):
        rows = slice(16 * q, 16 * q + 16)
        out_x[rows, pair(k)] = (part_x[rows, pair(k)] + value).astype(BF)

    unpack_channels(lambda q: home_x[8 * q : 8 * q + 8], put_sum)

    stores = [
        pltpu.make_async_copy(source, target, store_sem.at[i])
        for i, (source, target) in enumerate(
            [(out_x, out_x_hbm), (out_b, out_b_hbm), (out_c, out_c_hbm)])
    ]
    stores[0].start()

    wait_all(home_m, recv_sem.at[3])
    gather_back = maps_matrix(2, True)
    for q in range(4):
        rows = slice(32 * q, 32 * q + 32)
        tiles = home_m[16 * q : 16 * q + 16].astype(F32).reshape(64, LANES).astype(BF)
        both = nn(gather_back, tiles)
        out_b[rows, :] = (row_b[rows] + both[0:32]).astype(BF)
        out_c[rows, :] = (row_c[rows] + both[32:64]).astype(BF)

    stores[1].start()
    stores[2].start()
    chain_sent(0)
    chain_sent(1)
    wait_all(send_m, send_sem.at[4])
    wait_all(send_g, send_sem.at[0])
    wait_all(send_x, send_sem.at[1])
    wait_all(back_x, send_sem.at[2])
    wait_all(back_m, send_sem.at[3])
    for store in stores:
        store.wait()


def hand_over(x_in, b_in, c_in, x_out, b_out, c_out, x_held, b_held, c_held, load_sem, store_sem):
    parts = [(x_in, x_held, x_out), (b_in, b_held, b_out), (c_in, c_held, c_out)]
    loads = [pltpu.make_async_copy(p[0], p[1], load_sem.at[i]) for i, p in enumerate(parts)]
    stores = [pltpu.make_async_copy(p[1], p[2], store_sem.at[i]) for i, p in enumerate(parts)]
    for load in loads:
        load.start()
    for load, store in zip(loads, stores):
        load.wait()
        store.start()
    for store in stores:
        store.wait()


def shards(inputs, grad_out, b_proj, c_proj, log_decay, saved_raster, saved_column):
    anywhere = pl.BlockSpec(memory_space=pl.ANY)
    out_x, out_b, out_c = pl.pallas_call(
        kernel,
        out_shape=(
            jax.ShapeDtypeStruct((TOKENS, CHANNELS), BF),
            jax.ShapeDtypeStruct((TOKENS, STATE), BF),
            jax.ShapeDtypeStruct((TOKENS, STATE), BF),
        ),
        in_specs=[pl.BlockSpec(memory_space=pltpu.HBM)] * 7,
        out_specs=(anywhere, anywhere, anywhere),
        scratch_shapes=[
            pltpu.VMEM((TOKENS, CHANNELS), BF),
            pltpu.VMEM((TOKENS, STATE), BF),
            pltpu.VMEM((TOKENS, STATE), BF),
            pltpu.VMEM((TOKENS, CHANNELS), BF),
            pltpu.VMEM((TOKENS, CHANNELS), BF),
            pltpu.VMEM((TOKENS, STATE), BF),
            pltpu.VMEM((TOKENS, STATE), BF),
            pltpu.VMEM((HEADS, TOKENS), BF),
            pltpu.VMEM((CHANNELS, STATE), F32),
            pltpu.VMEM((CHANNELS, STATE), F32),
            pltpu.VMEM((TILES, 3, 2, LANES), BF),
            pltpu.VMEM((TILES, 2, 8, LANES), BF),
            pltpu.VMEM((TILES, 2, 8, LANES), BF),
            pltpu.VMEM((TILES, 3, 2, LANES), BF),
            pltpu.VMEM((TILES, 2, 8, LANES), BF),
            pltpu.VMEM((TILES, 2, 8, LANES), BF),
            pltpu.VMEM((TILES, 2, 8, LANES), BF),
            pltpu.VMEM((TILES, 4, LANES), BF),
            pltpu.VMEM((TILES, 2, 8, LANES), BF),
            pltpu.VMEM((TILES, 4, LANES), BF),
            pltpu.VMEM((TOKENS, CHANNELS), F32),
            pltpu.VMEM((TOKENS, CHANNELS), F32),
            pltpu.VMEM((TOKENS, CHANNELS), BF),
            pltpu.VMEM((TOKENS, CHANNELS), BF),
            pltpu.VMEM((TOKENS, CHANNELS), F32),
            pltpu.VMEM((TOKENS, CHANNELS), BF),
            pltpu.VMEM((TOKENS, CHANNELS), BF),
            pltpu.VMEM((2, PAIRS, STATE, LANES), F32),
            pltpu.VMEM((2, PAIRS, STATE, LANES), BF),
            pltpu.VMEM((2, PAIRS, 2, LANES), F32),
            pltpu.VMEM((2, HALF, STATE, LANES), BF),
            pltpu.VMEM((2, PAIRS, 2, LANES), F32),
            pltpu.VMEM((2, HALF, STATE, LANES), BF),
            pltpu.VMEM((2, HALF, STATE, LANES), BF),
            pltpu.VMEM((2, HALF, STATE, LANES), BF),
            pltpu.VMEM((2, PAIRS, STATE, LANES), BF),
            pltpu.VMEM((STATE, CHANNELS), BF),
            pltpu.VMEM((TOKENS, CHANNELS), BF),
            pltpu.VMEM((TOKENS, CHANNELS), BF),
            pltpu.VMEM((3, TOKENS, LANES), BF),
            pltpu.VMEM((TOKENS, CHANNELS), F32),
            pltpu.SemaphoreType.DMA((7,)),
            pltpu.SemaphoreType.DMA((3,)),
            pltpu.SemaphoreType.DMA((5,)),
            pltpu.SemaphoreType.DMA((5,)),
            pltpu.SemaphoreType.DMA((2, 2)),
            pltpu.SemaphoreType.DMA((2, 2)),
            pltpu.SemaphoreType.DMA((2, HALF, PIECES_MAX)),
            pltpu.SemaphoreType.DMA((2, HALF, PIECES_MAX)),
            pltpu.SemaphoreType.DMA((2, HALF, PIECES_MAX)),
            pltpu.SemaphoreType.DMA((2, HALF, PIECES_MAX)),
        ],
        compiler_params=pltpu.CompilerParams(
            collective_id=0, has_side_effects=True, vmem_limit_bytes=63 * 1024 * 1024
        ),
        cost_estimate=pl.CostEstimate(
            flops=800_000_000, bytes_accessed=2_600_000, transcendentals=1_000_000
        ),
        name="scan_backward",
    )(
        inputs.reshape(TOKENS, CHANNELS),
        grad_out.reshape(TOKENS, CHANNELS),
        b_proj.reshape(TOKENS, STATE),
        c_proj.reshape(TOKENS, STATE),
        log_decay.reshape(HEADS, TOKENS),
        saved_raster.reshape(CHANNELS, STATE),
        saved_column.reshape(CHANNELS, STATE),
    )
    out_x, out_b, out_c = pl.pallas_call(
        hand_over,
        out_shape=(
            jax.ShapeDtypeStruct((TOKENS, CHANNELS), BF),
            jax.ShapeDtypeStruct((TOKENS, STATE), BF),
            jax.ShapeDtypeStruct((TOKENS, STATE), BF),
        ),
        in_specs=[anywhere] * 3,
        out_specs=(anywhere, anywhere, anywhere),
        scratch_shapes=[
            pltpu.VMEM((TOKENS, CHANNELS), BF),
            pltpu.VMEM((TOKENS, STATE), BF),
            pltpu.VMEM((TOKENS, STATE), BF),
            pltpu.SemaphoreType.DMA((3,)),
            pltpu.SemaphoreType.DMA((3,)),
        ],
        compiler_params=pltpu.CompilerParams(vmem_limit_bytes=63 * 1024 * 1024),
        cost_estimate=pl.CostEstimate(flops=0, bytes_accessed=640_000, transcendentals=0),
        name="hand_over",
    )(out_x, out_b, out_c)
    return (
        out_x.reshape(1, 1, TOKENS, CHANNELS),
        out_b.reshape(1, 1, TOKENS, STATE),
        out_c.reshape(1, 1, TOKENS, STATE),
    )


def solution(mesh):
    in_specs = (
        P("frames", "tiles", None, None),
        P("frames", "tiles", None, None),
        P("frames", "tiles", None, None),
        P("frames", "tiles", None, None),
        P(None, "frames", "tiles", None),
        P("frames", "tiles", None, None, None),
        P("frames", "tiles", None, None, None),
    )
    out_specs = (
        P("frames", "tiles", None, None),
        P("frames", "tiles", None, None),
        P("frames", "tiles", None, None),
    )
    return jax.shard_map(shards, mesh=mesh, in_specs=in_specs, out_specs=out_specs, check_vma=False)
```

```python
import jax
import jax.numpy as jnp
from jax import lax
from jax.experimental import pallas as pl
from jax.experimental.pallas import tpu as pltpu
from jax.sharding import PartitionSpec as P

HEADS = 16
HEAD_DIM = 64
STATE = 128
TOKENS = 128
CHANNELS = 1024
LANES = 128
PAIRS = CHANNELS // LANES
TILES = 64
DEPTH_Z = 16
DEPTH_X = 4
FRAMES = 8
HALF = PAIRS // 2
BEHIND = 8
PER_HOP = 7
LEFT = 6
RETURNED = 20
PIECES = (1, 2)
PIECES_MAX = 2
BF = jnp.bfloat16
F32 = jnp.float32
MESH = pl.DeviceIdType.MESH


def nn(a, b):
    return lax.dot_general(a, b, (((1,), (0,)), ((), ())), preferred_element_type=F32)


def nt(a, b):
    return lax.dot_general(a, b, (((1,), (1,)), ((), ())), preferred_element_type=F32)


def iota(shape, dim):
    return lax.broadcasted_iota(jnp.int32, shape, dim)


def ones_where(cond):
    return jnp.where(cond, 1.0, 0.0).astype(BF)


def square(shape=(TOKENS, TOKENS)):
    return iota(shape, 0), iota(shape, 1)


def place(index, column_order):
    if not column_order:
        return index
    return lax.shift_left(index & 1, 6) + lax.shift_right_logical(index, 1)


def causal(column_order):
    t, s = square()
    return place(s, column_order) <= place(t, column_order)


def causal_transposed(column_order):
    s, t = square()
    return place(s, column_order) <= place(t, column_order)


def high(index, bits):
    return lax.shift_right_logical(index, bits)


def interleave(back=False):
    r, c = square()
    if back:
        r, c = c, r
    return ones_where((high(r, 3) == (c & 15)) & ((r & 7) == high(c, 4)))


def identity():
    r, c = square()
    return ones_where(r == c)


def maps_matrix(parts, back=False):
    shape = (32 * parts, 32 * parts)
    if back:
        c, r = square(shape[::-1])
    else:
        r, c = square(shape)
    part, token = high(c, 5), c & 31
    return ones_where(r == high(token, 1) * (2 * parts) + part * 2 + (token & 1))


def pair(k):
    return slice(LANES * k, LANES * k + LANES)


def pack_channels(read, write):
    mix = interleave()
    for q in range(8):
        stack = jnp.concatenate([read(q, k) for k in range(PAIRS)], axis=0)
        write(q, nn(mix, stack).reshape(8, 2, 8, LANES).astype(BF))


def unpack_channels(read, write):
    mix = interleave(True)
    for q in range(8):
        tiles = read(q).astype(F32).reshape(TOKENS, LANES).astype(BF)
        out = nn(mix, tiles)
        for k in range(PAIRS):
            write(q, k, out[16 * k : 16 * k + 16, :])


def block_scales(decays, column_order, shrink, grow, ends):
    run = ones_where(causal(column_order))
    head, channel = square((TOKENS, LANES))
    for k in range(PAIRS):
        spread = ones_where(high(channel, 6) + 2 * k == head)
        cum = nn(run, nn(decays, spread).astype(BF))
        total = cum[TOKENS - 1 : TOKENS, :]
        middle = total * 0.5
        shrink[:, pair(k)] = jnp.exp(cum - middle)
        grow[:, pair(k)] = jnp.exp(middle - cum)
        ends[k, 0:1, :] = jnp.exp(middle)
        ends[k, 1:2, :] = jnp.exp(total)


def scale_grad(value, rows, k, shrink, refs):
    grow, ends, centred, headed = refs
    shrunk = value.astype(F32) * shrink[rows, pair(k)]
    centred[rows, pair(k)] = shrunk.astype(BF)
    headed[rows, pair(k)] = (shrunk * ends[k, 0:1, :]).astype(BF)


def block_states(c_rows, refs, term, low):
    grow, ends, centred, headed = refs
    c_turned = nt(identity(), c_rows).astype(BF)
    for k in range(PAIRS):
        state = nn(c_turned, headed[:, pair(k)])
        term[k] = state
        low[k] = state.astype(BF)


def grad_of_x(b_rows, c_rows, carry, column_order, refs, tails, write):
    grow, ends, centred, headed = refs
    pairing = jnp.where(causal_transposed(column_order), nt(b_rows, c_rows), 0.0).astype(BF)
    both = jnp.concatenate([pairing, b_rows], axis=1)
    for k in range(PAIRS):
        tail = (carry(k).astype(F32) * ends[k, 0:1, :]).astype(BF)
        tails[:, pair(k)] = tail
        stack = jnp.concatenate([centred[:, pair(k)], tail], axis=0)
        write(k, nn(both, stack) * grow[:, pair(k)])


def grads_of_maps(x, b_rows, c_rows, saved, column_order, refs, tails, scaled):
    grow, ends, centred, headed = refs
    for k in range(PAIRS):
        scaled[:, pair(k)] = (x[:, pair(k)].astype(F32) * grow[:, pair(k)]).astype(BF)
    mixed = jnp.where(causal(column_order), nt(centred[...], scaled[...]), 0.0)
    part_b = nn(mixed.T.astype(BF), c_rows) + nt(scaled[...], tails[...])
    part_c = nn(mixed.astype(BF), b_rows) + nn(headed[...], saved[...].astype(BF))
    return part_b, part_c


def kernel(
    x_hbm, g_hbm, b_hbm, c_hbm, d_hbm, saved_row_hbm, saved_col_hbm,
    out_x_hbm, out_b_hbm, out_c_hbm,
    out_x, out_b, out_c,
    x_ref, g_ref, b_ref, c_ref, d_ref, saved_row, saved_col,
    send_m, send_g, send_x, got_m, got_g, got_x, back_x, back_m, home_x, home_m,
    shrink, row_grow, row_centred, row_headed, col_grow, col_centred, col_headed,
    term, low, ends, peer_low, peer_ends, incoming, outgoing, give, carry,
    tails, scaled, wide, col_maps, part_x,
    load_sem, store_sem, send_sem, recv_sem, swap_send, swap_recv, hop_send, hop_recv, give_send, give_recv,
):
    f = lax.axis_index("frames")
    me = lax.axis_index("tiles")
    z, x = lax.div(me, DEPTH_X), lax.rem(me, DEPTH_X)

    loads = [
        pltpu.make_async_copy(source, target, load_sem.at[i])
        for i, (source, target) in enumerate([
            (g_hbm, g_ref), (b_hbm, b_ref), (c_hbm, c_ref), (d_hbm, d_ref), (x_hbm, x_ref),
            (saved_row_hbm, saved_row), (saved_col_hbm, saved_col),
        ])
    ]
    for load in loads[:4]:
        load.start()

    xs = [lax.rem(x + dx, DEPTH_X) for dx in range(DEPTH_X)]

    def each_partner(act):
        opposite = lax.rem(z + DEPTH_Z // 2, DEPTH_Z) * DEPTH_X
        for dx in range(DEPTH_X):
            act(opposite + xs[dx])

        @pl.loop(1, DEPTH_Z // 2)
        def _(k):
            far = DEPTH_Z // 2 - k
            ahead = lax.rem(z + far, DEPTH_Z) * DEPTH_X
            behind = lax.rem(z - far + DEPTH_Z, DEPTH_Z) * DEPTH_X
            for dx in range(DEPTH_X):
                act(ahead + xs[dx])
                act(behind + xs[dx])

        for dx in range(1, DEPTH_X):
            act(z * DEPTH_X + xs[dx])

    def partner(k):
        step = TILES + 3 - k
        far, r = lax.div(step, 8), lax.rem(step, 8)
        most, none = lax.div(far, 8), lax.div(8 - far, 8)
        dx = (1 - most - none) * lax.div(r, 2) + most * r + none * (r - DEPTH_X)
        dz = far * (1 - 2 * lax.rem(r, 2))
        return lax.rem(z + dz + DEPTH_Z, DEPTH_Z) * DEPTH_X + lax.rem(x + dx, DEPTH_X)

    barrier = pltpu.get_barrier_semaphore()

    def greet(peer):
        pl.semaphore_signal(barrier, inc=1, device_id=(f, peer), device_id_type=MESH)

    each_partner(greet)

    core, chip_y = lax.rem(f, 2), lax.div(f, 2)
    other = f + 1 - 2 * core
    above, below = lax.rem(f + 2, FRAMES), lax.rem(f + FRAMES - 2, FRAMES)
    mine, theirs = core * HALF, HALF - core * HALF
    for neighbour in (other, above, below):
        pl.semaphore_signal(barrier, inc=1, device_id=(neighbour, me), device_id_type=MESH)

    for load in loads[4:]:
        load.start()

    def keep_own(source, target):
        target[pl.ds(me, 1)] = source[pl.ds(me, 1)]

    def send(source, target, which, peer):
        pltpu.make_async_remote_copy(
            src_ref=source.at[peer],
            dst_ref=target.at[me],
            send_sem=send_sem.at[which],
            recv_sem=recv_sem.at[which],
            device_id=(f, peer),
            device_id_type=MESH,
        ).start()

    def exchange(source, target, which):
        each_partner(lambda peer: send(source, target, which, peer))

    def exchange_some(source, target, which, first, last=TILES - 1):
        @pl.loop(first, last)
        def _(k):
            send(source, target, which, partner(k))

    def wait_all(ref, sem):
        some = ref.at[pl.ds(0, TILES - 1)]
        pltpu.make_async_copy(some, some, sem).wait()

    def put_g(q, value):
        send_g[8 * q : 8 * q + 8] = value

    def put_x(q, value):
        send_x[8 * q : 8 * q + 8] = value

    def reader(ref):
        return lambda q, k: ref[16 * q : 16 * q + 16, pair(k)]

    for i in (1, 2, 3):
        loads[i].wait()
    decays = nt(identity(), jnp.concatenate(
        [d_ref[...], jnp.zeros((TOKENS - HEADS, TOKENS), BF)], axis=0)).astype(BF)
    b_rows, c_rows = b_ref[...], c_ref[...]
    spread_maps = maps_matrix(3)
    for q in range(4):
        rows = slice(32 * q, 32 * q + 32)
        stack = jnp.concatenate([b_rows[rows], c_rows[rows], decays[rows]], axis=0)
        packed = nn(spread_maps, stack).reshape(16, 3, 2, LANES).astype(BF)
        send_m[16 * q : 16 * q + 16] = packed
    pl.semaphore_wait(barrier, TILES + 2)
    exchange(send_m, got_m, 4)
    loads[0].wait()
    pack_channels(reader(g_ref), put_g)
    exchange(send_g, got_g, 0)
    keep_own(send_m, got_m)
    keep_own(send_g, got_g)

    @pl.when(chip_y == FRAMES // 2 - 1)
    def _():
        incoming[...] = jnp.zeros_like(incoming)

    def swap_copies(order):
        return [
            pltpu.make_async_remote_copy(
                src_ref=source,
                dst_ref=target,
                send_sem=swap_send.at[order, i],
                recv_sem=swap_recv.at[order, i],
                device_id=(other, me),
                device_id_type=MESH,
            )
            for i, (source, target) in enumerate([
                (ends.at[order], peer_ends.at[order]),
                (low.at[order, pl.ds(theirs, HALF)], peer_low.at[order]),
            ])
        ]

    def rows_of(order, p):
        rows = STATE // PIECES[order]
        return pl.ds(rows * p, rows)

    def hop_copy(order, i, p):
        return pltpu.make_async_remote_copy(
            src_ref=outgoing.at[order, i, rows_of(order, p)],
            dst_ref=incoming.at[order, i, rows_of(order, p)],
            send_sem=hop_send.at[order, i, p],
            recv_sem=hop_recv.at[order, i, p],
            device_id=(below, me),
            device_id_type=MESH,
        )

    def give_copy(order, i, p):
        return pltpu.make_async_remote_copy(
            src_ref=give.at[order, i, rows_of(order, p)],
            dst_ref=carry.at[order, mine + i, rows_of(order, p)],
            send_sem=give_send.at[order, i, p],
            recv_sem=give_recv.at[order, i, p],
            device_id=(other, me),
            device_id_type=MESH,
        )

    def swapped(order):
        for copy in swap_copies(order):
            copy.wait_recv()

    def steps(order):
        return [(i, p) for i in range(HALF) for p in range(PIECES[order])]

    def chain(order):
        lower = core == 0
        for i, p in steps(order):
            k, rows = mine + i, rows_of(order, p)

            @pl.when(chip_y < FRAMES // 2 - 1)
            def _():
                hop_copy(order, i, p).wait_recv()

            own_state, peer_state = term[order, k, rows], peer_low[order, i, rows].astype(F32)
            own_decay, peer_decay = ends[order, k, 1:2, :], peer_ends[order, k, 1:2, :]
            lower_state = jnp.where(lower, own_state, peer_state)
            upper_state = jnp.where(lower, peer_state, own_state)
            lower_decay = jnp.where(lower, own_decay, peer_decay)
            upper_decay = jnp.where(lower, peer_decay, own_decay)
            entering = incoming[order, i, rows].astype(F32)
            between = upper_decay * entering + upper_state

            @pl.when(chip_y > 0)
            def _():
                outgoing[order, i, rows] = (lower_decay * between + lower_state).astype(BF)
                hop_copy(order, i, p).start()

            carry[order, k, rows] = jnp.where(lower, between, entering).astype(BF)
            give[order, i, rows] = jnp.where(lower, entering, between).astype(BF)
            give_copy(order, i, p).start()

    def chain_end(order):
        for i, p in steps(order):
            some = carry.at[order, theirs + i, rows_of(order, p)]
            pltpu.make_async_copy(some, some, give_recv.at[order, i, p]).wait()

    def chain_sent(order):
        for copy in swap_copies(order):
            copy.wait_send()
        for i, p in steps(order):
            give_copy(order, i, p).wait_send()

            @pl.when(chip_y > 0)
            def _():
                hop_copy(order, i, p).wait_send()

    row_refs = (row_grow, ends.at[0], row_centred, row_headed)
    block_scales(decays, False, shrink, row_grow, ends.at[0])
    for k in range(PAIRS):
        scale_grad(g_ref[:, pair(k)], slice(0, TOKENS), k, shrink, row_refs)
    block_states(c_rows, row_refs, term.at[0], low.at[0])
    for copy in swap_copies(0):
        copy.start()
    loads[4].wait()
    pack_channels(reader(x_ref), put_x)
    exchange_some(send_x, got_x, 1, 0, BEHIND)
    keep_own(send_x, got_x)

    wait_all(got_m, recv_sem.at[4])
    gather_maps = maps_matrix(3, True)
    for q in range(4):
        tiles = got_m[16 * q : 16 * q + 16].astype(F32).reshape(96, LANES).astype(BF)
        piece = nn(gather_maps, tiles).astype(BF)
        for p in range(3):
            col_maps[p, 32 * q : 32 * q + 32] = piece[32 * p : 32 * p + 32]
    col_refs = (col_grow, ends.at[1], col_centred, col_headed)
    block_scales(col_maps[2], True, shrink, col_grow, ends.at[1])
    swapped(0)

    wait_all(got_g, recv_sem.at[0])

    def put_wide(q, k, value):
        wide[16 * q : 16 * q + 16, pair(k)] = value.astype(BF)

    def put_scaled(q, k, value):
        scale_grad(value, slice(16 * q, 16 * q + 16), k, shrink, col_refs)

    unpack_channels(lambda q: got_g[8 * q : 8 * q + 8], put_scaled)
    block_states(col_maps[1], col_refs, term.at[1], low.at[1])
    for copy in swap_copies(1):
        copy.start()
    filled = BEHIND + PER_HOP * (FRAMES // 2 - chip_y)
    packed_by = TILES - 1 - LEFT * chip_y
    exchange_some(send_x, got_x, 1, BEHIND, filled)
    swapped(1)
    chain(1)
    exchange_some(send_x, got_x, 1, filled, packed_by)
    chain_end(1)

    def put_col(k, value):
        wide[:, pair(k)] = value.astype(BF)

    grad_of_x(col_maps[0], col_maps[1], lambda k: carry[1, k], True, col_refs, tails, put_col)

    def put_back(q, value):
        back_x[8 * q : 8 * q + 8] = value

    pack_channels(reader(wide), put_back)

    @pl.when(chip_y > 0)
    def _():
        chain(0)

    exchange_some(send_x, got_x, 1, packed_by)
    exchange_some(back_x, home_x, 2, 0, RETURNED)

    @pl.when(chip_y == 0)
    def _():
        chain(0)

    exchange_some(back_x, home_x, 2, RETURNED)
    keep_own(back_x, home_x)

    wait_all(got_x, recv_sem.at[1])
    loads[6].wait()
    unpack_channels(lambda q: got_x[8 * q : 8 * q + 8], put_wide)
    col_b, col_c = grads_of_maps(
        wide, col_maps[0], col_maps[1], saved_col, True, col_refs, tails, scaled)
    col_b, col_c = col_b.astype(BF), col_c.astype(BF)
    spread_back = maps_matrix(2)
    for q in range(4):
        rows = slice(32 * q, 32 * q + 32)
        stack = jnp.concatenate([col_b[rows], col_c[rows]], axis=0)
        packed = nn(spread_back, stack).reshape(16, 4, LANES).astype(BF)
        back_m[16 * q : 16 * q + 16] = packed
    exchange(back_m, home_m, 3)
    keep_own(back_m, home_m)

    def put_row(k, value):
        part_x[:, pair(k)] = value

    chain_end(0)
    grad_of_x(b_rows, c_rows, lambda k: carry[0, k], False, row_refs, tails, put_row)
    loads[5].wait()
    row_b, row_c = grads_of_maps(
        x_ref, b_rows, c_rows, saved_row, False, row_refs, tails, scaled)

    wait_all(home_x, recv_sem.at[2])

    def put_sum(q, k, value):
        rows = slice(16 * q, 16 * q + 16)
        out_x[rows, pair(k)] = (part_x[rows, pair(k)] + value).astype(BF)

    unpack_channels(lambda q: home_x[8 * q : 8 * q + 8], put_sum)

    stores = [
        pltpu.make_async_copy(source, target, store_sem.at[i])
        for i, (source, target) in enumerate(
            [(out_x, out_x_hbm), (out_b, out_b_hbm), (out_c, out_c_hbm)])
    ]
    stores[0].start()

    wait_all(home_m, recv_sem.at[3])
    gather_back = maps_matrix(2, True)
    for q in range(4):
        rows = slice(32 * q, 32 * q + 32)
        tiles = home_m[16 * q : 16 * q + 16].astype(F32).reshape(64, LANES).astype(BF)
        both = nn(gather_back, tiles)
        out_b[rows, :] = (row_b[rows] + both[0:32]).astype(BF)
        out_c[rows, :] = (row_c[rows] + both[32:64]).astype(BF)

    stores[1].start()
    stores[2].start()
    chain_sent(0)
    chain_sent(1)
    wait_all(send_m, send_sem.at[4])
    wait_all(send_g, send_sem.at[0])
    wait_all(send_x, send_sem.at[1])
    wait_all(back_x, send_sem.at[2])
    wait_all(back_m, send_sem.at[3])
    for store in stores:
        store.wait()


def hand_over(x_in, b_in, c_in, x_out, b_out, c_out, x_held, b_held, c_held, load_sem, store_sem):
    parts = [(x_in, x_held, x_out), (b_in, b_held, b_out), (c_in, c_held, c_out)]
    loads = [pltpu.make_async_copy(p[0], p[1], load_sem.at[i]) for i, p in enumerate(parts)]
    stores = [pltpu.make_async_copy(p[1], p[2], store_sem.at[i]) for i, p in enumerate(parts)]
    for load in loads:
        load.start()
    for load, store in zip(loads, stores):
        load.wait()
        store.start()
    for store in stores:
        store.wait()


def shards(inputs, grad_out, b_proj, c_proj, log_decay, saved_raster, saved_column):
    anywhere = pl.BlockSpec(memory_space=pl.ANY)
    out_x, out_b, out_c = pl.pallas_call(
        kernel,
        out_shape=(
            jax.ShapeDtypeStruct((TOKENS, CHANNELS), BF),
            jax.ShapeDtypeStruct((TOKENS, STATE), BF),
            jax.ShapeDtypeStruct((TOKENS, STATE), BF),
        ),
        in_specs=[pl.BlockSpec(memory_space=pltpu.HBM)] * 7,
        out_specs=(anywhere, anywhere, anywhere),
        scratch_shapes=[
            pltpu.VMEM((TOKENS, CHANNELS), BF),
            pltpu.VMEM((TOKENS, STATE), BF),
            pltpu.VMEM((TOKENS, STATE), BF),
            pltpu.VMEM((TOKENS, CHANNELS), BF),
            pltpu.VMEM((TOKENS, CHANNELS), BF),
            pltpu.VMEM((TOKENS, STATE), BF),
            pltpu.VMEM((TOKENS, STATE), BF),
            pltpu.VMEM((HEADS, TOKENS), BF),
            pltpu.VMEM((CHANNELS, STATE), F32),
            pltpu.VMEM((CHANNELS, STATE), F32),
            pltpu.VMEM((TILES, 3, 2, LANES), BF),
            pltpu.VMEM((TILES, 2, 8, LANES), BF),
            pltpu.VMEM((TILES, 2, 8, LANES), BF),
            pltpu.VMEM((TILES, 3, 2, LANES), BF),
            pltpu.VMEM((TILES, 2, 8, LANES), BF),
            pltpu.VMEM((TILES, 2, 8, LANES), BF),
            pltpu.VMEM((TILES, 2, 8, LANES), BF),
            pltpu.VMEM((TILES, 4, LANES), BF),
            pltpu.VMEM((TILES, 2, 8, LANES), BF),
            pltpu.VMEM((TILES, 4, LANES), BF),
            pltpu.VMEM((TOKENS, CHANNELS), F32),
            pltpu.VMEM((TOKENS, CHANNELS), F32),
            pltpu.VMEM((TOKENS, CHANNELS), BF),
            pltpu.VMEM((TOKENS, CHANNELS), BF),
            pltpu.VMEM((TOKENS, CHANNELS), F32),
            pltpu.VMEM((TOKENS, CHANNELS), BF),
            pltpu.VMEM((TOKENS, CHANNELS), BF),
            pltpu.VMEM((2, PAIRS, STATE, LANES), F32),
            pltpu.VMEM((2, PAIRS, STATE, LANES), BF),
            pltpu.VMEM((2, PAIRS, 2, LANES), F32),
            pltpu.VMEM((2, HALF, STATE, LANES), BF),
            pltpu.VMEM((2, PAIRS, 2, LANES), F32),
            pltpu.VMEM((2, HALF, STATE, LANES), BF),
            pltpu.VMEM((2, HALF, STATE, LANES), BF),
            pltpu.VMEM((2, HALF, STATE, LANES), BF),
            pltpu.VMEM((2, PAIRS, STATE, LANES), BF),
            pltpu.VMEM((STATE, CHANNELS), BF),
            pltpu.VMEM((TOKENS, CHANNELS), BF),
            pltpu.VMEM((TOKENS, CHANNELS), BF),
            pltpu.VMEM((3, TOKENS, LANES), BF),
            pltpu.VMEM((TOKENS, CHANNELS), F32),
            pltpu.SemaphoreType.DMA((7,)),
            pltpu.SemaphoreType.DMA((3,)),
            pltpu.SemaphoreType.DMA((5,)),
            pltpu.SemaphoreType.DMA((5,)),
            pltpu.SemaphoreType.DMA((2, 2)),
            pltpu.SemaphoreType.DMA((2, 2)),
            pltpu.SemaphoreType.DMA((2, HALF, PIECES_MAX)),
            pltpu.SemaphoreType.DMA((2, HALF, PIECES_MAX)),
            pltpu.SemaphoreType.DMA((2, HALF, PIECES_MAX)),
            pltpu.SemaphoreType.DMA((2, HALF, PIECES_MAX)),
        ],
        compiler_params=pltpu.CompilerParams(
            collective_id=0, has_side_effects=True, vmem_limit_bytes=63 * 1024 * 1024
        ),
        cost_estimate=pl.CostEstimate(
            flops=800_000_000, bytes_accessed=2_600_000, transcendentals=1_000_000
        ),
        name="scan_backward",
    )(
        inputs.reshape(TOKENS, CHANNELS),
        grad_out.reshape(TOKENS, CHANNELS),
        b_proj.reshape(TOKENS, STATE),
        c_proj.reshape(TOKENS, STATE),
        log_decay.reshape(HEADS, TOKENS),
        saved_raster.reshape(CHANNELS, STATE),
        saved_column.reshape(CHANNELS, STATE),
    )
    out_x, out_b, out_c = pl.pallas_call(
        hand_over,
        out_shape=(
            jax.ShapeDtypeStruct((TOKENS, CHANNELS), BF),
            jax.ShapeDtypeStruct((TOKENS, STATE), BF),
            jax.ShapeDtypeStruct((TOKENS, STATE), BF),
        ),
        in_specs=[anywhere] * 3,
        out_specs=(anywhere, anywhere, anywhere),
        scratch_shapes=[
            pltpu.VMEM((TOKENS, CHANNELS), BF),
            pltpu.VMEM((TOKENS, STATE), BF),
            pltpu.VMEM((TOKENS, STATE), BF),
            pltpu.SemaphoreType.DMA((3,)),
            pltpu.SemaphoreType.DMA((3,)),
        ],
        compiler_params=pltpu.CompilerParams(vmem_limit_bytes=63 * 1024 * 1024),
        cost_estimate=pl.CostEstimate(flops=0, bytes_accessed=640_000, transcendentals=0),
        name="hand_over",
    )(out_x, out_b, out_c)
    return (
        out_x.reshape(1, 1, TOKENS, CHANNELS),
        out_b.reshape(1, 1, TOKENS, STATE),
        out_c.reshape(1, 1, TOKENS, STATE),
    )


def solution(mesh):
    in_specs = (
        P("frames", "tiles", None, None),
        P("frames", "tiles", None, None),
        P("frames", "tiles", None, None),
        P("frames", "tiles", None, None),
        P(None, "frames", "tiles", None),
        P("frames", "tiles", None, None, None),
        P("frames", "tiles", None, None, None),
    )
    out_specs = (
        P("frames", "tiles", None, None),
        P("frames", "tiles", None, None),
        P("frames", "tiles", None, None),
    )
    return jax.shard_map(shards, mesh=mesh, in_specs=in_specs, out_specs=out_specs, check_vma=False)
```
